128 devices in a mesh: side: 2 (over z_hi), dev: 64 (over z_lo, x, y, core).
Axes of the slice: x: 4, y: 4, z: 4 (z_hi: 2, z_lo: 2; z = z_hi * 2 + z_lo), core: 2. Of those that a mesh axis runs over, the one named last changes fastest.
Arguments:
- query_latent: bfloat16 [384, 128, 576], P('dev'), may hold values from -192 to 192
- latent_cache: bfloat16 [384, 1024, 576], P('dev', 'side'), may hold values from -6 to 6
- lengths: int32 [384], P('dev'), may hold values from 128 to 1024, as said below
- stream: bfloat16 [384, 7168], P(('side', 'dev')), may hold values from -6 to 6
- norm_gain: float32 [7168], replicated, may hold values from 0.25 to 1.75
- value_up: bfloat16 [128, 512, 128], P(('side', 'dev')), may hold values from -1.5 to 1.5
- out_proj: bfloat16 [16384, 7168], P(('side', 'dev')), may hold values from -0.046875 to 0.046875
- gate_proj: bfloat16 [7168, 18432], P(None, 'dev'), may hold values from -0.0625 to 0.0625
- up_proj: bfloat16 [7168, 18432], P(None, 'dev'), may hold values from -0.0625 to 0.0625
- down_proj: bfloat16 [18432, 7168], P('dev'), may hold values from -0.046875 to 0.046875
Outputs:
- new_stream: bfloat16 [384, 7168], P(('side', 'dev'))
The draws below stay inside these ranges and needn't reach their ends.
Inputs may be any that keep to these rules, and one draw needn't show every extreme that they name: `lengths`: each row's number of valid cached positions, at least 128; some row has exactly 1024.
All inputs are finite; a program needn't handle non-finite values.
Results may differ from the reference program's by a relative error of at most 0.02.
Values may be sent and summed in bfloat16 or wider, within the bound.
No kernel may reach another device: no remote copies, remote signals or barrier semaphores. Data moves between devices by JAX's collectives and lax.ppermute only.
A program may use at most 128 MiB of HBM per device.

```python
import math
import jax
import jax.numpy as jnp
from jax import lax

D = 7168
H = 128
LAT = 512
ROPE = 64
VD = 128
FF = 18432
QKD = 192
RD = 6
LMAX = 1024
ROWS = 384


def draw_latent_cache(key, part):
    key = jax.random.fold_in(key, 1)
    base = jnp.clip(jax.random.normal(key, (ROWS, LMAX, LAT + ROPE), jnp.float32), -6.0, 6.0)
    return base.astype(jnp.bfloat16)


def draw_query_latent(key, part):
    key = jax.random.fold_in(key, 2)
    base = jnp.clip(jax.random.normal(key, (ROWS, H, LAT + ROPE), jnp.float32), -6.0, 6.0)
    return base.astype(jnp.bfloat16)


def draw_lengths(key, part):
    key = jax.random.fold_in(key, 3)
    key_level, key_length, key_pick = jax.random.split(key, 3)
    level = 2 ** jax.random.randint(key_level, (ROWS // RD,), 0, 4)
    level_rows = jnp.repeat(level, RD)
    lowest = LMAX // 8
    upper_bound = lowest * level_rows + 1
    draws = jax.random.randint(key_length, (ROWS,), 0, 1 << 30)
    length = lowest + draws % (upper_bound - lowest)
    picked = jax.random.randint(key_pick, (), 0, ROWS)
    length = jnp.where(lax.iota(jnp.int32, ROWS) == picked, LMAX, length)
    return length.astype(jnp.int32)


def shard_levels(key, dims, cuts, smallest, top_value):
    gain = 1.0
    for dim, parts in cuts:
        heights = jax.random.uniform(jax.random.fold_in(jax.random.fold_in(key, 6), dim), (parts,), jnp.float32, smallest / len(cuts), top_value / len(cuts))
        gain = gain * jnp.repeat(jnp.exp(heights), dims[dim] // parts).reshape((-1,) + (1,) * (len(dims) - 1 - dim))
    return gain


def gaussian(own_key, dims, spread, most, shards=(), held_as=jnp.bfloat16):
    loudness = shard_levels(own_key, dims, shards, -0.22, 0.18) if shards else 1.0
    entries = jax.random.normal(own_key, dims, jnp.float32) * spread * loudness
    return jnp.minimum(jnp.maximum(entries, -most), most).astype(held_as)


def setup_inputs(seed: int = 0) -> dict:
    arg_keys = jax.random.split(jax.random.key(seed), 11)
    query_latent = draw_query_latent(jax.random.fold_in(arg_keys[10], 71), 0)
    latent_cache = draw_latent_cache(jax.random.fold_in(arg_keys[10], 71), 0)
    lengths = draw_lengths(jax.random.fold_in(arg_keys[10], 71), 0)
    stream = gaussian(arg_keys[3], (ROWS, D), 1.0, 6.0, ((0, 128),))
    norm_gain = jnp.clip(1.0 + 0.15 * jax.random.normal(arg_keys[4], (D,), jnp.float32), 0.25, 1.75)
    value_up = gaussian(arg_keys[5], (H, LAT, VD), 16 ** -0.5, 1.5, ((0, 128),))
    out_proj = gaussian(arg_keys[6], (H * VD, D), (H * VD) ** -0.5, 0.046875, ((0, 128),))
    gate_proj = gaussian(arg_keys[7], (D, FF), D ** -0.5, 0.0625, ((1, 64),))
    up_proj = gaussian(arg_keys[8], (D, FF), D ** -0.5, 0.0625, ((1, 64),))
    down_proj = gaussian(arg_keys[9], (FF, D), FF ** -0.5, 0.046875, ((0, 64),))
    return {"query_latent": query_latent, "latent_cache": latent_cache, "lengths": lengths, "stream": stream, "norm_gain": norm_gain, "value_up": value_up, "out_proj": out_proj, "gate_proj": gate_proj, "up_proj": up_proj, "down_proj": down_proj}


def attend_row(operands):
    query, cached, length = operands
    scores = jnp.dot(query, cached.T, preferred_element_type=jnp.float32) * (1.0 / math.sqrt(QKD))
    usable = (lax.iota(jnp.int32, cached.shape[0]) < length)[None, :]
    scores = jnp.where(usable, scores, jnp.float32(-1e+30))
    row_peak = lax.optimization_barrier(jnp.max(scores, axis=1, keepdims=True))
    exponent = jnp.where(usable, jnp.exp(scores - row_peak), jnp.float32(0.0))
    row_total = lax.optimization_barrier(jnp.sum(exponent, axis=1, keepdims=True))
    probs = exponent.astype(jnp.bfloat16)
    weighted = jnp.dot(probs, cached[:, :LAT], preferred_element_type=jnp.float32)
    return (weighted / row_total).astype(jnp.bfloat16)

def reference(query_latent, latent_cache, lengths, stream, norm_gain, value_up, out_proj, gate_proj, up_proj, down_proj):
    latent = lax.map(attend_row, (query_latent, latent_cache, lengths))
    values = jnp.einsum('rhc,hcd->rhd', latent.astype(jnp.float32), value_up.astype(jnp.float32)).astype(jnp.bfloat16)
    attended = jnp.dot(values.reshape(ROWS, H * VD), out_proj, preferred_element_type=jnp.float32)
    residual = stream.astype(jnp.float32) + attended
    mean_square = lax.optimization_barrier(jnp.mean(residual * residual, axis=1, keepdims=True))
    normalized = (residual * lax.rsqrt(mean_square + 1e-06) * norm_gain.astype(jnp.float32)).astype(jnp.bfloat16)
    gate = jnp.dot(normalized, gate_proj, preferred_element_type=jnp.float32)
    upper = jnp.dot(normalized, up_proj, preferred_element_type=jnp.float32)
    hidden = (jax.nn.silu(gate) * upper).astype(jnp.bfloat16)
    feed_out = jnp.dot(hidden, down_proj, preferred_element_type=jnp.float32)
    return (residual + feed_out).astype(jnp.bfloat16)
```

```python
import math

import jax
import jax.numpy as jnp
from jax import lax
from jax.sharding import Mesh, PartitionSpec as P

LAT = 512
QKD = 192
AXES = ("zh", "zl", "x", "y", "core")
DEV = ("zl", "x", "y", "core")
CHIPS = ("zh", "zl", "x", "y")
SIDE_CHIPS = ("zl", "x", "y")
SWAP = [(0, 1), (1, 0)]
F32 = jnp.float32
BF16 = jnp.bfloat16


def swap_halves(array, core, axis):
    half = array.shape[axis] // 2
    mine = lax.dynamic_slice_in_dim(array, core * half, half, axis)
    theirs = lax.dynamic_slice_in_dim(array, (1 - core) * half, half, axis)
    return mine, lax.ppermute(theirs, "core", SWAP)


def split_pair(value):
    high = lax.reduce_precision(value, 8, 7)
    low = lax.reduce_precision(value - high, 8, 7)
    return high, low


def local(
    query_latent,
    latent_cache,
    lengths,
    stream,
    norm_gain,
    value_up,
    out_proj,
    gate_proj,
    up_proj,
    down_proj,
):
    core = lax.axis_index("core")
    rows_own, width = stream.shape
    half = width // 2
    out_mine, out_theirs = swap_halves(out_proj, core, 1)
    down_mine, down_theirs = swap_halves(down_proj, core, 1)
    stream_mine, stream_theirs = swap_halves(stream, core, 1)
    first = core == 0
    stream_rows = jnp.concatenate(
        [
            jnp.where(first, stream_mine, stream_theirs),
            jnp.where(first, stream_theirs, stream_mine),
        ],
        axis=0,
    ).astype(F32)

    rows, heads, _ = query_latent.shape
    half_keys = latent_cache.shape[1]
    positions = lax.axis_index("zh") * half_keys + lax.iota(jnp.int32, half_keys)
    usable = (positions[None, :] < lengths[:, None])[:, None, :]
    scores = jnp.einsum(
        "rhc,rkc->rhk", query_latent, latent_cache, preferred_element_type=F32
    ) * (1.0 / math.sqrt(QKD))
    scores = jnp.where(usable, scores, F32(-1e30))
    peak_high, peak_low = split_pair(jnp.max(scores, axis=2))
    peak = peak_high + peak_low
    exponent = jnp.where(usable, jnp.exp(scores - peak[:, :, None]), F32(0.0))
    total_high, total_low = split_pair(jnp.sum(exponent, axis=2))
    weighted = jnp.einsum(
        "rhk,rkc->rhc",
        exponent.astype(BF16),
        latent_cache[:, :, :LAT],
        preferred_element_type=F32,
    ).astype(BF16)
    stats = jnp.stack([peak_high, peak_low, total_high, total_low]).astype(BF16)
    stats = stats.transpose(2, 0, 1).reshape(heads, 1, 4 * rows)
    stats = jnp.pad(stats, ((0, 0), (0, 1), (0, LAT - 4 * rows)))
    payload = jnp.concatenate([weighted.transpose(1, 0, 2), stats], axis=1)
    received = lax.all_to_all(payload, AXES, split_axis=0, concat_axis=0, tiled=True)

    devs = received.shape[0] // 2
    received = received.reshape(2, devs, rows + 2, LAT)
    stats = received[:, :, rows, : 4 * rows].reshape(2, devs, 4, rows).astype(F32)
    peaks = stats[:, :, 0] + stats[:, :, 1]
    totals = stats[:, :, 2] + stats[:, :, 3]
    factor = jnp.exp(peaks - jnp.max(peaks, axis=0, keepdims=True))
    factor = factor / jnp.sum(factor * totals, axis=0, keepdims=True)
    latent = jnp.sum(received[:, :, :rows].astype(F32) * factor[..., None], axis=0).astype(BF16)
    latent = latent.reshape(devs * rows, LAT)
    values = jnp.dot(latent, value_up[0], preferred_element_type=F32).astype(BF16)
    values_theirs = lax.ppermute(values, "core", SWAP)
    partial = jnp.dot(values, out_mine, preferred_element_type=F32) + jnp.dot(
        values_theirs, out_theirs, preferred_element_type=F32
    )

    chips = devs
    chunk = 2 * rows_own
    partial = partial.astype(BF16).reshape(chips, chunk * half // 128, 128)
    parts = lax.all_to_all(partial, CHIPS, split_axis=0, concat_axis=0, tiled=True)
    attended = jnp.sum(parts.astype(F32), axis=0).reshape(chunk, half)
    residual = stream_rows + attended
    squares = jnp.sum(residual * residual, axis=1)
    squares = squares + lax.ppermute(squares, "core", SWAP)
    scale = lax.rsqrt(squares / width + 1e-06)
    gain = lax.dynamic_slice_in_dim(norm_gain, core * half, half, 0)
    normalized = (residual * scale[:, None] * gain).astype(BF16)

    side_chips = chips // 2
    normalized = normalized.reshape(1, chunk * half // 128, 128)
    normalized = jnp.broadcast_to(normalized, (side_chips,) + normalized.shape[1:])
    piece = lax.all_to_all(normalized, SIDE_CHIPS, split_axis=0, concat_axis=0, tiled=True)
    piece = piece.reshape(side_chips * chunk, half)
    piece_theirs = lax.ppermute(piece, "core", SWAP)

    def hidden_units(weight):
        mine = lax.dynamic_slice_in_dim(weight, core * half, half, 0)
        theirs = lax.dynamic_slice_in_dim(weight, (1 - core) * half, half, 0)
        return jnp.dot(piece, mine, preferred_element_type=F32) + jnp.dot(
            piece_theirs, theirs, preferred_element_type=F32
        )

    hidden = (jax.nn.silu(hidden_units(gate_proj)) * hidden_units(up_proj)).astype(BF16)
    hidden_theirs = lax.ppermute(hidden, "core", SWAP)
    partial = jnp.dot(hidden, down_mine, preferred_element_type=F32) + jnp.dot(
        hidden_theirs, down_theirs, preferred_element_type=F32
    )
    partial = partial.astype(BF16).reshape(side_chips, chunk * half // 128, 128)
    parts = lax.all_to_all(partial, SIDE_CHIPS, split_axis=0, concat_axis=0, tiled=True)
    feed_out = jnp.sum(parts.astype(F32), axis=0).reshape(chunk, half)
    new_stream = (residual + feed_out).astype(BF16)
    mine = lax.dynamic_slice_in_dim(new_stream, core * rows_own, rows_own, 0)
    theirs = lax.dynamic_slice_in_dim(new_stream, (1 - core) * rows_own, rows_own, 0)
    theirs = lax.ppermute(theirs, "core", SWAP)
    return jnp.concatenate(
        [jnp.where(first, mine, theirs), jnp.where(first, theirs, mine)], axis=1
    )


def solution(mesh):
    fine = Mesh(mesh.devices.reshape(2, 2, 4, 4, 2), AXES)
    placed = (
        P(DEV, None, None),
        P(DEV, "zh", None),
        P(DEV),
        P(AXES, None),
        P(),
        P(AXES, None, None),
        P(AXES, None),
        P(None, DEV),
        P(None, DEV),
        P(DEV, None),
    )
    return jax.shard_map(
        local, mesh=fine, in_specs=placed, out_specs=P(AXES, None), check_vma=False
    )
```

```python
import math

import jax
import jax.numpy as jnp
from jax import lax
from jax.sharding import Mesh, PartitionSpec as P

LAT = 512
QKD = 192
LANES = 128
AXES = ("zh", "zl", "x", "y", "core")
DEV = ("zl", "x", "y", "core")
RING = ("y", "core")
OUTER = ("zh", "zl", "x")
SIDE_CHIPS = ("zl", "x", "y")
SWAP = [(0, 1), (1, 0)]
F32 = jnp.float32
BF16 = jnp.bfloat16


def swap(array):
    return lax.ppermute(array, "core", SWAP)


def shift(array, step):
    return lax.ppermute(array, "y", [(i, (i + step) % 4) for i in range(4)])


def block(array, index, size, axis):
    return lax.dynamic_slice_in_dim(array, index * size, size, axis)


def swap_halves(array, core, axis):
    half = array.shape[axis] // 2
    return block(array, core, half, axis), swap(block(array, 1 - core, half, axis))


def split_pair(value):
    high = lax.reduce_precision(value, 8, 7)
    low = lax.reduce_precision(value - high, 8, 7)
    return high, low


def local(
    query_latent,
    latent_cache,
    lengths,
    stream,
    norm_gain,
    value_up,
    out_proj,
    gate_proj,
    up_proj,
    down_proj,
):
    core = lax.axis_index("core")
    ring = lax.axis_index("y")
    rows_own, width = stream.shape
    half = width // 2
    eighth = width // 8
    first = core == 0

    ring_up = lax.all_gather(value_up, RING, axis=0, tiled=True)
    out_mine, out_theirs = swap_halves(out_proj, core, 1)
    out_pair = jnp.stack([out_mine, out_theirs])
    out_parts = [block(out_pair, ring, eighth, 2)]
    for step in (1, 2, 3):
        out_parts.append(shift(block(out_pair, (ring + step) % 4, eighth, 2), step))
    ring_stream = lax.all_gather(stream, RING, axis=0, tiled=True)
    ring_stream = block(ring_stream, core * 4 + ring, eighth, 1).astype(F32)
    down_mine, down_theirs = swap_halves(down_proj, core, 1)

    rows, heads, _ = query_latent.shape
    half_keys = latent_cache.shape[1]
    positions = lax.axis_index("zh") * half_keys + lax.iota(jnp.int32, half_keys)
    usable = (positions[None, :] < lengths[:, None])[:, None, :]
    scores = jnp.einsum(
        "rhc,rkc->rhk", query_latent, latent_cache, preferred_element_type=F32
    ) * (1.0 / math.sqrt(QKD))
    scores = jnp.where(usable, scores, F32(-1e30))
    peak_high, peak_low = split_pair(jnp.max(scores, axis=2))
    peak = peak_high + peak_low
    exponent = jnp.where(usable, jnp.exp(scores - peak[:, :, None]), F32(0.0))
    total_high, total_low = split_pair(jnp.sum(exponent, axis=2))
    weighted = jnp.einsum(
        "rhk,rkc->rhc",
        exponent.astype(BF16),
        latent_cache[:, :, :LAT],
        preferred_element_type=F32,
    ).astype(BF16)
    stats = jnp.stack([peak_high, peak_low, total_high, total_low], axis=-1).astype(BF16)
    stats = stats.transpose(1, 0, 2).reshape(heads // 8, 1, 8, 4 * rows)
    stats = jnp.pad(stats, ((0, 0), (0, 0), (0, 0), (0, LANES - 4 * rows)))
    tiles = LAT // LANES
    weighted = weighted.reshape(rows, heads // 8, 8, tiles, LANES).transpose(1, 0, 3, 2, 4)
    weighted = weighted.reshape(heads // 8, rows * tiles, 8, LANES)
    payload = jnp.concatenate([weighted, stats], axis=1)
    received = lax.all_to_all(payload, OUTER, split_axis=0, concat_axis=0, tiled=True)

    stats = received[:, rows * tiles, :, : 4 * rows].astype(F32).reshape(2, 8, 8, rows, 4)
    peaks = stats[..., 0] + stats[..., 1]
    totals = stats[..., 2] + stats[..., 3]
    factor = jnp.exp(peaks - jnp.max(peaks, axis=0, keepdims=True))
    factor = factor / jnp.sum(factor * totals, axis=0, keepdims=True)
    factor = factor.transpose(0, 1, 3, 2)
    parts = received[:, : rows * tiles].reshape(2, 8, rows, tiles, 8, LANES)
    latent = jnp.sum(parts.astype(F32) * factor[:, :, :, None, :, None], axis=0).astype(BF16)
    latent = latent.transpose(0, 1, 3, 2, 4).reshape(8 * rows, 8, LAT)
    values = jnp.einsum("rhc,hcd->rhd", latent, ring_up, preferred_element_type=F32)
    values = values.astype(BF16).reshape(8 * rows, 8 * LANES)

    ring_values = jnp.stack([values] + [shift(values, step) for step in (1, 2, 3)])
    both = jnp.stack([ring_values, swap(ring_values)], axis=1)
    both = both.reshape(4, 2, 8, rows, 8 * LANES)
    back = (ring - jnp.arange(4)) % 4
    both = jnp.take(both, back, axis=0)
    both = jnp.take(both, jnp.stack([core, 1 - core]), axis=1)
    left = both.transpose(2, 0, 1, 3, 4).reshape(64 * rows, 8 * LANES)
    weight = jnp.take(jnp.stack(out_parts), back, axis=0)
    weight = jnp.take(weight, jnp.stack([core, 1 - core]), axis=1)
    weight = weight.reshape(8 * LANES, eighth)
    partial = jnp.dot(left, weight, preferred_element_type=F32).astype(BF16)
    partial = partial.reshape(16, -1, eighth)
    parts = lax.all_to_all(partial, OUTER, split_axis=0, concat_axis=0, tiled=True)
    residual = ring_stream + jnp.sum(parts.astype(F32), axis=0)

    group_rows = residual.shape[0]
    squares = jnp.stack(split_pair(jnp.sum(residual * residual, axis=1)), axis=1).astype(BF16)
    squares = jnp.pad(squares, ((0, 0), (0, LANES - 2)))
    gain = block(norm_gain, core * 4 + ring, eighth, 0)
    normalized = jnp.concatenate([(residual * gain).astype(BF16), squares], axis=1)
    normalized = jnp.broadcast_to(normalized, (32,) + normalized.shape)
    piece = lax.all_to_all(normalized, SIDE_CHIPS, split_axis=0, concat_axis=0, tiled=True)
    side_rows = 8 * group_rows

    def unpack(gathered):
        gathered = gathered.reshape(8, 4, group_rows, -1)
        squares = gathered[..., eighth : eighth + 2].astype(F32)
        squares = jnp.sum(squares, axis=(1, 3)).reshape(side_rows)
        data = gathered[..., :eighth].transpose(0, 2, 1, 3).reshape(side_rows, half)
        return data, squares

    mine, squares_mine = unpack(piece)
    theirs, squares_theirs = unpack(swap(piece))
    scale = lax.rsqrt((squares_mine + squares_theirs) / width + 1e-06)[:, None]

    def hidden_units(weight):
        own = jnp.dot(mine, block(weight, core, half, 0), preferred_element_type=F32)
        other = jnp.dot(theirs, block(weight, 1 - core, half, 0), preferred_element_type=F32)
        return (own + other) * scale

    hidden = (jax.nn.silu(hidden_units(gate_proj)) * hidden_units(up_proj)).astype(BF16)
    partial = jnp.dot(hidden, down_mine, preferred_element_type=F32) + jnp.dot(
        swap(hidden), down_theirs, preferred_element_type=F32
    )
    group = lax.axis_index("zl") * 4 + lax.axis_index("x")
    start = (group * group_rows, ring * eighth)
    held = lax.dynamic_slice(partial, start, residual.shape)
    partial = lax.dynamic_update_slice(partial, held + residual, start)
    chunk = 2 * rows_own
    partial = partial.astype(BF16).reshape(32, chunk * half // LANES, LANES)
    parts = lax.all_to_all(partial, SIDE_CHIPS, split_axis=0, concat_axis=0, tiled=True)
    new_stream = jnp.sum(parts.astype(F32), axis=0).reshape(chunk, half).astype(BF16)
    mine = block(new_stream, core, rows_own, 0)
    theirs = swap(block(new_stream, 1 - core, rows_own, 0))
    return jnp.concatenate(
        [jnp.where(first, mine, theirs), jnp.where(first, theirs, mine)], axis=1
    )


def solution(mesh):
    fine = Mesh(mesh.devices.reshape(2, 2, 4, 4, 2), AXES)
    placed = (
        P(DEV, None, None),
        P(DEV, "zh", None),
        P(DEV),
        P(AXES, None),
        P(),
        P(AXES, None, None),
        P(AXES, None),
        P(None, DEV),
        P(None, DEV),
        P(DEV, None),
    )
    return jax.shard_map(
        local, mesh=fine, in_specs=placed, out_specs=P(AXES, None), check_vma=False
    )
```

```python
import functools
import math

import jax
import jax.numpy as jnp
import numpy as np
from jax import lax
from jax.experimental import pallas as pl
from jax.experimental.pallas import tpu as pltpu
from jax.sharding import Mesh, PartitionSpec as P

LAT = 512
QKD = 192
LANES = 128
SUB = 8
AXES = ("zh", "zl", "x", "y", "core")
DEV = ("zl", "x", "y", "core")
OUTER = ("zh", "zl", "x")
SIDE_CHIPS = ("zl", "x", "y")
SWAP = [(0, 1), (1, 0)]
F32 = jnp.float32
BF16 = jnp.bfloat16
VMEM_LIMIT = 40 * 1024 * 1024


def swap(array):
    return lax.ppermute(array, "core", SWAP)


def shift(array, step):
    return lax.ppermute(array, "y", [(i, (i + step) % 4) for i in range(4)])


def block(array, index, size, axis):
    return lax.dynamic_slice_in_dim(array, index * size, size, axis)


def swap_halves(array, core, axis):
    half = array.shape[axis] // 2
    return block(array, core, half, axis), swap(block(array, 1 - core, half, axis))


def spread(groups, rows):
    matrix = np.zeros((groups * SUB, groups * rows), np.float32)
    for group in range(groups):
        for row in range(rows):
            matrix[group * SUB + row, group * rows + row] = 1.0
    return matrix


def params(*semantics):
    return pltpu.CompilerParams(
        vmem_limit_bytes=VMEM_LIMIT, dimension_semantics=semantics or None
    )


def cost(flops, read):
    return pl.CostEstimate(flops=flops, bytes_accessed=read, transcendentals=0)


WHOLE = pl.BlockSpec(memory_space=pltpu.VMEM)


def rounded(value):
    return value.astype(BF16).astype(F32)


def attend_kernel(info_ref, query_ref, cache_ref, out_ref, held, stats):
    row = pl.program_id(0)
    rows = pl.num_programs(0)
    keys = cache_ref.shape[1]
    heads = query_ref.shape[1]
    cached = cache_ref[0]
    scores = lax.dot_general(
        query_ref[0], cached, (((1,), (1,)), ((), ())), preferred_element_type=F32
    ) * (1.0 / math.sqrt(QKD))
    position = lax.broadcasted_iota(jnp.int32, (1, keys), 1) + info_ref[rows]
    usable = position < info_ref[row]
    scores = jnp.where(usable, scores, F32(-1e30))
    top = jnp.max(scores, axis=1, keepdims=True)
    top_high = rounded(top)
    top_low = rounded(top - top_high)
    exponent = jnp.where(usable, jnp.exp(scores - (top_high + top_low)), F32(0.0))
    total = jnp.sum(exponent, axis=1, keepdims=True)
    total_high = rounded(total)
    total_low = rounded(total - total_high)
    weighted = jnp.dot(
        exponent.astype(BF16), cached[:, :LAT], preferred_element_type=F32
    )
    tiles = [slice(start, start + LANES) for start in range(0, LAT, LANES)]
    for index, tile in enumerate(tiles):
        held[index, pl.ds(row, heads, stride=SUB), :] = weighted[:, tile]
    lane = lax.broadcasted_iota(jnp.int32, (heads, LANES), 1)
    new = jnp.where(lane == row, top_high, stats[...])
    new = jnp.where(lane == row + SUB, top_low, new)
    new = jnp.where(lane == row + 2 * SUB, total_high, new)
    stats[...] = jnp.where(lane == row + 3 * SUB, total_low, new)

    @pl.when(row == rows - 1)
    def _():
        zero = jnp.zeros((heads, LANES), F32)
        for index, tile in enumerate(tiles):
            filler = zero if index else stats[...]
            held[index, pl.ds(SUB - 2, heads, stride=SUB), :] = filler
            held[index, pl.ds(SUB - 1, heads, stride=SUB), :] = zero
            out_ref[:, :, tile] = held[index].reshape(heads, SUB, LANES).astype(BF16)


def attend(info, query, cache):
    rows, heads, depth = query.shape
    keys = cache.shape[1]
    return pl.pallas_call(
        attend_kernel,
        out_shape=jax.ShapeDtypeStruct((heads, SUB, LAT), BF16),
        grid_spec=pltpu.PrefetchScalarGridSpec(
            num_scalar_prefetch=1,
            grid=(rows,),
            in_specs=[
                pl.BlockSpec((1, heads, depth), lambda r, info: (r, 0, 0)),
                pl.BlockSpec((1, keys, depth), lambda r, info: (r, 0, 0)),
            ],
            out_specs=pl.BlockSpec((heads, SUB, LAT), lambda r, info: (0, 0, 0)),
            scratch_shapes=[
                pltpu.VMEM((LAT // LANES, heads * SUB, LANES), F32),
                pltpu.VMEM((heads, LANES), F32),
            ],
        ),
        compiler_params=params("arbitrary"),
        cost_estimate=cost(2 * rows * heads * keys * (depth + LAT), 5_000_000),
        name="attend",
    )(info, query, cache)


def join_kernel(rows, recv_ref, up_ref, gather_ref, out_ref):
    devs = recv_ref.shape[0] // 2
    parts = recv_ref[...].astype(F32).reshape(2, devs, SUB, LAT)
    table = parts[:, :, SUB - 2 : SUB - 1, :LANES]
    lane = lax.broadcasted_iota(jnp.int32, (SUB, LANES), 1)
    sub = lax.broadcasted_iota(jnp.int32, (SUB, LANES), 0)

    def pick(first):
        chosen = (lane == sub + first) | (lane == sub + first + SUB)
        return jnp.sum(jnp.where(chosen & (sub < rows), table, F32(0.0)), axis=3, keepdims=True)

    peaks = pick(0)
    totals = pick(2 * SUB)
    factor = jnp.exp(peaks - jnp.maximum(peaks[:1], peaks[1:]))
    total = factor[0] * totals[0] + factor[1] * totals[1]
    valid = lax.broadcasted_iota(jnp.int32, (1, SUB, 1), 1) < rows
    scale = jnp.where(valid, 1.0 / jnp.where(valid, total, F32(1.0)), F32(0.0))
    latent = parts[0] * (factor[0] * scale) + parts[1] * (factor[1] * scale)
    latent = latent.reshape(devs * SUB, LAT).astype(BF16)
    values = jnp.dot(latent, up_ref[0], preferred_element_type=F32).astype(BF16)
    out_ref[...] = jnp.dot(gather_ref[...], values, preferred_element_type=F32).astype(BF16)


def join(received, value_up, rows):
    devs = received.shape[0] // 2
    gather = jnp.asarray(spread(devs, rows).T, BF16)
    return pl.pallas_call(
        functools.partial(join_kernel, rows),
        out_shape=jax.ShapeDtypeStruct((devs * rows, value_up.shape[2]), BF16),
        in_specs=[WHOLE] * 3,
        out_specs=WHOLE,
        compiler_params=params(),
        cost_estimate=cost(120_000_000, 1_500_000),
        name="join",
    )(received, value_up, gather)


def project_kernel(info_ref, *refs):
    values, theirs, out_ref = refs[:8], refs[8:16], refs[16]
    del info_ref
    left = jnp.concatenate([ref[...] for ref in values], axis=1)
    right = jnp.concatenate([ref[...] for ref in theirs], axis=0)
    total = jnp.dot(left, right, preferred_element_type=F32)
    out_ref[...] = total.reshape(out_ref.shape).astype(BF16)


def project(info, values, out_proj, parts, theirs, chips):
    rows, lanes = values[0].shape
    eighth = theirs[0].shape[1]
    full = lambda shape: pl.BlockSpec(shape, lambda i, info: (0,) * len(shape))
    held = pl.BlockSpec((lanes, eighth), lambda i, info: (0, info[1]))
    own = pl.BlockSpec((lanes, eighth), lambda i, info: (0, info[0]))
    return pl.pallas_call(
        project_kernel,
        out_shape=jax.ShapeDtypeStruct((chips, rows // chips, eighth), BF16),
        grid_spec=pltpu.PrefetchScalarGridSpec(
            num_scalar_prefetch=1,
            grid=(1,),
            in_specs=[full((rows, lanes))] * 8
            + [own]
            + [held] * 3
            + [full((lanes, eighth))] * 4,
            out_specs=full((chips, rows // chips, eighth)),
        ),
        compiler_params=params("arbitrary"),
        cost_estimate=cost(2 * rows * 8 * lanes * eighth, 3_500_000),
        name="project",
    )(info, *values, out_proj, *parts, *theirs)


def residual_kernel(parts_ref, stream_ref, gain_ref, residual_ref, out_ref):
    residual = stream_ref[...].astype(F32) + jnp.sum(parts_ref[...].astype(F32), axis=0)
    residual_ref[...] = residual
    rows, width = residual.shape
    squares = jnp.sum(residual * residual, axis=1, keepdims=True)
    high = rounded(squares)
    low = rounded(squares - high)
    lane = lax.broadcasted_iota(jnp.int32, (SUB, LANES), 1)
    table = jnp.zeros((SUB, LANES), F32)
    scaled = residual * gain_ref[...]
    groups = rows // SUB
    columns = width // LANES
    chips = out_ref.shape[0]
    for group in range(groups):
        span = slice(group * SUB, group * SUB + SUB)
        table = jnp.where(lane == group, high[span], table)
        table = jnp.where(lane == SUB + group, low[span], table)
    tiles = [
        scaled[group * SUB : group * SUB + SUB, column * LANES : column * LANES + LANES]
        for column in range(columns)
        for group in range(groups)
    ] + [table]
    for index, tile in enumerate(tiles):
        out_ref[:, index] = jnp.broadcast_to(tile.astype(BF16)[None], (chips, SUB, LANES))


def residual_rows(parts, stream, gain, chips):
    _, rows, width = parts.shape
    tiles = rows * width // (SUB * LANES) + 1
    return pl.pallas_call(
        residual_kernel,
        out_shape=(
            jax.ShapeDtypeStruct((rows, width), F32),
            jax.ShapeDtypeStruct((chips, tiles, SUB, LANES), BF16),
        ),
        in_specs=[WHOLE] * 3,
        out_specs=(WHOLE, WHOLE),
        compiler_params=params(),
        cost_estimate=cost(2_000_000, 2_500_000),
        name="residual",
    )(parts, stream, gain)


def units_kernel(groups, width, last, info_ref, *refs):
    if last:
        recv_ref, gate_ref, up_ref, gate_in, up_in, sq_in, out_ref, gate_acc, up_acc, sq_acc = refs
    else:
        recv_ref, gate_ref, up_ref, gate_acc, up_acc, sq_acc = refs
    step = pl.program_id(0)
    sides, _, tiles, _, _ = recv_ref.shape
    columns = (tiles - 1) // groups
    rows = sides * groups * SUB
    left = jnp.concatenate(
        [
            recv_ref[:, 0, column * groups : column * groups + groups]
            .astype(F32)
            .reshape(rows, LANES)
            for column in range(columns)
        ],
        axis=1,
    ).astype(BF16)
    gate = jnp.dot(left, gate_ref[...], preferred_element_type=F32)
    upper = jnp.dot(left, up_ref[...], preferred_element_type=F32)
    table = recv_ref[:, 0, tiles - 1].astype(F32)
    lane = lax.broadcasted_iota(jnp.int32, (SUB, LANES), 1)
    pieces = [
        jnp.sum(
            jnp.where((lane == group) | (lane == SUB + group), table, F32(0.0)),
            axis=2,
            keepdims=True,
        )
        for group in range(groups)
    ]
    squares = jnp.stack(pieces, axis=1).reshape(rows, 1)
    squares = jnp.broadcast_to(squares, (rows, LANES))

    @pl.when(step == 0)
    def _():
        if last:
            gate_acc[...] = gate_in[...] + gate
            up_acc[...] = up_in[...] + upper
            sq_acc[...] = sq_in[...] + squares
        else:
            gate_acc[...] = gate
            up_acc[...] = upper
            sq_acc[...] = squares

    @pl.when(step > 0)
    def _():
        gate_acc[...] += gate
        up_acc[...] += upper
        sq_acc[...] += squares

    if last:

        @pl.when(step == pl.num_programs(0) - 1)
        def _():
            scale = lax.rsqrt(sq_acc[:, :1] / width + 1e-06)
            gate = gate_acc[...] * scale
            out_ref[...] = (gate / (1.0 + jnp.exp(-gate)) * (up_acc[...] * scale)).astype(BF16)


def units(info, which, received, gate_proj, up_proj, groups, carry=None):
    sides, quarters, tiles = received.shape[:3]
    depth = (tiles - 1) // groups * LANES
    hidden = gate_proj.shape[1]
    rows = sides * groups * SUB
    whole = lambda shape: pl.BlockSpec(shape, lambda i, info: (0,) * len(shape))
    weight = pl.BlockSpec((depth, hidden), lambda i, info: (info[which] * quarters + i, 0))
    shapes = [(rows, hidden), (rows, hidden), (rows, LANES)]
    last = carry is not None
    return pl.pallas_call(
        functools.partial(units_kernel, groups, gate_proj.shape[0], last),
        out_shape=jax.ShapeDtypeStruct((rows, hidden), BF16)
        if last
        else [jax.ShapeDtypeStruct(shape, F32) for shape in shapes],
        grid_spec=pltpu.PrefetchScalarGridSpec(
            num_scalar_prefetch=1,
            grid=(quarters,),
            in_specs=[
                pl.BlockSpec(
                    (sides, 1, tiles, SUB, LANES), lambda i, info: (0, i, 0, 0, 0)
                ),
                weight,
                weight,
            ]
            + ([whole(shape) for shape in shapes] if last else []),
            out_specs=whole((rows, hidden)) if last else [whole(shape) for shape in shapes],
            scratch_shapes=[pltpu.VMEM(shape, F32) for shape in shapes] if last else [],
        ),
        compiler_params=params("arbitrary"),
        cost_estimate=cost(4 * rows * depth * quarters * hidden, 8_000_000),
        name="units_last" if last else "units_first",
    )(info, received, gate_proj, up_proj, *(carry or ()))


def down_kernel(info_ref, mine_ref, theirs_ref, spread_ref, own_ref, other_ref, held_ref, out_ref, left, right):
    @pl.when(pl.program_id(0) == 0)
    def _():
        left[...] = jnp.dot(
            spread_ref[...], mine_ref[...], preferred_element_type=F32
        ).astype(BF16)
        right[...] = jnp.dot(
            spread_ref[...], theirs_ref[...], preferred_element_type=F32
        ).astype(BF16)

    total = jnp.dot(left[...], own_ref[...], preferred_element_type=F32) + jnp.dot(
        right[...], other_ref[...], preferred_element_type=F32
    )
    span = held_ref.shape[0]
    place = lax.broadcasted_iota(jnp.int32, (total.shape[0] // span, 1, 1), 0) == info_ref[2]
    total = total.reshape(-1, span, total.shape[1])
    total = total + jnp.where(place, held_ref[...][None], F32(0.0))
    chips = out_ref.shape[0]
    total = total.reshape(chips, SUB, -1)
    quads = [total[:, :, tile * LANES : tile * LANES + LANES] for tile in range(4)]
    sub = lax.broadcasted_iota(jnp.int32, (1, SUB, LANES), 1)
    packed = [
        jnp.where(sub < 6, quads[tile], pltpu.roll(quads[3], 6 - 2 * tile, 1))
        for tile in range(3)
    ]
    out_ref[:, 0] = jnp.concatenate(packed, axis=1).astype(BF16)


def down(info, mine, theirs, down_proj, down_theirs, held, chips):
    rows, hidden = mine.shape
    half = down_theirs.shape[1]
    width = 4 * LANES
    steps = half // width
    put = jnp.asarray(spread(chips, rows // chips), BF16)
    whole = lambda shape: pl.BlockSpec(shape, lambda i, info: (0,) * len(shape))
    return pl.pallas_call(
        down_kernel,
        out_shape=jax.ShapeDtypeStruct((chips, steps, 3 * SUB, LANES), BF16),
        grid_spec=pltpu.PrefetchScalarGridSpec(
            num_scalar_prefetch=1,
            grid=(steps,),
            in_specs=[
                whole((rows, hidden)),
                whole((rows, hidden)),
                whole(put.shape),
                pl.BlockSpec((hidden, width), lambda i, info: (0, info[3] * steps + i)),
                pl.BlockSpec((hidden, width), lambda i, info: (0, i)),
                pl.BlockSpec((held.shape[0], width), lambda i, info: (0, i)),
            ],
            out_specs=pl.BlockSpec(
                (chips, 1, 3 * SUB, LANES), lambda i, info: (0, i, 0, 0)
            ),
            scratch_shapes=[pltpu.VMEM((chips * SUB, hidden), BF16)] * 2,
        ),
        compiler_params=params("arbitrary"),
        cost_estimate=cost(4 * chips * SUB * hidden * half, 6_000_000),
        name="down",
    )(info, mine, theirs, put, down_proj, down_theirs, held)


def finish_kernel(info_ref, parts_ref, mine_ref, theirs_ref):
    total = jnp.sum(parts_ref[...].astype(F32), axis=0)
    sub = lax.broadcasted_iota(jnp.int32, (SUB, LANES), 0)
    columns = []
    for step in range(total.shape[0]):
        quads = [total[step, tile * SUB : tile * SUB + SUB] for tile in range(3)]
        last = jnp.where(
            sub < 2,
            pltpu.roll(quads[0], 2, 0),
            jnp.where(sub < 4, pltpu.roll(quads[1], 4, 0), pltpu.roll(quads[2], 6, 0)),
        )
        columns += quads + [last]
    rows = jnp.concatenate(columns, axis=1)
    first, second = rows[0:3], rows[3:6]
    is_first = info_ref[3] == 0
    mine_ref[...] = jnp.where(is_first, first, second).astype(BF16)
    theirs_ref[...] = jnp.where(is_first, second, first).astype(BF16)


def finish(info, parts):
    shape = jax.ShapeDtypeStruct((3, parts.shape[1] * 4 * LANES), BF16)
    return pl.pallas_call(
        finish_kernel,
        out_shape=(shape, shape),
        in_specs=[pl.BlockSpec(memory_space=pltpu.SMEM), WHOLE],
        out_specs=(WHOLE, WHOLE),
        compiler_params=params(),
        cost_estimate=cost(1_000_000, 1_500_000),
        name="finish",
    )(info, parts)


def local(
    query_latent,
    latent_cache,
    lengths,
    stream,
    norm_gain,
    value_up,
    out_proj,
    gate_proj,
    up_proj,
    down_proj,
):
    core = lax.axis_index("core")
    ring = lax.axis_index("y")
    group = lax.axis_index("zl") * 4 + lax.axis_index("x")
    rows_own, width = stream.shape
    rows = query_latent.shape[0]
    half = width // 2
    eighth = width // 8
    first = core == 0
    info = jnp.stack([core * 4 + ring, core, group, core, 1 - core]).astype(jnp.int32)

    def ring_part(step):
        chip = (ring + step) % 4
        return jnp.concatenate(
            [
                lax.dynamic_slice_in_dim(out_proj, start + chip * eighth, eighth, 1)
                for start in (0, half)
            ],
            axis=1,
        )

    part_one, part_three = shift(ring_part(1), 1), shift(ring_part(3), 3)
    stream_mine, stream_theirs = swap_halves(stream, core, 1)
    stream_rows = jnp.concatenate(
        [
            jnp.where(first, stream_mine, stream_theirs),
            jnp.where(first, stream_theirs, stream_mine),
        ],
        axis=0,
    )
    stream_parts = [block(stream_rows, ring, eighth, 1)]
    for step in (1, 2, 3):
        stream_parts.append(shift(block(stream_rows, (ring + step) % 4, eighth, 1), step))
    back = (ring - jnp.arange(4)) % 4
    ring_stream = jnp.take(jnp.stack(stream_parts), back, axis=0)
    ring_stream = ring_stream.reshape(8 * rows_own, eighth)
    _, down_theirs = swap_halves(down_proj, core, 1)
    gain = block(norm_gain, core * 4 + ring, eighth, 0)[None]

    offset = lax.axis_index("zh") * latent_cache.shape[1]
    payload = attend(
        jnp.concatenate([lengths, offset[None].astype(jnp.int32)]), query_latent, latent_cache
    )
    payload, part_one, part_three = lax.optimization_barrier((payload, part_one, part_three))
    part_two = shift(lax.optimization_barrier((ring_part(2), part_one))[0], 2)
    received = lax.all_to_all(payload, AXES, split_axis=0, concat_axis=0, tiled=True)
    values = join(received, value_up, rows)

    ring_values = [values] + [shift(values, step) for step in (1, 2, 3)]
    parts = [part_one, part_two, part_three]
    theirs = [swap(block(out_proj, (1 - core) * 4 + ring, eighth, 1))]
    theirs += [swap(block(part, 1 - core, eighth, 1)) for part in parts]
    partial = project(
        info,
        ring_values + [swap(piece) for piece in ring_values],
        out_proj,
        parts,
        theirs,
        16,
    )
    parts = lax.all_to_all(partial, OUTER, split_axis=0, concat_axis=0, tiled=True)

    residual, payload = residual_rows(parts, ring_stream, gain, 32)
    held = residual.reshape(4, 2 * rows_own, eighth)
    held = jnp.pad(held, ((0, 0), (0, SUB - 2 * rows_own), (0, 0))).reshape(4 * SUB, eighth)
    held = lax.dynamic_update_slice(
        jnp.zeros((4 * SUB, half), F32), held, (0, ring * eighth)
    )
    piece = lax.all_to_all(payload, SIDE_CHIPS, split_axis=0, concat_axis=0, tiled=True)
    piece = piece.reshape((8, 4) + piece.shape[1:])
    other = swap(piece)
    groups = 8 * rows_own // SUB
    carry = units(info, 3, piece, gate_proj, up_proj, groups)
    hidden = units(info, 4, other, gate_proj, up_proj, groups, carry)
    partial = down(info, hidden, swap(hidden), down_proj, down_theirs, held, 32)
    parts = lax.all_to_all(partial, SIDE_CHIPS, split_axis=0, concat_axis=0, tiled=True)
    mine, theirs = finish(info, parts)
    theirs = swap(theirs)
    return jnp.concatenate(
        [jnp.where(first, mine, theirs), jnp.where(first, theirs, mine)], axis=1
    )


def solution(mesh):
    fine = Mesh(mesh.devices.reshape(2, 2, 4, 4, 2), AXES)
    placed = (
        P(DEV, None, None),
        P(DEV, "zh", None),
        P(DEV),
        P(AXES, None),
        P(),
        P(AXES, None, None),
        P(AXES, None),
        P(None, DEV),
        P(None, DEV),
        P(DEV, None),
    )
    return jax.shard_map(
        local, mesh=fine, in_specs=placed, out_specs=P(AXES, None), check_vma=False
    )
```

```python
import functools
import math

import jax
import jax.numpy as jnp
import numpy as np
from jax import lax
from jax.experimental import pallas as pl
from jax.experimental.pallas import tpu as pltpu
from jax.sharding import Mesh, PartitionSpec as P

LAT = 512
QKD = 192
LANES = 128
SUB = 8
AXES = ("zh", "zl", "x", "y", "core")
DEV = ("zl", "x", "y", "core")
OUTER = ("zh", "zl", "x")
SIDE_CHIPS = ("zl", "x", "y")
SWAP = [(0, 1), (1, 0)]
F32 = jnp.float32
BF16 = jnp.bfloat16
VMEM_MOST = 60 * 1024 * 1024
VMEM_SOME = 24 * 1024 * 1024


def swap(array):
    return lax.ppermute(array, "core", SWAP)


def shift(array, step):
    return lax.ppermute(array, "y", [(i, (i + step) % 4) for i in range(4)])


def block(array, index, size, axis):
    return lax.dynamic_slice_in_dim(array, index * size, size, axis)


def swap_halves(array, core, axis):
    half = array.shape[axis] // 2
    return block(array, core, half, axis), swap(block(array, 1 - core, half, axis))


def params(limit, *semantics):
    return pltpu.CompilerParams(
        vmem_limit_bytes=limit, dimension_semantics=semantics or None
    )


def cost(flops, read):
    return pl.CostEstimate(flops=flops, bytes_accessed=read, transcendentals=0)


WHOLE = pl.BlockSpec(memory_space=pltpu.VMEM)


def rounded(value):
    return value.astype(BF16).astype(F32)


def attend_kernel(rows, info_ref, query_ref, cache_ref, out_ref, stats):
    count, _, heads = query_ref.shape
    keys = cache_ref.shape[2]
    tiles = [slice(start, start + LANES) for start in range(0, LAT, LANES)]
    position = lax.broadcasted_iota(jnp.int32, (1, keys), 1) + info_ref[rows]
    lane = lax.broadcasted_iota(jnp.int32, (heads, LANES), 1)
    table = stats[...]
    for index in range(count):
        row = pl.program_id(0) * count + index
        cached = cache_ref[index]
        scores = lax.dot_general(
            query_ref[index], cached, (((0,), (0,)), ((), ())), preferred_element_type=F32
        ) * (1.0 / math.sqrt(QKD))
        usable = position < info_ref[row]
        scores = jnp.where(usable, scores, F32(-1e30))
        top = jnp.max(scores, axis=1, keepdims=True)
        top_high = rounded(top)
        top_low = rounded(top - top_high)
        exponent = jnp.where(usable, jnp.exp(scores - (top_high + top_low)), F32(0.0))
        total = jnp.sum(exponent, axis=1, keepdims=True)
        total_high = rounded(total)
        total_low = rounded(total - total_high)
        weighted = lax.dot_general(
            exponent.astype(BF16),
            cached[:LAT],
            (((1,), (1,)), ((), ())),
            preferred_element_type=F32,
        )
        for number, tile in enumerate(tiles):
            out_ref[:, row * len(tiles) + number] = (
                weighted[:, tile].reshape(heads // SUB, SUB, LANES).astype(BF16)
            )
        table = jnp.where(lane == row, top_high, table)
        table = jnp.where(lane == row + SUB, top_low, table)
        table = jnp.where(lane == row + 2 * SUB, total_high, table)
        table = jnp.where(lane == row + 3 * SUB, total_low, table)
    stats[...] = table

    @pl.when(pl.program_id(0) == pl.num_programs(0) - 1)
    def _():
        out_ref[:, rows * len(tiles)] = (
            stats[...].reshape(heads // SUB, SUB, LANES).astype(BF16)
        )


def attend(info, query, cache):
    rows, depth, heads = query.shape
    keys = cache.shape[2]
    count = 2
    shape = (heads // SUB, rows * (LAT // LANES) + 1, SUB, LANES)
    return pl.pallas_call(
        functools.partial(attend_kernel, rows),
        out_shape=jax.ShapeDtypeStruct(shape, BF16),
        grid_spec=pltpu.PrefetchScalarGridSpec(
            num_scalar_prefetch=1,
            grid=(rows // count,),
            in_specs=[
                pl.BlockSpec((count, depth, heads), lambda r, info: (r, 0, 0)),
                pl.BlockSpec((count, depth, keys), lambda r, info: (r, 0, 0)),
            ],
            out_specs=pl.BlockSpec(shape, lambda r, info: (0, 0, 0, 0)),
            scratch_shapes=[pltpu.VMEM((heads, LANES), F32)],
        ),
        compiler_params=params(VMEM_MOST, "arbitrary"),
        cost_estimate=cost(2 * rows * heads * keys * (depth + LAT), 5_000_000),
        name="attend",
    )(info, query, cache)


def cut_kernel(info_ref, up_ref, *refs):
    del info_ref
    blocks, outs = refs[:7], refs[7:]
    lanes = [slice(start, start + LANES) for start in range(0, blocks[0].shape[1], LANES)]
    ups = up_ref.shape[1] // LANES
    for step in range(4):
        outs[step][:ups] = up_ref[0].reshape(ups, LANES, LANES)
        for index, lane in enumerate(lanes):
            outs[step][ups + index] = blocks[step][:, lane]
    for step in range(3):
        for index, lane in enumerate(lanes):
            outs[4 + step][index] = blocks[4 + step][:, lane]


def cut(info, value_up, out_proj):
    rows, width = out_proj.shape
    eighth = width // 8
    columns = eighth // LANES
    ups = value_up.shape[1] // LANES
    first = (ups + columns, LANES, LANES)
    second = (columns, LANES, LANES)
    full = lambda shape: pl.BlockSpec(shape, lambda i, info: (0,) * len(shape))

    def column(side, step):
        return pl.BlockSpec(
            (rows, eighth),
            lambda i, info: (0, info[side] * 4 + lax.rem(info[5] + step, 4)),
        )

    return pl.pallas_call(
        cut_kernel,
        out_shape=[jax.ShapeDtypeStruct(first, BF16)] * 4
        + [jax.ShapeDtypeStruct(second, BF16)] * 3,
        grid_spec=pltpu.PrefetchScalarGridSpec(
            num_scalar_prefetch=1,
            grid=(1,),
            in_specs=[full(value_up.shape)]
            + [column(4, step) for step in range(4)]
            + [column(3, step) for step in range(1, 4)],
            out_specs=[full(first)] * 4 + [full(second)] * 3,
        ),
        compiler_params=params(VMEM_SOME, "arbitrary"),
        cost_estimate=cost(0, 4_000_000),
        name="cut",
    )(info, value_up, *([out_proj] * 7))


def join_kernel(rows, info_ref, recv_ref, own_ref, *refs):
    firsts, theirs, sum_ref, out_ref = refs[:3], refs[3:7], refs[7], refs[8]
    sides = 2
    devs = recv_ref.shape[0] // sides
    tiles = LAT // LANES
    table = recv_ref[:, rows * tiles].astype(F32).reshape(sides, devs, SUB, LANES)
    lane = lax.broadcasted_iota(jnp.int32, (SUB, LANES), 1)

    def pick(first):
        chosen = (lane == first) | (lane == first + SUB)
        return jnp.sum(jnp.where(chosen, table, F32(0.0)), axis=3, keepdims=True)

    latents = []
    for row in range(rows):
        peaks = pick(row)
        totals = pick(2 * SUB + row)
        factor = jnp.exp(peaks - jnp.maximum(peaks[:1], peaks[1:]))
        factor = factor / (factor[:1] * totals[:1] + factor[1:] * totals[1:])
        parts = [
            recv_ref[:, row * tiles + number].astype(F32).reshape(sides, devs, SUB, LANES)
            for number in range(tiles)
        ]
        joined = [part[0] * factor[0] + part[1] * factor[1] for part in parts]
        latents.append(
            jnp.concatenate([part.reshape(devs * SUB, LANES) for part in joined], axis=1)
        )
    latent = jnp.concatenate(latents, axis=0).astype(BF16)
    maps = [own_ref[0]]
    maps += [ref[:tiles].reshape(LAT, LANES) for ref in firsts]
    maps += [ref[:tiles].reshape(LAT, LANES) for ref in theirs]
    products = jnp.dot(
        latent, jnp.concatenate(maps, axis=1), preferred_element_type=F32
    ).reshape(rows * devs, SUB, len(maps) * LANES)
    sub = lax.broadcasted_iota(jnp.int32, (1, SUB, LANES), 1)
    masked = []
    for piece in range(len(maps)):
        chip = lax.rem(info_ref[5] + 4 - piece % 4, 4)
        head = chip * 2 + info_ref[3 + piece // 4]
        part = products[:, :, piece * LANES : piece * LANES + LANES]
        masked.append(jnp.where(sub == head, part, F32(0.0)))
    masked = jnp.concatenate(masked, axis=2).reshape(rows * devs * SUB, len(maps) * LANES)
    out_ref[...] = jnp.dot(
        sum_ref[...], masked.astype(BF16), preferred_element_type=F32
    ).astype(BF16)


def join(info, received, value_up, firsts, theirs, rows):
    devs = received.shape[0] // 2
    count = rows * devs
    sums = np.repeat(np.eye(count, dtype=np.float32), SUB, axis=1)
    return pl.pallas_call(
        functools.partial(join_kernel, rows),
        out_shape=jax.ShapeDtypeStruct((count, SUB * LANES), BF16),
        in_specs=[pl.BlockSpec(memory_space=pltpu.SMEM)] + [WHOLE] * 10,
        out_specs=WHOLE,
        compiler_params=params(VMEM_SOME),
        cost_estimate=cost(480_000_000, 3_000_000),
        name="join",
    )(info, received, value_up, *firsts, *theirs, jnp.asarray(sums, BF16))


def project_kernel(info_ref, place_ref, *refs):
    values, own_ref = refs[:8], refs[8]
    seconds, theirs, out_ref = refs[9:12], refs[12:16], refs[16]
    del info_ref
    rows = []
    for source, ref in enumerate(values):
        data = ref[...]
        lanes = []
        for piece in range(8):
            step = (piece - source) % 4
            side = piece // 4 ^ source // 4
            start = (side * 4 + step) * LANES
            lanes.append(data[:, start : start + LANES])
        rows.append(jnp.concatenate(lanes, axis=1))
    left = jnp.concatenate(rows, axis=0)
    count = left.shape[0]
    order = lax.broadcasted_iota(jnp.int32, (count, count), 0) == place_ref[...]
    order = jnp.where(order, F32(1.0), F32(0.0)).astype(BF16)
    left = jnp.dot(order, left, preferred_element_type=F32).astype(BF16)
    columns = own_ref.shape[1] // LANES
    right = [own_ref[...]]
    for ref in seconds + theirs:
        first = ref.shape[0] - columns
        right.append(
            jnp.concatenate([ref[first + column] for column in range(columns)], axis=1)
        )
    right = jnp.concatenate(right, axis=0)
    total = jnp.dot(left, right, preferred_element_type=F32)
    out_ref[...] = total.reshape(out_ref.shape).astype(BF16)


def project(info, place, values, out_proj, seconds, theirs, chips):
    rows = sum(value.shape[0] for value in values)
    lanes = out_proj.shape[0]
    eighth = out_proj.shape[1] // 8
    full = lambda shape: pl.BlockSpec(shape, lambda i, info: (0,) * len(shape))
    own = pl.BlockSpec((lanes, eighth), lambda i, info: (0, info[0]))
    return pl.pallas_call(
        project_kernel,
        out_shape=jax.ShapeDtypeStruct((chips, rows // chips, eighth), BF16),
        grid_spec=pltpu.PrefetchScalarGridSpec(
            num_scalar_prefetch=1,
            grid=(1,),
            in_specs=[full(place.shape)]
            + [full(value.shape) for value in values]
            + [own]
            + [full(part.shape) for part in seconds + theirs],
            out_specs=full((chips, rows // chips, eighth)),
        ),
        compiler_params=params(VMEM_SOME, "arbitrary"),
        cost_estimate=cost(2 * rows * 8 * lanes * eighth, 3_500_000),
        name="project",
    )(info, place, *values, out_proj, *seconds, *theirs)


def residual_kernel(parts_ref, stream_ref, gain_ref, residual_ref, out_ref):
    residual = stream_ref[...].astype(F32) + jnp.sum(parts_ref[...].astype(F32), axis=0)
    residual_ref[...] = residual
    rows, width = residual.shape
    squares = jnp.sum(residual * residual, axis=1, keepdims=True)
    high = rounded(squares)
    low = rounded(squares - high)
    lane = lax.broadcasted_iota(jnp.int32, (SUB, LANES), 1)
    table = jnp.zeros((SUB, LANES), F32)
    scaled = residual * gain_ref[...]
    groups = rows // SUB
    columns = width // LANES
    chips = out_ref.shape[0]
    for group in range(groups):
        span = slice(group * SUB, group * SUB + SUB)
        table = jnp.where(lane == group, high[span], table)
        table = jnp.where(lane == SUB + group, low[span], table)
    tiles = [
        scaled[group * SUB : group * SUB + SUB, column * LANES : column * LANES + LANES]
        for column in range(columns)
        for group in range(groups)
    ] + [table]
    for index, tile in enumerate(tiles):
        out_ref[:, index] = jnp.broadcast_to(tile.astype(BF16)[None], (chips, SUB, LANES))


def residual_rows(parts, stream, gain, chips):
    _, rows, width = parts.shape
    tiles = rows * width // (SUB * LANES) + 1
    return pl.pallas_call(
        residual_kernel,
        out_shape=(
            jax.ShapeDtypeStruct((rows, width), F32),
            jax.ShapeDtypeStruct((chips, tiles, SUB, LANES), BF16),
        ),
        in_specs=[WHOLE] * 3,
        out_specs=(WHOLE, WHOLE),
        compiler_params=params(VMEM_SOME),
        cost_estimate=cost(2_000_000, 2_500_000),
        name="residual",
    )(parts, stream, gain)


def units_kernel(groups, width, last, info_ref, *refs):
    if last:
        recv_ref, gate_ref, up_ref, acc_in, sq_in, out_ref, acc, sq_acc = refs
    else:
        recv_ref, gate_ref, up_ref, acc, sq_acc = refs
    step = pl.program_id(0)
    sides, _, tiles, _, _ = recv_ref.shape
    columns = (tiles - 1) // groups
    rows = sides * groups * SUB
    left = jnp.concatenate(
        [
            recv_ref[:, 0, column * groups : column * groups + groups]
            .astype(F32)
            .reshape(rows, LANES)
            for column in range(columns)
        ],
        axis=1,
    ).astype(BF16)
    both = jnp.concatenate([gate_ref[...], up_ref[...]], axis=0)
    total = lax.dot_general(
        left, both, (((1,), (1,)), ((), ())), preferred_element_type=F32
    )
    table = recv_ref[:, 0, tiles - 1].astype(F32)
    lane = lax.broadcasted_iota(jnp.int32, (SUB, LANES), 1)
    pieces = [
        jnp.sum(
            jnp.where((lane == group) | (lane == SUB + group), table, F32(0.0)),
            axis=2,
            keepdims=True,
        )
        for group in range(groups)
    ]
    squares = jnp.stack(pieces, axis=1).reshape(rows, 1)
    squares = jnp.broadcast_to(squares, (rows, LANES))

    @pl.when(step == 0)
    def _():
        acc[...] = acc_in[...] + total if last else total
        sq_acc[...] = sq_in[...] + squares if last else squares

    @pl.when(step > 0)
    def _():
        acc[...] += total
        sq_acc[...] += squares

    if last:

        @pl.when(step == pl.num_programs(0) - 1)
        def _():
            hidden = out_ref.shape[1]
            scale = lax.rsqrt(sq_acc[:, :1] / width + 1e-06)
            gate = acc[:, :hidden] * scale
            upper = acc[:, hidden:] * scale
            out_ref[...] = (gate / (1.0 + jnp.exp(-gate)) * upper).astype(BF16)


def units(info, which, received, gate_proj, up_proj, groups, carry=None):
    sides, quarters, tiles = received.shape[:3]
    depth = (tiles - 1) // groups * LANES
    hidden, width = gate_proj.shape
    rows = sides * groups * SUB
    whole = lambda shape: pl.BlockSpec(shape, lambda i, info: (0,) * len(shape))
    weight = pl.BlockSpec((hidden, depth), lambda i, info: (0, info[which] * quarters + i))
    shapes = [(rows, 2 * hidden), (rows, LANES)]
    last = carry is not None
    return pl.pallas_call(
        functools.partial(units_kernel, groups, width, last),
        out_shape=jax.ShapeDtypeStruct((rows, hidden), BF16)
        if last
        else [jax.ShapeDtypeStruct(shape, F32) for shape in shapes],
        grid_spec=pltpu.PrefetchScalarGridSpec(
            num_scalar_prefetch=1,
            grid=(quarters,),
            in_specs=[
                pl.BlockSpec(
                    (sides, 1, tiles, SUB, LANES), lambda i, info: (0, i, 0, 0, 0)
                ),
                weight,
                weight,
            ]
            + ([whole(shape) for shape in shapes] if last else []),
            out_specs=whole((rows, hidden)) if last else [whole(shape) for shape in shapes],
            scratch_shapes=[pltpu.VMEM(shape, F32) for shape in shapes] if last else [],
        ),
        compiler_params=params(VMEM_MOST, "arbitrary"),
        cost_estimate=cost(4 * rows * depth * quarters * hidden, 5_000_000),
        name="units_last" if last else "units_first",
    )(info, received, gate_proj, up_proj, *(carry or ()))


def down_kernel(info_ref, mine_ref, theirs_ref, own_ref, other_ref, held_ref, out_ref, left, total):
    chips = out_ref.shape[0]
    rows = mine_ref.shape[0]
    count = rows // chips
    hidden = mine_ref.shape[1]

    @pl.when(pl.program_id(0) == 0)
    def _():
        left[...] = jnp.concatenate(
            [mine_ref[...].astype(F32), theirs_ref[...].astype(F32)], axis=1
        ).astype(BF16)
        total[pl.ds(rows, SUB), :] = jnp.zeros((SUB, total.shape[1]), F32)

    weight = jnp.concatenate([own_ref[...], other_ref[...]], axis=0)
    total[pl.ds(0, rows), :] = jnp.dot(left[...], weight, preferred_element_type=F32)
    span = held_ref.shape[0]
    place = pl.ds(pl.multiple_of(info_ref[2] * span, SUB), span)
    total[place, :] += held_ref[...]
    sub = lax.broadcasted_iota(jnp.int32, (SUB, LANES), 0)
    for chip in range(chips):
        part = total[chip * count : chip * count + SUB, :]
        quads = [part[:, tile * LANES : tile * LANES + LANES] for tile in range(4)]
        packed = [
            jnp.where(sub < count, quads[tile], pltpu.roll(quads[3], count - 2 * tile, 0))
            for tile in range(3)
        ]
        out_ref[chip, 0] = jnp.concatenate(packed, axis=0).astype(BF16)


def down(info, mine, theirs, down_proj, down_theirs, held, chips):
    rows, hidden = mine.shape
    half = down_theirs.shape[1]
    width = 4 * LANES
    steps = half // width
    whole = lambda shape: pl.BlockSpec(shape, lambda i, info: (0,) * len(shape))
    return pl.pallas_call(
        down_kernel,
        out_shape=jax.ShapeDtypeStruct((chips, steps, 3 * SUB, LANES), BF16),
        grid_spec=pltpu.PrefetchScalarGridSpec(
            num_scalar_prefetch=1,
            grid=(steps,),
            in_specs=[
                whole((rows, hidden)),
                whole((rows, hidden)),
                pl.BlockSpec((hidden, width), lambda i, info: (0, info[3] * steps + i)),
                pl.BlockSpec((hidden, width), lambda i, info: (0, i)),
                pl.BlockSpec((held.shape[0], width), lambda i, info: (0, i)),
            ],
            out_specs=pl.BlockSpec(
                (chips, 1, 3 * SUB, LANES), lambda i, info: (0, i, 0, 0)
            ),
            scratch_shapes=[
                pltpu.VMEM((rows, 2 * hidden), BF16),
                pltpu.VMEM((rows + SUB, width), F32),
            ],
        ),
        compiler_params=params(VMEM_SOME, "arbitrary"),
        cost_estimate=cost(4 * rows * hidden * half, 6_000_000),
        name="down",
    )(info, mine, theirs, down_proj, down_theirs, held)


def finish_kernel(info_ref, parts_ref, mine_ref, theirs_ref):
    total = jnp.sum(parts_ref[...].astype(F32), axis=0)
    sub = lax.broadcasted_iota(jnp.int32, (SUB, LANES), 0)
    columns = []
    for step in range(total.shape[0]):
        quads = [total[step, tile * SUB : tile * SUB + SUB] for tile in range(3)]
        last = jnp.where(
            sub < 2,
            pltpu.roll(quads[0], 2, 0),
            jnp.where(sub < 4, pltpu.roll(quads[1], 4, 0), pltpu.roll(quads[2], 6, 0)),
        )
        columns += quads + [last]
    rows = jnp.concatenate(columns, axis=1)
    first, second = rows[0:3], rows[3:6]
    is_first = info_ref[3] == 0
    mine_ref[...] = jnp.where(is_first, first, second).astype(BF16)
    theirs_ref[...] = jnp.where(is_first, second, first).astype(BF16)


def finish(info, parts):
    shape = jax.ShapeDtypeStruct((3, parts.shape[1] * 4 * LANES), BF16)
    return pl.pallas_call(
        finish_kernel,
        out_shape=(shape, shape),
        in_specs=[pl.BlockSpec(memory_space=pltpu.SMEM), WHOLE],
        out_specs=(WHOLE, WHOLE),
        compiler_params=params(VMEM_SOME),
        cost_estimate=cost(1_000_000, 1_500_000),
        name="finish",
    )(info, parts)


def local(
    query_latent,
    latent_cache,
    lengths,
    stream,
    norm_gain,
    value_up,
    out_proj,
    gate_proj,
    up_proj,
    down_proj,
):
    core = lax.axis_index("core")
    ring = lax.axis_index("y")
    group = lax.axis_index("zl") * 4 + lax.axis_index("x")
    rows_own, width = stream.shape
    rows = query_latent.shape[0]
    half = width // 2
    eighth = width // 8
    first = core == 0
    info = jnp.stack([core * 4 + ring, core, group, core, 1 - core, ring]).astype(jnp.int32)

    cuts = cut(info, value_up, out_proj)
    own = cuts[0]
    first_one, first_three = shift(cuts[1], 1), shift(cuts[3], 3)
    stream_mine, stream_theirs = swap_halves(stream, core, 1)
    stream_rows = jnp.concatenate(
        [
            jnp.where(first, stream_mine, stream_theirs),
            jnp.where(first, stream_theirs, stream_mine),
        ],
        axis=0,
    )
    stream_parts = [block(stream_rows, ring, eighth, 1)]
    for step in (1, 2, 3):
        stream_parts.append(shift(block(stream_rows, (ring + step) % 4, eighth, 1), step))
    back = (ring - jnp.arange(4)) % 4
    ring_stream = jnp.take(jnp.stack(stream_parts), back, axis=0)
    ring_stream = ring_stream.reshape(8 * rows_own, eighth)
    _, down_theirs = swap_halves(down_proj, core, 1)
    gain = block(norm_gain, core * 4 + ring, eighth, 0)[None]

    offset = lax.axis_index("zh") * latent_cache.shape[1]
    payload = attend(
        jnp.concatenate([lengths, offset[None].astype(jnp.int32)]),
        query_latent.transpose(0, 2, 1),
        latent_cache.transpose(0, 2, 1),
    )
    payload, first_one, first_three = lax.optimization_barrier(
        (payload, first_one, first_three)
    )
    first_two = shift(lax.optimization_barrier((cuts[2], first_one))[0], 2)
    seconds = [shift(cuts[3 + step], step) for step in (1, 2, 3)]
    firsts = [first_one, first_two, first_three]
    theirs = [swap(part) for part in [own] + firsts]
    received = lax.all_to_all(payload, OUTER, split_axis=0, concat_axis=0, tiled=True)
    values = join(info, received, value_up, firsts, theirs, rows)

    ring_values = [values] + [shift(values, step) for step in (1, 2, 3)]
    row = jnp.arange(8 * rows)
    natural = jnp.tile(row % 8 * (8 * rows) + row // 8, 8).reshape(8, 8 * rows)
    chip = (ring - jnp.arange(8)) % 4
    side = jnp.where(jnp.arange(8) < 4, core, 1 - core)
    place = natural[:, : 8 * rows] + ((chip * 2 + side) * rows)[:, None]
    place = place.reshape(1, 64 * rows).astype(jnp.int32)
    partial = project(
        info,
        place,
        ring_values + [swap(piece) for piece in ring_values],
        out_proj,
        seconds,
        theirs,
        16,
    )
    parts = lax.all_to_all(partial, OUTER, split_axis=0, concat_axis=0, tiled=True)

    residual, payload = residual_rows(parts, ring_stream, gain, 32)
    held = lax.dynamic_update_slice(
        jnp.zeros((8 * rows_own, half), F32), residual, (0, ring * eighth)
    )
    piece = lax.all_to_all(payload, SIDE_CHIPS, split_axis=0, concat_axis=0, tiled=True)
    piece = piece.reshape((8, 4) + piece.shape[1:])
    other = swap(piece)
    groups = 8 * rows_own // SUB
    gate_proj, up_proj = gate_proj.T, up_proj.T
    carry = units(info, 3, piece, gate_proj, up_proj, groups)
    hidden = units(info, 4, other, gate_proj, up_proj, groups, carry)
    partial = down(info, hidden, swap(hidden), down_proj, down_theirs, held, 32)
    parts = lax.all_to_all(partial, SIDE_CHIPS, split_axis=0, concat_axis=0, tiled=True)
    mine, theirs = finish(info, parts)
    theirs = swap(theirs)
    return jnp.concatenate(
        [jnp.where(first, mine, theirs), jnp.where(first, theirs, mine)], axis=1
    )


def solution(mesh):
    fine = Mesh(mesh.devices.reshape(2, 2, 4, 4, 2), AXES)
    placed = (
        P(DEV, None, None),
        P(DEV, "zh", None),
        P(DEV),
        P(AXES, None),
        P(),
        P(AXES, None, None),
        P(AXES, None),
        P(None, DEV),
        P(None, DEV),
        P(DEV, None),
    )
    return jax.shard_map(
        local, mesh=fine, in_specs=placed, out_specs=P(AXES, None), check_vma=False
    )
```

```python
import functools
import math

import jax
import jax.numpy as jnp
import numpy as np
from jax import lax
from jax.experimental import pallas as pl
from jax.experimental.pallas import tpu as pltpu
from jax.sharding import Mesh, PartitionSpec as P

LAT = 512
QKD = 192
LANES = 128
SUB = 8
AXES = ("zh", "zl", "x", "y", "core")
DEV = ("zl", "x", "y", "core")
OUTER = ("zh", "zl", "x")
SIDE_CHIPS = ("zl", "x", "y")
SWAP = [(0, 1), (1, 0)]
F32 = jnp.float32
BF16 = jnp.bfloat16
VMEM_MOST = 60 * 1024 * 1024
VMEM_SOME = 24 * 1024 * 1024


def swap(array):
    return lax.ppermute(array, "core", SWAP)


def shift(array, step):
    return lax.ppermute(array, "y", [(i, (i + step) % 4) for i in range(4)])


def block(array, index, size, axis):
    return lax.dynamic_slice_in_dim(array, index * size, size, axis)


def params(limit, *semantics):
    return pltpu.CompilerParams(
        vmem_limit_bytes=limit, dimension_semantics=semantics or None
    )


def cost(flops, read):
    return pl.CostEstimate(flops=flops, bytes_accessed=read, transcendentals=0)


WHOLE = pl.BlockSpec(memory_space=pltpu.VMEM)


def rounded(value):
    return value.astype(BF16).astype(F32)


def attend_kernel(rows, info_ref, query_ref, cache_ref, out_ref, stats):
    count, _, heads = query_ref.shape
    keys = cache_ref.shape[2]
    tiles = [slice(start, start + LANES) for start in range(0, LAT, LANES)]
    position = lax.broadcasted_iota(jnp.int32, (1, keys), 1) + info_ref[rows]
    lane = lax.broadcasted_iota(jnp.int32, (heads, LANES), 1)
    table = stats[...]
    for index in range(count):
        row = pl.program_id(0) * count + index
        cached = cache_ref[index]
        scores = lax.dot_general(
            query_ref[index], cached, (((0,), (0,)), ((), ())), preferred_element_type=F32
        ) * (1.0 / math.sqrt(QKD))
        usable = position < info_ref[row]
        scores = jnp.where(usable, scores, F32(-1e30))
        top = jnp.max(scores, axis=1, keepdims=True)
        top_high = rounded(top)
        top_low = rounded(top - top_high)
        exponent = jnp.where(usable, jnp.exp(scores - (top_high + top_low)), F32(0.0))
        total = jnp.sum(exponent, axis=1, keepdims=True)
        total_high = rounded(total)
        total_low = rounded(total - total_high)
        weighted = lax.dot_general(
            exponent.astype(BF16),
            cached[:LAT],
            (((1,), (1,)), ((), ())),
            preferred_element_type=F32,
        )
        for number, tile in enumerate(tiles):
            out_ref[:, row * len(tiles) + number] = (
                weighted[:, tile].reshape(heads // SUB, SUB, LANES).astype(BF16)
            )
        table = jnp.where(lane == row, top_high, table)
        table = jnp.where(lane == row + SUB, top_low, table)
        table = jnp.where(lane == row + 2 * SUB, total_high, table)
        table = jnp.where(lane == row + 3 * SUB, total_low, table)
    stats[...] = table

    @pl.when(pl.program_id(0) == pl.num_programs(0) - 1)
    def _():
        out_ref[:, rows * len(tiles)] = (
            stats[...].reshape(heads // SUB, SUB, LANES).astype(BF16)
        )


def attend(info, query, cache):
    rows, depth, heads = query.shape
    keys = cache.shape[2]
    count = 2
    shape = (heads // SUB, rows * (LAT // LANES) + 1, SUB, LANES)
    return pl.pallas_call(
        functools.partial(attend_kernel, rows),
        out_shape=jax.ShapeDtypeStruct(shape, BF16),
        grid_spec=pltpu.PrefetchScalarGridSpec(
            num_scalar_prefetch=1,
            grid=(rows // count,),
            in_specs=[
                pl.BlockSpec((count, depth, heads), lambda r, info: (r, 0, 0)),
                pl.BlockSpec((count, depth, keys), lambda r, info: (r, 0, 0)),
            ],
            out_specs=pl.BlockSpec(shape, lambda r, info: (0, 0, 0, 0)),
            scratch_shapes=[pltpu.VMEM((heads, LANES), F32)],
        ),
        compiler_params=params(VMEM_MOST, "arbitrary"),
        cost_estimate=cost(2 * rows * heads * keys * (depth + LAT), 5_000_000),
        name="attend",
    )(info, query, cache)


def early_kernel(info_ref, up_ref, stream_ref, *outs):
    rows, width = stream_ref.shape
    eighth = width // 8
    ups = up_ref.shape[1] // LANES
    for step, out_ref in enumerate(outs):
        out_ref[:ups] = up_ref[0].reshape(ups, LANES, LANES)
        chip = lax.rem(info_ref[5] + step, 4)
        lines = []
        for side in (3, 4):
            start = pl.multiple_of((info_ref[side] * 4 + chip) * eighth, LANES)
            data = stream_ref[:, pl.ds(start, eighth)].astype(F32)
            for lane in range(0, eighth, LANES):
                lines.append(data[:, lane : lane + LANES])
                lines.append(jnp.zeros((SUB - rows, LANES), F32))
            lines.append(jnp.zeros((LANES // 2 - eighth // LANES * SUB, LANES), F32))
        out_ref[ups] = jnp.concatenate(lines, axis=0).astype(BF16)


def early(info, value_up, stream):
    shape = (value_up.shape[1] // LANES + 1, LANES, LANES)
    return pl.pallas_call(
        early_kernel,
        out_shape=[jax.ShapeDtypeStruct(shape, BF16)] * 4,
        in_specs=[pl.BlockSpec(memory_space=pltpu.SMEM), WHOLE, WHOLE],
        out_specs=[WHOLE] * 4,
        compiler_params=params(VMEM_SOME),
        cost_estimate=cost(0, 800_000),
        name="early",
    )(info, value_up, stream)


def cut_kernel(info_ref, *refs):
    del info_ref
    count = len(refs) // 2
    for source, out_ref in zip(refs[:count], refs[count:]):
        for index in range(out_ref.shape[0]):
            out_ref[index] = source[:, index * LANES : index * LANES + LANES]


def cut(info, out_proj):
    rows, width = out_proj.shape
    eighth = width // 8
    shape = (eighth // LANES, rows, LANES)

    def column(side, step):
        return pl.BlockSpec(
            (rows, eighth),
            lambda i, info: (0, info[side] * 4 + lax.rem(info[5] + step, 4)),
        )

    return pl.pallas_call(
        cut_kernel,
        out_shape=[jax.ShapeDtypeStruct(shape, BF16)] * 7,
        grid_spec=pltpu.PrefetchScalarGridSpec(
            num_scalar_prefetch=1,
            grid=(1,),
            in_specs=[column(4, step) for step in range(4)]
            + [column(3, step) for step in range(1, 4)],
            out_specs=[pl.BlockSpec(shape, lambda i, info: (0, 0, 0))] * 7,
        ),
        compiler_params=params(VMEM_MOST, "arbitrary"),
        cost_estimate=cost(0, 4_000_000),
        name="cut",
    )(info, *([out_proj] * 7))


def stage_kernel(info_ref, first_ref, second_ref, out_ref, sems):
    rows, width = first_ref.shape
    columns = out_ref.shape[1]
    lines = rows // 9
    copies = []
    for index, ref in enumerate((first_ref, second_ref)):
        for piece in range(9):
            span = pl.ds(piece * lines, lines)
            place = pl.ds(index * rows + piece * lines, lines)
            if ref.shape[1] == columns:
                source = ref.at[span, :]
            else:
                start = pl.multiple_of(info_ref[3] * columns, LANES)
                source = ref.at[span, pl.ds(start, columns)]
            copies.append(
                pltpu.make_async_copy(source, out_ref.at[place, :], sems.at[index * 9 + piece])
            )
    for copy in copies:
        copy.start()
    for copy in copies:
        copy.wait()


def stage(info, first, second):
    anywhere = pl.BlockSpec(memory_space=pl.ANY)
    return pl.pallas_call(
        stage_kernel,
        out_shape=jax.ShapeDtypeStruct((2 * first.shape[0], second.shape[1]), BF16),
        in_specs=[pl.BlockSpec(memory_space=pltpu.SMEM), anywhere, anywhere],
        out_specs=WHOLE,
        scratch_shapes=[pltpu.SemaphoreType.DMA((18,))],
        compiler_params=params(VMEM_SOME),
        cost_estimate=cost(0, 2 * second.size * 2),
        name="stage",
    )(info, first, second)


def join_kernel(rows, info_ref, recv_ref, own_ref, *refs):
    firsts, theirs, sum_ref, out_ref = refs[:3], refs[3:7], refs[7], refs[8]
    sides = 2
    devs = recv_ref.shape[0] // sides
    tiles = LAT // LANES
    table = recv_ref[:, rows * tiles].astype(F32).reshape(sides, devs, SUB, LANES)
    lane = lax.broadcasted_iota(jnp.int32, (SUB, LANES), 1)

    def pick(first):
        chosen = (lane == first) | (lane == first + SUB)
        return jnp.sum(jnp.where(chosen, table, F32(0.0)), axis=3, keepdims=True)

    latents = []
    for row in range(rows):
        peaks = pick(row)
        totals = pick(2 * SUB + row)
        factor = jnp.exp(peaks - jnp.maximum(peaks[:1], peaks[1:]))
        factor = factor / (factor[:1] * totals[:1] + factor[1:] * totals[1:])
        parts = [
            recv_ref[:, row * tiles + number].astype(F32).reshape(sides, devs, SUB, LANES)
            for number in range(tiles)
        ]
        joined = [part[0] * factor[0] + part[1] * factor[1] for part in parts]
        latents.append(
            jnp.concatenate([part.reshape(devs * SUB, LANES) for part in joined], axis=1)
        )
    latent = jnp.concatenate(latents, axis=0).astype(BF16)
    maps = [own_ref[0]]
    maps += [ref[:tiles].reshape(LAT, LANES) for ref in firsts]
    maps += [ref[:tiles].reshape(LAT, LANES) for ref in theirs]
    products = jnp.dot(
        latent, jnp.concatenate(maps, axis=1), preferred_element_type=F32
    ).reshape(rows * devs, SUB, len(maps) * LANES)
    sub = lax.broadcasted_iota(jnp.int32, (1, SUB, LANES), 1)
    masked = []
    for piece in range(len(maps)):
        chip = lax.rem(info_ref[5] + 4 - piece % 4, 4)
        head = chip * 2 + info_ref[3 + piece // 4]
        part = products[:, :, piece * LANES : piece * LANES + LANES]
        masked.append(jnp.where(sub == head, part, F32(0.0)))
    masked = jnp.concatenate(masked, axis=2).reshape(rows * devs * SUB, len(maps) * LANES)
    out_ref[...] = jnp.dot(
        sum_ref[...], masked.astype(BF16), preferred_element_type=F32
    ).astype(BF16)


def join(info, received, value_up, firsts, theirs, rows):
    devs = received.shape[0] // 2
    count = rows * devs
    sums = np.repeat(np.eye(count, dtype=np.float32), SUB, axis=1)
    return pl.pallas_call(
        functools.partial(join_kernel, rows),
        out_shape=jax.ShapeDtypeStruct((count, SUB * LANES), BF16),
        in_specs=[pl.BlockSpec(memory_space=pltpu.SMEM)] + [WHOLE] * 10,
        out_specs=WHOLE,
        compiler_params=params(VMEM_SOME),
        cost_estimate=cost(480_000_000, 3_000_000),
        name="join",
    )(info, received, value_up, *firsts, *theirs, jnp.asarray(sums, BF16))


def project_kernel(info_ref, place_ref, *refs):
    values, own_ref = refs[:8], refs[8]
    seconds, theirs, out_ref = refs[9:12], refs[12:16], refs[16]
    del info_ref
    rows = []
    for source, ref in enumerate(values):
        data = ref[...]
        lanes = []
        for piece in range(8):
            step = (piece - source) % 4
            side = piece // 4 ^ source // 4
            start = (side * 4 + step) * LANES
            lanes.append(data[:, start : start + LANES])
        rows.append(jnp.concatenate(lanes, axis=1))
    left = jnp.concatenate(rows, axis=0)
    count = left.shape[0]
    order = lax.broadcasted_iota(jnp.int32, (count, count), 0) == place_ref[...]
    order = jnp.where(order, F32(1.0), F32(0.0)).astype(BF16)
    left = jnp.dot(order, left, preferred_element_type=F32).astype(BF16)
    columns = own_ref.shape[1] // LANES
    right = [own_ref[...]]
    for ref in seconds + theirs:
        first = ref.shape[0] - columns
        right.append(
            jnp.concatenate([ref[first + column] for column in range(columns)], axis=1)
        )
    right = jnp.concatenate(right, axis=0)
    total = jnp.dot(left, right, preferred_element_type=F32)
    out_ref[...] = total.reshape(out_ref.shape).astype(BF16)


def project(info, place, values, out_proj, seconds, theirs, chips):
    rows = sum(value.shape[0] for value in values)
    lanes = out_proj.shape[0]
    eighth = out_proj.shape[1] // 8
    full = lambda shape: pl.BlockSpec(shape, lambda i, info: (0,) * len(shape))
    own = pl.BlockSpec((lanes, eighth), lambda i, info: (0, info[0]))
    return pl.pallas_call(
        project_kernel,
        out_shape=jax.ShapeDtypeStruct((chips, rows // chips, eighth), BF16),
        grid_spec=pltpu.PrefetchScalarGridSpec(
            num_scalar_prefetch=1,
            grid=(1,),
            in_specs=[full(place.shape)]
            + [full(value.shape) for value in values]
            + [own]
            + [full(part.shape) for part in seconds + theirs],
            out_specs=full((chips, rows // chips, eighth)),
        ),
        compiler_params=params(VMEM_SOME, "arbitrary"),
        cost_estimate=cost(2 * rows * 8 * lanes * eighth, 3_500_000),
        name="project",
    )(info, place, *values, out_proj, *seconds, *theirs)


def residual_kernel(parts_ref, place_ref, gain_ref, *refs):
    blocks, residual_ref, out_ref = refs[:8], refs[8], refs[9]
    rows, width = residual_ref.shape
    stream = []
    for index, ref in enumerate(blocks):
        lines = ref[ref.shape[0] - 1].astype(F32)
        base = LANES // 2 * (index // 4)
        stream.append(
            jnp.concatenate(
                [
                    lines[base + SUB * column : base + SUB * column + SUB]
                    for column in range(width // LANES)
                ],
                axis=1,
            )
        )
    stream = jnp.concatenate(stream, axis=0).astype(BF16)
    order = lax.broadcasted_iota(jnp.int32, (rows, stream.shape[0]), 0) == place_ref[...]
    order = jnp.where(order, F32(1.0), F32(0.0)).astype(BF16)
    residual = jnp.dot(order, stream, preferred_element_type=F32)
    residual = residual + jnp.sum(parts_ref[...].astype(F32), axis=0)
    residual_ref[...] = residual
    squares = jnp.sum(residual * residual, axis=1, keepdims=True)
    high = rounded(squares)
    low = rounded(squares - high)
    lane = lax.broadcasted_iota(jnp.int32, (SUB, LANES), 1)
    table = jnp.zeros((SUB, LANES), F32)
    scaled = residual * gain_ref[...]
    groups = rows // SUB
    columns = width // LANES
    chips = out_ref.shape[0]
    for group in range(groups):
        span = slice(group * SUB, group * SUB + SUB)
        table = jnp.where(lane == group, high[span], table)
        table = jnp.where(lane == SUB + group, low[span], table)
    tiles = [
        scaled[group * SUB : group * SUB + SUB, column * LANES : column * LANES + LANES]
        for column in range(columns)
        for group in range(groups)
    ] + [table]
    for index, tile in enumerate(tiles):
        out_ref[:, index] = jnp.broadcast_to(tile.astype(BF16)[None], (chips, SUB, LANES))


def residual_rows(parts, place, gain, blocks, chips):
    _, rows, width = parts.shape
    tiles = rows * width // (SUB * LANES) + 1
    return pl.pallas_call(
        residual_kernel,
        out_shape=(
            jax.ShapeDtypeStruct((rows, width), F32),
            jax.ShapeDtypeStruct((chips, tiles, SUB, LANES), BF16),
        ),
        in_specs=[WHOLE] * 11,
        out_specs=(WHOLE, WHOLE),
        compiler_params=params(VMEM_SOME),
        cost_estimate=cost(2_000_000, 2_500_000),
        name="residual",
    )(parts, place, gain, *blocks)


def units_kernel(groups, last, info_ref, recv_ref, weight_ref, *refs):
    sides, quarters, tiles, _, _ = recv_ref.shape
    columns = (tiles - 1) // groups
    rows = sides * groups * SUB
    depth = columns * LANES
    which = 4 if last else 3
    lane = lax.broadcasted_iota(jnp.int32, (SUB, LANES), 1)
    total = squares = None
    for quarter in range(quarters):
        left = jnp.concatenate(
            [
                recv_ref[:, quarter, column * groups : column * groups + groups]
                .astype(F32)
                .reshape(rows, LANES)
                for column in range(columns)
            ],
            axis=1,
        ).astype(BF16)
        start = pl.multiple_of((info_ref[which] * quarters + quarter) * depth, LANES)
        part = lax.dot_general(
            left,
            weight_ref[:, pl.ds(start, depth)],
            (((1,), (1,)), ((), ())),
            preferred_element_type=F32,
        )
        total = part if total is None else total + part
        table = recv_ref[:, quarter, tiles - 1].astype(F32)
        pieces = [
            jnp.sum(
                jnp.where((lane == group) | (lane == SUB + group), table, F32(0.0)),
                axis=2,
                keepdims=True,
            )
            for group in range(groups)
        ]
        part = jnp.stack(pieces, axis=1).reshape(rows, 1)
        squares = part if squares is None else squares + part
    if not last:
        acc_ref, sq_ref = refs
        acc_ref[...] = total
        sq_ref[...] = jnp.broadcast_to(squares, (rows, LANES))
    else:
        acc_ref, sq_ref, out_ref = refs
        hidden = out_ref.shape[1]
        scale = lax.rsqrt((sq_ref[:, :1] + squares) / weight_ref.shape[1] + 1e-06)
        total = total + acc_ref[...]
        gate = total[:, :hidden] * scale
        upper = total[:, hidden:] * scale
        out_ref[...] = (gate / (1.0 + jnp.exp(-gate)) * upper).astype(BF16)


def units(info, received, weight, groups, carry=()):
    sides, quarters, tiles = received.shape[:3]
    hidden = weight.shape[0] // 2
    rows = sides * groups * SUB
    last = bool(carry)
    return pl.pallas_call(
        functools.partial(units_kernel, groups, last),
        out_shape=jax.ShapeDtypeStruct((rows, hidden), BF16)
        if last
        else [
            jax.ShapeDtypeStruct((rows, 2 * hidden), F32),
            jax.ShapeDtypeStruct((rows, LANES), F32),
        ],
        in_specs=[pl.BlockSpec(memory_space=pltpu.SMEM)] + [WHOLE] * (2 + len(carry)),
        out_specs=WHOLE if last else [WHOLE, WHOLE],
        compiler_params=params(VMEM_SOME),
        cost_estimate=cost(2 * rows * weight.size // 2, 5_000_000),
        name="units_last" if last else "units_first",
    )(info, received, weight, *carry)


def down_kernel(info_ref, mine_ref, theirs_ref, weight_ref, held_ref, out_ref, total):
    chips, steps = out_ref.shape[:2]
    rows = mine_ref.shape[0]
    count = rows // chips
    left = jnp.concatenate(
        [mine_ref[...].astype(F32), theirs_ref[...].astype(F32)], axis=1
    ).astype(BF16)
    width = 4 * LANES
    for step in range(steps):
        span = slice(step * width, step * width + width)
        total[:rows, span] = jnp.dot(
            left, weight_ref[:, span], preferred_element_type=F32
        )
    total[pl.ds(rows, SUB), :] = jnp.zeros((SUB, total.shape[1]), F32)
    lines, columns = held_ref.shape
    place = pl.ds(pl.multiple_of(info_ref[2] * lines, SUB), lines)
    across = pl.ds(pl.multiple_of(info_ref[5] * columns, LANES), columns)
    total[place, across] += held_ref[...]
    sub = lax.broadcasted_iota(jnp.int32, (SUB, LANES), 0)
    for chip in range(chips):
        for step in range(steps):
            span = slice(step * width, step * width + width)
            part = total[chip * count : chip * count + SUB, span]
            quads = [part[:, tile * LANES : tile * LANES + LANES] for tile in range(4)]
            packed = [
                jnp.where(
                    sub < count, quads[tile], pltpu.roll(quads[3], count - 2 * tile, 0)
                )
                for tile in range(3)
            ]
            out_ref[chip, step] = jnp.concatenate(packed, axis=0).astype(BF16)


def down(info, mine, theirs, weight, held, chips):
    rows = mine.shape[0]
    half = weight.shape[1]
    return pl.pallas_call(
        down_kernel,
        out_shape=jax.ShapeDtypeStruct((chips, half // (4 * LANES), 3 * SUB, LANES), BF16),
        in_specs=[pl.BlockSpec(memory_space=pltpu.SMEM)] + [WHOLE] * 4,
        out_specs=WHOLE,
        scratch_shapes=[pltpu.VMEM((rows + SUB, half), F32)],
        compiler_params=params(VMEM_SOME),
        cost_estimate=cost(2 * rows * weight.size, 6_000_000),
        name="down",
    )(info, mine, theirs, weight, held)


def finish_kernel(info_ref, parts_ref, mine_ref, theirs_ref):
    total = jnp.sum(parts_ref[...].astype(F32), axis=0)
    sub = lax.broadcasted_iota(jnp.int32, (SUB, LANES), 0)
    columns = []
    for step in range(total.shape[0]):
        quads = [total[step, tile * SUB : tile * SUB + SUB] for tile in range(3)]
        last = jnp.where(
            sub < 2,
            pltpu.roll(quads[0], 2, 0),
            jnp.where(sub < 4, pltpu.roll(quads[1], 4, 0), pltpu.roll(quads[2], 6, 0)),
        )
        columns += quads + [last]
    rows = jnp.concatenate(columns, axis=1)
    first, second = rows[0:3], rows[3:6]
    is_first = info_ref[3] == 0
    mine_ref[...] = jnp.where(is_first, first, second).astype(BF16)
    theirs_ref[...] = jnp.where(is_first, second, first).astype(BF16)


def finish(info, parts):
    shape = jax.ShapeDtypeStruct((3, parts.shape[1] * 4 * LANES), BF16)
    return pl.pallas_call(
        finish_kernel,
        out_shape=(shape, shape),
        in_specs=[pl.BlockSpec(memory_space=pltpu.SMEM), WHOLE],
        out_specs=(WHOLE, WHOLE),
        compiler_params=params(VMEM_SOME),
        cost_estimate=cost(1_000_000, 1_500_000),
        name="finish",
    )(info, parts)


def local(
    query_latent,
    latent_cache,
    lengths,
    stream,
    norm_gain,
    value_up,
    out_proj,
    gate_proj,
    up_proj,
    down_proj,
):
    core = lax.axis_index("core")
    ring = lax.axis_index("y")
    group = lax.axis_index("zl") * 4 + lax.axis_index("x")
    rows_own, width = stream.shape
    rows = query_latent.shape[0]
    half = width // 2
    eighth = width // 8
    first = core == 0
    info = jnp.stack([core * 4 + ring, core, group, core, 1 - core, ring]).astype(jnp.int32)

    own, *starts = early(info, value_up, stream)
    firsts = [shift(part, step) for step, part in zip((1, 2, 3), starts)]
    gain = block(norm_gain, core * 4 + ring, eighth, 0)[None]

    offset = lax.axis_index("zh") * latent_cache.shape[1]
    payload = attend(
        jnp.concatenate([lengths, offset[None].astype(jnp.int32)]),
        query_latent.transpose(0, 2, 1),
        latent_cache.transpose(0, 2, 1),
    )
    payload, out_proj, *firsts = lax.optimization_barrier((payload, out_proj, *firsts))
    firsts_theirs = [swap(part) for part in [own] + firsts]
    cuts = cut(info, out_proj)
    others = [cuts[0]] + [shift(part, step) for step, part in zip((1, 2, 3), cuts[1:4])]
    seconds = [shift(part, step) for step, part in zip((1, 2, 3), cuts[4:])]
    theirs = [swap(part) for part in others]
    received = lax.all_to_all(payload, OUTER, split_axis=0, concat_axis=0, tiled=True)
    values = join(info, received, value_up, firsts, firsts_theirs, rows)

    ring_values = [values] + [shift(values, step) for step in (1, 2, 3)]
    row = jnp.arange(8 * rows)
    natural = jnp.tile(row % 8 * (8 * rows) + row // 8, 8).reshape(8, 8 * rows)
    chip = (ring - jnp.arange(8)) % 4
    side = jnp.where(jnp.arange(8) < 4, core, 1 - core)
    place = natural[:, : 8 * rows] + ((chip * 2 + side) * rows)[:, None]
    place = place.reshape(1, 64 * rows).astype(jnp.int32)
    line = jnp.arange(SUB)[None]
    stream_place = ((chip * 2 + side) * rows_own)[:, None] + line
    stream_place = jnp.where(line < rows_own, stream_place, -1)
    stream_place = stream_place.reshape(1, 8 * SUB).astype(jnp.int32)
    partial = project(
        info,
        place,
        ring_values + [swap(piece) for piece in ring_values],
        out_proj,
        seconds,
        theirs,
        16,
    )
    parts = lax.all_to_all(partial, OUTER, split_axis=0, concat_axis=0, tiled=True)

    residual, payload = residual_rows(
        parts, stream_place, gain, [own] + firsts + firsts_theirs, 32
    )
    payload, gate_proj, up_proj, down_proj = lax.optimization_barrier(
        (payload, gate_proj, up_proj, down_proj)
    )
    piece = lax.all_to_all(payload, SIDE_CHIPS, split_axis=0, concat_axis=0, tiled=True)
    piece = piece.reshape((8, 4) + piece.shape[1:])
    other = swap(piece)
    down_theirs = swap(block(down_proj, 1 - core, half, 1))
    weight = stage(info, gate_proj.T, up_proj.T)
    groups = 8 * rows_own // SUB
    carry = units(info, piece, weight, groups)
    hidden = units(info, other, weight, groups, carry)
    partial = down(info, hidden, swap(hidden), stage(info, down_proj, down_theirs), residual, 32)
    parts = lax.all_to_all(partial, SIDE_CHIPS, split_axis=0, concat_axis=0, tiled=True)
    mine, theirs = finish(info, parts)
    theirs = swap(theirs)
    return jnp.concatenate(
        [jnp.where(first, mine, theirs), jnp.where(first, theirs, mine)], axis=1
    )


def solution(mesh):
    fine = Mesh(mesh.devices.reshape(2, 2, 4, 4, 2), AXES)
    placed = (
        P(DEV, None, None),
        P(DEV, "zh", None),
        P(DEV),
        P(AXES, None),
        P(),
        P(AXES, None, None),
        P(AXES, None),
        P(None, DEV),
        P(None, DEV),
        P(DEV, None),
    )
    return jax.shard_map(
        local, mesh=fine, in_specs=placed, out_specs=P(AXES, None), check_vma=False
    )
```

```python
import functools
import math

import jax
import jax.numpy as jnp
import numpy as np
from jax import lax
from jax.experimental import pallas as pl
from jax.experimental.pallas import tpu as pltpu
from jax.sharding import Mesh, PartitionSpec as P

LAT = 512
QKD = 192
LANES = 128
SUB = 8
AXES = ("zh", "zl", "x", "y", "core")
DEV = ("zl", "x", "y", "core")
OUTER = ("zh", "zl", "x")
SIDE_CHIPS = ("zl", "x", "y")
SWAP = [(0, 1), (1, 0)]
F32 = jnp.float32
BF16 = jnp.bfloat16
VMEM_MOST = 60 * 1024 * 1024


def swap(array):
    return lax.ppermute(array, "core", SWAP)


def shift(array, step):
    return lax.ppermute(array, "y", [(i, (i + step) % 4) for i in range(4)])


def block(array, index, size, axis):
    return lax.dynamic_slice_in_dim(array, index * size, size, axis)


ANYWHERE = pl.BlockSpec(memory_space=pl.ANY)


def full(shape):
    return pl.BlockSpec(shape, lambda i, *info: (0,) * len(shape))


def call(kernel, name, scalars, arrays, specs, outs, scratch=(), work=None):
    single = not isinstance(outs, list)
    shapes = [outs] if single else outs
    return pl.pallas_call(
        kernel,
        out_shape=outs,
        grid_spec=pltpu.PrefetchScalarGridSpec(
            num_scalar_prefetch=len(scalars),
            grid=(1,),
            in_specs=[full(a.shape) if s is None else s for a, s in zip(arrays, specs)],
            out_specs=full(outs.shape) if single else [full(o.shape) for o in outs],
            scratch_shapes=list(scratch),
        ),
        compiler_params=pltpu.CompilerParams(
            vmem_limit_bytes=VMEM_MOST, dimension_semantics=("arbitrary",)
        ),
        cost_estimate=pl.CostEstimate(
            flops=work or 0,
            bytes_accessed=2 * sum(math.prod(a.shape) for a in list(arrays) + shapes),
            transcendentals=0,
        ),
        name=name,
    )(*scalars, *arrays)


def rounded(value):
    return value.astype(BF16).astype(F32)


def attend_kernel(info_ref, lengths_ref, query_hbm, cache_hbm, out_ref, query_ref, cache_ref, sems):
    rows, _, heads = query_ref.shape
    keys = cache_ref.shape[2]
    pairs = rows // 2
    copies = [pltpu.make_async_copy(query_hbm, query_ref, sems.at[pairs])] + [
        pltpu.make_async_copy(
            cache_hbm.at[pl.ds(2 * pair, 2)], cache_ref.at[pl.ds(2 * pair, 2)], sems.at[pair]
        )
        for pair in range(pairs)
    ]
    for copy in copies:
        copy.start()
    copies[0].wait()
    tiles = [slice(start, start + LANES) for start in range(0, LAT, LANES)]
    position = lax.broadcasted_iota(jnp.int32, (1, keys), 1) + info_ref[6] * keys
    lane = lax.broadcasted_iota(jnp.int32, (heads, LANES), 1)
    table = jnp.zeros((heads, LANES), F32)
    for row in range(rows):
        if row % 2 == 0:
            copies[1 + row // 2].wait()
        cached = cache_ref[row]
        scores = lax.dot_general(
            query_ref[row], cached, (((0,), (0,)), ((), ())), preferred_element_type=F32
        ) * (1.0 / math.sqrt(QKD))
        usable = position < lengths_ref[row]
        scores = jnp.where(usable, scores, F32(-1e30))
        top = jnp.max(scores, axis=1, keepdims=True)
        top_high = rounded(top)
        top_low = rounded(top - top_high)
        exponent = jnp.where(usable, jnp.exp(scores - (top_high + top_low)), F32(0.0))
        total = jnp.sum(exponent, axis=1, keepdims=True)
        total_high = rounded(total)
        total_low = rounded(total - total_high)
        weighted = lax.dot_general(
            exponent.astype(BF16),
            cached[:LAT],
            (((1,), (1,)), ((), ())),
            preferred_element_type=F32,
        )
        for number, tile in enumerate(tiles):
            out_ref[:, row * len(tiles) + number] = (
                weighted[:, tile].reshape(heads // SUB, SUB, LANES).astype(BF16)
            )
        table = jnp.where(lane == row, top_high, table)
        table = jnp.where(lane == row + SUB, top_low, table)
        table = jnp.where(lane == row + 2 * SUB, total_high, table)
        table = jnp.where(lane == row + 3 * SUB, total_low, table)
    out_ref[:, rows * len(tiles)] = table.reshape(heads // SUB, SUB, LANES).astype(BF16)


def attend(info, lengths, query, cache):
    rows, depth, heads = query.shape
    keys = cache.shape[2]
    shape = (heads // SUB, rows * (LAT // LANES) + 1, SUB, LANES)
    return call(
        attend_kernel,
        "attend",
        [info, lengths],
        [query, cache],
        [ANYWHERE, ANYWHERE],
        jax.ShapeDtypeStruct(shape, BF16),
        [
            pltpu.VMEM(query.shape, BF16),
            pltpu.VMEM(cache.shape, BF16),
            pltpu.SemaphoreType.DMA((rows // 2 + 1,)),
        ],
        2 * rows * heads * keys * (depth + LAT),
    )


def early_kernel(info_ref, up_ref, stream_ref, half_ref, send_ref, *outs):
    send_ref[...] = half_ref[...]
    rows, width = stream_ref.shape
    eighth = width // 8
    ups = up_ref.shape[1] // LANES
    for step, out_ref in enumerate(outs):
        out_ref[:ups] = up_ref[0].reshape(ups, LANES, LANES)
        chip = lax.rem(info_ref[5] + step, 4)
        lines = []
        for side in (3, 4):
            start = pl.multiple_of((info_ref[side] * 4 + chip) * eighth, LANES)
            data = stream_ref[:, pl.ds(start, eighth)].astype(F32)
            for lane in range(0, eighth, LANES):
                lines.append(data[:, lane : lane + LANES])
                lines.append(jnp.zeros((SUB - rows, LANES), F32))
            lines.append(jnp.zeros((LANES // 2 - eighth // LANES * SUB, LANES), F32))
        out_ref[ups] = jnp.concatenate(lines, axis=0).astype(BF16)


def early(info, value_up, stream, out_proj):
    part = jax.ShapeDtypeStruct((value_up.shape[1] // LANES + 1, LANES, LANES), BF16)
    half = (out_proj.shape[0], out_proj.shape[1] // 2)
    return call(
        early_kernel,
        "early",
        [info],
        [value_up, stream, out_proj],
        [None, None, pl.BlockSpec(half, lambda i, info: (0, info[4]))],
        [jax.ShapeDtypeStruct(half, BF16)] + [part] * 4,
    )


def cut_kernel(info_ref, *refs):
    del info_ref
    steps = len(refs) // 3
    for step in range(steps):
        out_ref = refs[2 * steps + step]
        columns = out_ref.shape[0] // 2
        for side in range(2):
            for column in range(columns):
                span = slice(column * LANES, column * LANES + LANES)
                out_ref[side * columns + column] = refs[side * steps + step][:, span]


def cut(info, mine, theirs):
    rows, half = theirs.shape
    eighth = half // 4
    part = jax.ShapeDtypeStruct((2 * eighth // LANES, rows, LANES), BF16)

    def column(side, step):
        return pl.BlockSpec(
            (rows, eighth),
            lambda i, info: (0, info[side] * 4 + lax.rem(info[5] + step, 4)),
        )

    return call(
        cut_kernel,
        "cut",
        [info],
        [mine] * 3 + [theirs] * 3,
        [column(3, step) for step in (1, 2, 3)] + [column(7, step) for step in (1, 2, 3)],
        [part] * 3,
    )


def join_kernel(rows, info_ref, recv_ref, own_ref, *refs):
    firsts, theirs, sum_ref, out_ref = refs[:3], refs[3:7], refs[7], refs[8]
    sides = 2
    devs = recv_ref.shape[0] // sides
    tiles = LAT // LANES
    table = recv_ref[:, rows * tiles].astype(F32).reshape(sides, devs, SUB, LANES)
    lane = lax.broadcasted_iota(jnp.int32, (SUB, LANES), 1)

    def pick(first):
        chosen = (lane == first) | (lane == first + SUB)
        return jnp.sum(jnp.where(chosen, table, F32(0.0)), axis=3, keepdims=True)

    latents = []
    for row in range(rows):
        peaks = pick(row)
        totals = pick(2 * SUB + row)
        factor = jnp.exp(peaks - jnp.maximum(peaks[:1], peaks[1:]))
        factor = factor / (factor[:1] * totals[:1] + factor[1:] * totals[1:])
        parts = [
            recv_ref[:, row * tiles + number].astype(F32).reshape(sides, devs, SUB, LANES)
            for number in range(tiles)
        ]
        joined = [part[0] * factor[0] + part[1] * factor[1] for part in parts]
        latents.append(
            jnp.concatenate([part.reshape(devs * SUB, LANES) for part in joined], axis=1)
        )
    latent = jnp.concatenate(latents, axis=0).astype(BF16)
    maps = [own_ref[0]]
    maps += [ref[:tiles].reshape(LAT, LANES) for ref in firsts]
    maps += [ref[:tiles].reshape(LAT, LANES) for ref in theirs]
    products = jnp.dot(
        latent, jnp.concatenate(maps, axis=1), preferred_element_type=F32
    ).reshape(rows * devs, SUB, len(maps) * LANES)
    sub = lax.broadcasted_iota(jnp.int32, (1, SUB, LANES), 1)
    masked = []
    for piece in range(len(maps)):
        chip = lax.rem(info_ref[5] + 4 - piece % 4, 4)
        head = chip * 2 + info_ref[3 + piece // 4]
        part = products[:, :, piece * LANES : piece * LANES + LANES]
        masked.append(jnp.where(sub == head, part, F32(0.0)))
    masked = jnp.concatenate(masked, axis=2).reshape(rows * devs * SUB, len(maps) * LANES)
    out_ref[...] = jnp.dot(
        sum_ref[...], masked.astype(BF16), preferred_element_type=F32
    ).astype(BF16)


def join(info, received, value_up, firsts, theirs, rows):
    devs = received.shape[0] // 2
    count = rows * devs
    sums = np.repeat(np.eye(count, dtype=np.float32), SUB, axis=1)
    arrays = [received, value_up, *firsts, *theirs, jnp.asarray(sums, BF16)]
    return call(
        functools.partial(join_kernel, rows),
        "join",
        [info],
        arrays,
        [None] * len(arrays),
        jax.ShapeDtypeStruct((count, SUB * LANES), BF16),
        work=480_000_000,
    )


def project_kernel(info_ref, place_ref, *refs):
    values, own_ref, theirs_ref = refs[:8], refs[8], refs[9]
    parts, out_ref = refs[10:13], refs[13]
    del info_ref
    rows = []
    for source, ref in enumerate(values):
        data = ref[...]
        lanes = []
        for piece in range(8):
            step = (piece - source) % 4
            side = piece // 4 ^ source // 4
            start = (side * 4 + step) * LANES
            lanes.append(data[:, start : start + LANES])
        rows.append(jnp.concatenate(lanes, axis=1))
    left = jnp.concatenate(rows, axis=0)
    count = left.shape[0]
    order = lax.broadcasted_iota(jnp.int32, (count, count), 0) == place_ref[...]
    order = jnp.where(order, F32(1.0), F32(0.0)).astype(BF16)
    left = jnp.dot(order, left, preferred_element_type=F32).astype(BF16)
    columns = own_ref.shape[1] // LANES
    right = []
    for side, held_ref in enumerate((own_ref, theirs_ref)):
        right.append(held_ref[...])
        for ref in parts:
            tiles = [ref[side * columns + column] for column in range(columns)]
            right.append(jnp.concatenate(tiles, axis=1))
    right = jnp.concatenate(right, axis=0)
    total = jnp.dot(left, right, preferred_element_type=F32)
    out_ref[...] = total.reshape(out_ref.shape).astype(BF16)


def project(info, place, values, out_proj, out_theirs, parts, chips):
    rows = sum(value.shape[0] for value in values)
    lanes = out_proj.shape[0]
    eighth = out_proj.shape[1] // 8
    own = pl.BlockSpec((lanes, eighth), lambda i, info: (0, info[0]))
    other = pl.BlockSpec((lanes, eighth), lambda i, info: (0, info[5]))
    return call(
        project_kernel,
        "project",
        [info],
        [place, *values, out_proj, out_theirs, *parts],
        [None] * 9 + [own, other] + [None] * 3,
        jax.ShapeDtypeStruct((chips, rows // chips, eighth), BF16),
        work=2 * rows * 8 * lanes * eighth,
    )


def residual_kernel(parts_ref, place_ref, gain_ref, *refs):
    blocks, residual_ref, out_ref = refs[:8], refs[8], refs[9]
    rows, width = residual_ref.shape
    stream = []
    for index, ref in enumerate(blocks):
        lines = ref[ref.shape[0] - 1].astype(F32)
        base = LANES // 2 * (index // 4)
        stream.append(
            jnp.concatenate(
                [
                    lines[base + SUB * column : base + SUB * column + SUB]
                    for column in range(width // LANES)
                ],
                axis=1,
            )
        )
    stream = jnp.concatenate(stream, axis=0).astype(BF16)
    order = lax.broadcasted_iota(jnp.int32, (rows, stream.shape[0]), 0) == place_ref[...]
    order = jnp.where(order, F32(1.0), F32(0.0)).astype(BF16)
    residual = jnp.dot(order, stream, preferred_element_type=F32)
    residual = residual + jnp.sum(parts_ref[...].astype(F32), axis=0)
    residual_ref[...] = residual
    squares = jnp.sum(residual * residual, axis=1, keepdims=True)
    high = rounded(squares)
    low = rounded(squares - high)
    lane = lax.broadcasted_iota(jnp.int32, (SUB, LANES), 1)
    table = jnp.zeros((SUB, LANES), F32)
    scaled = residual * gain_ref[...]
    groups = rows // SUB
    columns = width // LANES
    chips = out_ref.shape[0]
    for group in range(groups):
        span = slice(group * SUB, group * SUB + SUB)
        table = jnp.where(lane == group, high[span], table)
        table = jnp.where(lane == SUB + group, low[span], table)
    tiles = [
        scaled[group * SUB : group * SUB + SUB, column * LANES : column * LANES + LANES]
        for column in range(columns)
        for group in range(groups)
    ] + [table]
    for index, tile in enumerate(tiles):
        out_ref[:, index] = jnp.broadcast_to(tile.astype(BF16)[None], (chips, SUB, LANES))


def residual_rows(parts, place, gain, blocks, chips):
    _, rows, width = parts.shape
    tiles = rows * width // (SUB * LANES) + 1
    last = blocks[0].shape[0] - 1
    line = pl.BlockSpec((1, LANES, LANES), lambda i: (last, 0, 0))
    return call(
        residual_kernel,
        "residual",
        [],
        [parts, place, gain, *blocks],
        [None] * 3 + [line] * 8,
        [
            jax.ShapeDtypeStruct((rows, width), F32),
            jax.ShapeDtypeStruct((chips, tiles, SUB, LANES), BF16),
        ],
    )


def units_kernel(groups, last, info_ref, recv_ref, gate_hbm, up_hbm, *refs):
    weight_ref, sems = refs[-2:]
    refs = refs[:-2]
    sides, quarters, tiles, _, _ = recv_ref.shape
    columns = (tiles - 1) // groups
    rows = sides * groups * SUB
    depth = columns * LANES
    which = 4 if last else 3
    hidden = gate_hbm.shape[0]
    copies = []
    for quarter in range(quarters):
        start = pl.multiple_of((info_ref[which] * quarters + quarter) * depth, LANES)
        for index, ref in enumerate((gate_hbm, up_hbm)):
            target = weight_ref.at[
                pl.ds(index * hidden, hidden), pl.ds(quarter * depth, depth)
            ]
            copies.append(
                pltpu.make_async_copy(
                    ref.at[:, pl.ds(start, depth)], target, sems.at[2 * quarter + index]
                )
            )
    for copy in copies:
        copy.start()
    lane = lax.broadcasted_iota(jnp.int32, (SUB, LANES), 1)
    total = squares = None
    for quarter in range(quarters):
        left = jnp.concatenate(
            [
                recv_ref[:, quarter, column * groups : column * groups + groups]
                .astype(F32)
                .reshape(rows, LANES)
                for column in range(columns)
            ],
            axis=1,
        ).astype(BF16)
        copies[2 * quarter].wait()
        copies[2 * quarter + 1].wait()
        part = lax.dot_general(
            left,
            weight_ref[:, quarter * depth : quarter * depth + depth],
            (((1,), (1,)), ((), ())),
            preferred_element_type=F32,
        )
        total = part if total is None else total + part
        table = recv_ref[:, quarter, tiles - 1].astype(F32)
        pieces = [
            jnp.sum(
                jnp.where((lane == group) | (lane == SUB + group), table, F32(0.0)),
                axis=2,
                keepdims=True,
            )
            for group in range(groups)
        ]
        part = jnp.stack(pieces, axis=1).reshape(rows, 1)
        squares = part if squares is None else squares + part
    if not last:
        acc_ref, sq_ref = refs
        acc_ref[...] = total
        sq_ref[...] = jnp.broadcast_to(squares, (rows, LANES))
    else:
        acc_ref, sq_ref, out_ref = refs
        scale = lax.rsqrt((sq_ref[:, :1] + squares) / gate_hbm.shape[1] + 1e-06)
        total = total + acc_ref[...]
        gate = total[:, :hidden] * scale
        upper = total[:, hidden:] * scale
        out_ref[...] = (gate / (1.0 + jnp.exp(-gate)) * upper).astype(BF16)


def units(info, received, gate, up, groups, carry=()):
    sides, quarters, tiles = received.shape[:3]
    hidden, width = gate.shape
    rows = sides * groups * SUB
    last = bool(carry)
    return call(
        functools.partial(units_kernel, groups, last),
        "units_last" if last else "units_first",
        [info],
        [received, gate, up, *carry],
        [None, ANYWHERE, ANYWHERE] + [None] * len(carry),
        jax.ShapeDtypeStruct((rows, hidden), BF16)
        if last
        else [
            jax.ShapeDtypeStruct((rows, 2 * hidden), F32),
            jax.ShapeDtypeStruct((rows, LANES), F32),
        ],
        [
            pltpu.VMEM((2 * hidden, width // 2), BF16),
            pltpu.SemaphoreType.DMA((2 * quarters,)),
        ],
        2 * rows * hidden * width,
    )


def down_kernel(
    info_ref, mine_ref, theirs_ref, own_hbm, other_hbm, held_ref, out_ref, total, weight_ref, sems
):
    chips, steps = out_ref.shape[:2]
    rows = mine_ref.shape[0]
    count = rows // chips
    hidden, half = other_hbm.shape
    width = 4 * LANES
    copies = []
    for piece in range(0, half, width):
        for index, ref in enumerate((own_hbm, other_hbm)):
            start = info_ref[3] * half + piece if index == 0 else piece
            copies.append(
                pltpu.make_async_copy(
                    ref.at[:, pl.ds(pl.multiple_of(start, LANES), width)],
                    weight_ref.at[pl.ds(index * hidden, hidden), pl.ds(piece, width)],
                    sems.at[len(copies)],
                )
            )
    for copy in copies:
        copy.start()
    left = jnp.concatenate(
        [mine_ref[...].astype(F32), theirs_ref[...].astype(F32)], axis=1
    ).astype(BF16)
    for step in range(steps):
        span = slice(step * width, step * width + width)
        copies[2 * step].wait()
        copies[2 * step + 1].wait()
        total[:rows, span] = jnp.dot(
            left, weight_ref[:, span], preferred_element_type=F32
        )
    total[pl.ds(rows, SUB), :] = jnp.zeros((SUB, total.shape[1]), F32)
    lines, columns = held_ref.shape
    place = pl.ds(pl.multiple_of(info_ref[2] * lines, SUB), lines)
    across = pl.ds(pl.multiple_of(info_ref[5] * columns, LANES), columns)
    total[place, across] += held_ref[...]
    sub = lax.broadcasted_iota(jnp.int32, (SUB, LANES), 0)
    for chip in range(chips):
        for step in range(steps):
            span = slice(step * width, step * width + width)
            part = total[chip * count : chip * count + SUB, span]
            quads = [part[:, tile * LANES : tile * LANES + LANES] for tile in range(4)]
            packed = [
                jnp.where(
                    sub < count, quads[tile], pltpu.roll(quads[3], count - 2 * tile, 0)
                )
                for tile in range(3)
            ]
            out_ref[chip, step] = jnp.concatenate(packed, axis=0).astype(BF16)


def down(info, mine, theirs, down_proj, other, held, chips):
    rows = mine.shape[0]
    hidden, half = other.shape
    steps = half // (4 * LANES)
    return call(
        down_kernel,
        "down",
        [info],
        [mine, theirs, down_proj, other, held],
        [None, None, ANYWHERE, ANYWHERE, None],
        jax.ShapeDtypeStruct((chips, steps, 3 * SUB, LANES), BF16),
        [
            pltpu.VMEM((rows + SUB, half), F32),
            pltpu.VMEM((2 * hidden, half), BF16),
            pltpu.SemaphoreType.DMA((2 * steps,)),
        ],
        4 * rows * hidden * half,
    )


def finish_kernel(info_ref, parts_ref, mine_ref, theirs_ref):
    total = jnp.sum(parts_ref[...].astype(F32), axis=0)
    sub = lax.broadcasted_iota(jnp.int32, (SUB, LANES), 0)
    columns = []
    for step in range(total.shape[0]):
        quads = [total[step, tile * SUB : tile * SUB + SUB] for tile in range(3)]
        last = jnp.where(
            sub < 2,
            pltpu.roll(quads[0], 2, 0),
            jnp.where(sub < 4, pltpu.roll(quads[1], 4, 0), pltpu.roll(quads[2], 6, 0)),
        )
        columns += quads + [last]
    rows = jnp.concatenate(columns, axis=1)
    first, second = rows[0:3], rows[3:6]
    is_first = info_ref[3] == 0
    mine_ref[...] = jnp.where(is_first, first, second).astype(BF16)
    theirs_ref[...] = jnp.where(is_first, second, first).astype(BF16)


def finish(info, parts):
    shape = jax.ShapeDtypeStruct((3, parts.shape[1] * 4 * LANES), BF16)
    return call(finish_kernel, "finish", [info], [parts], [None], [shape, shape])


def local(
    query_latent,
    latent_cache,
    lengths,
    stream,
    norm_gain,
    value_up,
    out_proj,
    gate_proj,
    up_proj,
    down_proj,
):
    core = lax.axis_index("core")
    ring = lax.axis_index("y")
    group = lax.axis_index("zl") * 4 + lax.axis_index("x")
    rows_own, width = stream.shape
    rows = query_latent.shape[0]
    half = width // 2
    eighth = width // 8
    first = core == 0
    info = [core * 4 + ring, core, group, core, 1 - core, ring, lax.axis_index("zh"), 0]
    info = jnp.stack(info).astype(jnp.int32)

    out_send, own, *starts = early(info, value_up, stream, out_proj)
    out_theirs = swap(out_send)
    firsts = [shift(part, step) for step, part in zip((1, 2, 3), starts)]
    gain = block(norm_gain, core * 4 + ring, eighth, 0)[None]

    payload = attend(
        info, lengths, query_latent.transpose(0, 2, 1), latent_cache.transpose(0, 2, 1)
    )
    payload, out_theirs, *firsts = lax.optimization_barrier((payload, out_theirs, *firsts))
    firsts_theirs = [swap(part) for part in [own] + firsts]
    parts = [
        shift(part, step) for step, part in zip((1, 2, 3), cut(info, out_proj, out_theirs))
    ]
    received = lax.all_to_all(payload, OUTER, split_axis=0, concat_axis=0, tiled=True)
    values = join(info, received, value_up, firsts, firsts_theirs, rows)

    ring_values = [values] + [shift(values, step) for step in (1, 2, 3)]
    row = jnp.arange(8 * rows)
    natural = jnp.tile(row % 8 * (8 * rows) + row // 8, 8).reshape(8, 8 * rows)
    chip = (ring - jnp.arange(8)) % 4
    side = jnp.where(jnp.arange(8) < 4, core, 1 - core)
    place = natural[:, : 8 * rows] + ((chip * 2 + side) * rows)[:, None]
    place = place.reshape(1, 64 * rows).astype(jnp.int32)
    line = jnp.arange(SUB)[None]
    stream_place = ((chip * 2 + side) * rows_own)[:, None] + line
    stream_place = jnp.where(line < rows_own, stream_place, -1)
    stream_place = stream_place.reshape(1, 8 * SUB).astype(jnp.int32)
    partial = project(
        info,
        place,
        ring_values + [swap(piece) for piece in ring_values],
        out_proj,
        out_theirs,
        parts,
        16,
    )
    parts = lax.all_to_all(partial, OUTER, split_axis=0, concat_axis=0, tiled=True)

    residual, payload = residual_rows(
        parts, stream_place, gain, [own] + firsts + firsts_theirs, 32
    )
    payload, gate_proj, up_proj, down_proj = lax.optimization_barrier(
        (payload, gate_proj, up_proj, down_proj)
    )
    piece = lax.all_to_all(payload, SIDE_CHIPS, split_axis=0, concat_axis=0, tiled=True)
    piece = piece.reshape((8, 4) + piece.shape[1:])
    other = swap(piece)
    down_theirs = swap(block(down_proj, 1 - core, half, 1))
    gate_proj, up_proj = gate_proj.T, up_proj.T
    groups = 8 * rows_own // SUB
    carry = units(info, piece, gate_proj, up_proj, groups)
    hidden = units(info, other, gate_proj, up_proj, groups, carry)
    partial = down(info, hidden, swap(hidden), down_proj, down_theirs, residual, 32)
    parts = lax.all_to_all(partial, SIDE_CHIPS, split_axis=0, concat_axis=0, tiled=True)
    mine, theirs = finish(info, parts)
    theirs = swap(theirs)
    return jnp.concatenate(
        [jnp.where(first, mine, theirs), jnp.where(first, theirs, mine)], axis=1
    )


def solution(mesh):
    fine = Mesh(mesh.devices.reshape(2, 2, 4, 4, 2), AXES)
    placed = (
        P(DEV, None, None),
        P(DEV, "zh", None),
        P(DEV),
        P(AXES, None),
        P(),
        P(AXES, None, None),
        P(AXES, None),
        P(None, DEV),
        P(None, DEV),
        P(DEV, None),
    )
    return jax.shard_map(
        local, mesh=fine, in_specs=placed, out_specs=P(AXES, None), check_vma=False
    )
```

```python
import functools
import math

import jax
import jax.numpy as jnp
import numpy as np
from jax import lax
from jax.experimental import pallas as pl
from jax.experimental.pallas import tpu as pltpu
from jax.sharding import Mesh, PartitionSpec as P

LAT = 512
QKD = 192
LANES = 128
SUB = 8
AXES = ("zh", "zl", "x", "y", "core")
DEV = ("zl", "x", "y", "core")
OUTER = ("zh", "zl", "x")
SIDE_CHIPS = ("zl", "x", "y")
SWAP = [(0, 1), (1, 0)]
F32 = jnp.float32
BF16 = jnp.bfloat16
VMEM_MOST = 60 * 1024 * 1024
VMEM_STAGE = 44 * 1024 * 1024
VMEM_SOME = 24 * 1024 * 1024


def swap(array):
    return lax.ppermute(array, "core", SWAP)


def shift(array, step):
    return lax.ppermute(array, "y", [(i, (i + step) % 4) for i in range(4)])


def block(array, index, size, axis):
    return lax.dynamic_slice_in_dim(array, index * size, size, axis)


WHOLE = pl.BlockSpec(memory_space=pltpu.VMEM)
ANYWHERE = pl.BlockSpec(memory_space=pl.ANY)


def full(shape):
    return pl.BlockSpec(shape, lambda i, *info: (0,) * len(shape))


def call(kernel, name, scalars, arrays, specs, outs, scratch=(), work=None, limit=VMEM_SOME, out_specs=None):
    single = not isinstance(outs, list)
    shapes = [outs] if single else outs
    return pl.pallas_call(
        kernel,
        out_shape=outs,
        grid_spec=pltpu.PrefetchScalarGridSpec(
            num_scalar_prefetch=len(scalars),
            grid=(1,),
            in_specs=[full(a.shape) if s is None else s for a, s in zip(arrays, specs)],
            out_specs=out_specs
            or (full(outs.shape) if single else [full(o.shape) for o in outs]),
            scratch_shapes=list(scratch),
        ),
        compiler_params=pltpu.CompilerParams(
            vmem_limit_bytes=limit, dimension_semantics=("arbitrary",)
        ),
        cost_estimate=pl.CostEstimate(
            flops=work or 0,
            bytes_accessed=2 * sum(math.prod(a.shape) for a in list(arrays) + shapes),
            transcendentals=0,
        ),
        name=name,
    )(*scalars, *arrays)


def rounded(value):
    return value.astype(BF16).astype(F32)


def attend_kernel(
    info_ref, lengths_ref, query_hbm, cache_hbm, out_proj_hbm, theirs_hbm, out_ref, *refs
):
    cuts, (query_ref, cache_ref, weight_ref, sems) = refs[:3], refs[3:]
    half = theirs_hbm.shape[1]
    mine = out_proj_hbm.at[:, pl.ds(pl.multiple_of(info_ref[3] * half, LANES), half)]
    rows, _, heads = query_ref.shape
    keys = cache_ref.shape[2]
    pairs = rows // 2
    copies = [pltpu.make_async_copy(query_hbm, query_ref, sems.at[pairs])] + [
        pltpu.make_async_copy(
            cache_hbm.at[pl.ds(2 * pair, 2)], cache_ref.at[pl.ds(2 * pair, 2)], sems.at[pair]
        )
        for pair in range(pairs)
    ]
    for side, ref in enumerate((mine, theirs_hbm)):
        copies.append(
            pltpu.make_async_copy(ref, weight_ref.at[side], sems.at[pairs + 1 + side])
        )
    for copy in copies:
        copy.start()
    copies[0].wait()
    tiles = [slice(start, start + LANES) for start in range(0, LAT, LANES)]
    position = lax.broadcasted_iota(jnp.int32, (1, keys), 1) + info_ref[6] * keys
    lane = lax.broadcasted_iota(jnp.int32, (heads, LANES), 1)
    table = jnp.zeros((heads, LANES), F32)
    for row in range(rows):
        if row % 2 == 0:
            copies[1 + row // 2].wait()
        cached = cache_ref[row]
        scores = lax.dot_general(
            query_ref[row], cached, (((0,), (0,)), ((), ())), preferred_element_type=F32
        ) * (1.0 / math.sqrt(QKD))
        usable = position < lengths_ref[row]
        scores = jnp.where(usable, scores, F32(-1e30))
        top = jnp.max(scores, axis=1, keepdims=True)
        top_high = rounded(top)
        top_low = rounded(top - top_high)
        exponent = jnp.where(usable, jnp.exp(scores - (top_high + top_low)), F32(0.0))
        total = jnp.sum(exponent, axis=1, keepdims=True)
        total_high = rounded(total)
        total_low = rounded(total - total_high)
        weighted = lax.dot_general(
            exponent.astype(BF16),
            cached[:LAT],
            (((1,), (1,)), ((), ())),
            preferred_element_type=F32,
        )
        for number, tile in enumerate(tiles):
            out_ref[:, row * len(tiles) + number] = (
                weighted[:, tile].reshape(heads // SUB, SUB, LANES).astype(BF16)
            )
        table = jnp.where(lane == row, top_high, table)
        table = jnp.where(lane == row + SUB, top_low, table)
        table = jnp.where(lane == row + 2 * SUB, total_high, table)
        table = jnp.where(lane == row + 3 * SUB, total_low, table)
    out_ref[:, rows * len(tiles)] = table.reshape(heads // SUB, SUB, LANES).astype(BF16)
    copies[-2].wait()
    copies[-1].wait()
    for step, cut_ref in enumerate(cuts):
        columns = cut_ref.shape[0] // 2
        first = lax.rem(info_ref[5] + step + 1, 4) * columns
        for side in range(2):
            for column in range(columns):
                start = pl.multiple_of((first + column) * LANES, LANES)
                cut_ref[side * columns + column] = weight_ref[side, :, pl.ds(start, LANES)]


def attend(info, lengths, query, cache, out_proj, theirs):
    rows, depth, heads = query.shape
    keys = cache.shape[2]
    shape = (heads // SUB, rows * (LAT // LANES) + 1, SUB, LANES)
    columns = out_proj.shape[1] // 8 // LANES
    return call(
        attend_kernel,
        "attend",
        [info, lengths],
        [query, cache, out_proj, theirs],
        [ANYWHERE] * 4,
        [jax.ShapeDtypeStruct(shape, BF16)]
        + [jax.ShapeDtypeStruct((2 * columns, LANES, LANES), BF16)] * 3,
        [
            pltpu.VMEM(query.shape, BF16),
            pltpu.VMEM(cache.shape, BF16),
            pltpu.VMEM((2,) + theirs.shape, BF16),
            pltpu.SemaphoreType.DMA((rows // 2 + 3,)),
        ],
        2 * rows * heads * keys * (depth + LAT),
        VMEM_MOST,
    )


def early_kernel(info_ref, up_ref, stream_ref, half_ref, send_ref, *outs):
    send_ref[...] = half_ref[...]
    rows, width = stream_ref.shape
    eighth = width // 8
    ups = up_ref.shape[1] // LANES
    for step, out_ref in enumerate(outs):
        out_ref[:ups] = up_ref[0].reshape(ups, LANES, LANES)
        chip = lax.rem(info_ref[5] + step, 4)
        lines = []
        for side in (3, 4):
            start = pl.multiple_of((info_ref[side] * 4 + chip) * eighth, LANES)
            data = stream_ref[:, pl.ds(start, eighth)].astype(F32)
            for lane in range(0, eighth, LANES):
                lines.append(data[:, lane : lane + LANES])
                lines.append(jnp.zeros((SUB - rows, LANES), F32))
            lines.append(jnp.zeros((LANES // 2 - eighth // LANES * SUB, LANES), F32))
        out_ref[ups] = jnp.concatenate(lines, axis=0).astype(BF16)


def early(info, value_up, stream, out_proj):
    part = jax.ShapeDtypeStruct((value_up.shape[1] // LANES + 1, LANES, LANES), BF16)
    half = (out_proj.shape[0], out_proj.shape[1] // 2)
    return call(
        early_kernel,
        "early",
        [info],
        [value_up, stream, out_proj],
        [None, None, pl.BlockSpec(half, lambda i, info: (0, info[4]))],
        [jax.ShapeDtypeStruct(half, BF16)] + [part] * 4,
        limit=VMEM_MOST,
    )


def stage_kernel(info_ref, gate_ref, up_ref, down_ref, out_ref, own_ref, send_ref, sems):
    rows = gate_ref.shape[0]
    half = own_ref.shape[1]
    sides = [
        down_ref.at[:, pl.ds(pl.multiple_of(info_ref[side] * half, LANES), half)]
        for side in (4, 3)
    ]
    copies = [
        pltpu.make_async_copy(source, target, sems.at[index])
        for index, (source, target) in enumerate(
            [
                (sides[0], send_ref),
                (gate_ref, out_ref.at[pl.ds(0, rows), :]),
                (up_ref, out_ref.at[pl.ds(rows, rows), :]),
                (sides[1], own_ref),
            ]
        )
    ]
    for copy in copies:
        copy.start()
    for copy in copies:
        copy.wait()


def stage(info, gate, up, down_proj):
    rows, width = gate.shape
    half = jax.ShapeDtypeStruct((down_proj.shape[0], down_proj.shape[1] // 2), BF16)
    return call(
        stage_kernel,
        "stage",
        [info],
        [gate, up, down_proj],
        [ANYWHERE] * 3,
        [jax.ShapeDtypeStruct((2 * rows, width), BF16), half, half],
        [pltpu.SemaphoreType.DMA((4,))],
        limit=VMEM_STAGE,
        out_specs=[WHOLE] * 3,
    )


def join_kernel(rows, info_ref, recv_ref, own_ref, place_ref, *refs):
    blocks, sum_ref, out_ref, stream_ref = refs[:8], refs[8], refs[9], refs[10]
    stream = []
    for index, ref in enumerate(blocks):
        lines = ref[ref.shape[0] - 1].astype(F32)
        base = LANES // 2 * (index // 4)
        spans = range(base, base + stream_ref.shape[1] // LANES * SUB, SUB)
        stream.append(jnp.concatenate([lines[span : span + SUB] for span in spans], axis=1))
    stream = jnp.concatenate(stream, axis=0).astype(BF16)
    shape = (stream_ref.shape[0], stream.shape[0])
    order = lax.broadcasted_iota(jnp.int32, shape, 0) == place_ref[...]
    order = jnp.where(order, F32(1.0), F32(0.0)).astype(BF16)
    stream_ref[...] = jnp.dot(order, stream, preferred_element_type=F32)
    sides = 2
    devs = recv_ref.shape[0] // sides
    tiles = LAT // LANES
    table = recv_ref[:, rows * tiles].astype(F32).reshape(sides, devs, SUB, LANES)
    lane = lax.broadcasted_iota(jnp.int32, (SUB, LANES), 1)

    def pick(first):
        chosen = (lane == first) | (lane == first + SUB)
        return jnp.sum(jnp.where(chosen, table, F32(0.0)), axis=3, keepdims=True)

    latents = []
    for row in range(rows):
        peaks = pick(row)
        totals = pick(2 * SUB + row)
        factor = jnp.exp(peaks - jnp.maximum(peaks[:1], peaks[1:]))
        factor = factor / (factor[:1] * totals[:1] + factor[1:] * totals[1:])
        parts = [
            recv_ref[:, row * tiles + number].astype(F32).reshape(sides, devs, SUB, LANES)
            for number in range(tiles)
        ]
        joined = [part[0] * factor[0] + part[1] * factor[1] for part in parts]
        latents.append(
            jnp.concatenate([part.reshape(devs * SUB, LANES) for part in joined], axis=1)
        )
    latent = jnp.concatenate(latents, axis=0).astype(BF16)
    maps = [own_ref[0]]
    maps += [ref[:tiles].reshape(LAT, LANES) for ref in blocks[1:]]
    products = jnp.dot(
        latent, jnp.concatenate(maps, axis=1), preferred_element_type=F32
    ).reshape(rows * devs, SUB, len(maps) * LANES)
    sub = lax.broadcasted_iota(jnp.int32, (1, SUB, LANES), 1)
    masked = []
    for piece in range(len(maps)):
        chip = lax.rem(info_ref[5] + 4 - piece % 4, 4)
        head = chip * 2 + info_ref[3 + piece // 4]
        part = products[:, :, piece * LANES : piece * LANES + LANES]
        masked.append(jnp.where(sub == head, part, F32(0.0)))
    masked = jnp.concatenate(masked, axis=2).reshape(rows * devs * SUB, len(maps) * LANES)
    out_ref[...] = jnp.dot(
        sum_ref[...], masked.astype(BF16), preferred_element_type=F32
    ).astype(BF16)


def join(info, received, value_up, place, blocks, rows, eighth):
    devs = received.shape[0] // 2
    count = rows * devs
    sums = np.repeat(np.eye(count, dtype=np.float32), SUB, axis=1)
    arrays = [received, value_up, place, *blocks, jnp.asarray(sums, BF16)]
    return call(
        functools.partial(join_kernel, rows),
        "join",
        [info],
        arrays,
        [None] * len(arrays),
        [
            jax.ShapeDtypeStruct((count, SUB * LANES), BF16),
            jax.ShapeDtypeStruct((4 * rows, eighth), F32),
        ],
        work=480_000_000,
        limit=VMEM_MOST,
    )


def project_kernel(info_ref, place_ref, *refs):
    values, own_ref, theirs_ref = refs[:8], refs[8], refs[9]
    parts, out_ref = refs[10:13], refs[13]
    del info_ref
    rows = []
    for source, ref in enumerate(values):
        data = ref[...]
        lanes = []
        for piece in range(8):
            step = (piece - source) % 4
            side = piece // 4 ^ source // 4
            start = (side * 4 + step) * LANES
            lanes.append(data[:, start : start + LANES])
        rows.append(jnp.concatenate(lanes, axis=1))
    left = jnp.concatenate(rows, axis=0)
    count = left.shape[0]
    order = lax.broadcasted_iota(jnp.int32, (count, count), 0) == place_ref[...]
    order = jnp.where(order, F32(1.0), F32(0.0)).astype(BF16)
    left = jnp.dot(order, left, preferred_element_type=F32).astype(BF16)
    columns = own_ref.shape[1] // LANES
    right = []
    for side, held_ref in enumerate((own_ref, theirs_ref)):
        right.append(held_ref[...])
        for ref in parts:
            tiles = [ref[side * columns + column] for column in range(columns)]
            right.append(jnp.concatenate(tiles, axis=1))
    right = jnp.concatenate(right, axis=0)
    total = jnp.dot(left, right, preferred_element_type=F32)
    out_ref[...] = total.reshape(out_ref.shape).astype(BF16)


def project(info, place, values, out_proj, out_theirs, parts, chips):
    rows = sum(value.shape[0] for value in values)
    lanes = out_proj.shape[0]
    eighth = out_proj.shape[1] // 8
    own = pl.BlockSpec((lanes, eighth), lambda i, info: (0, info[0]))
    other = pl.BlockSpec((lanes, eighth), lambda i, info: (0, info[5]))
    return call(
        project_kernel,
        "project",
        [info],
        [place, *values, out_proj, out_theirs, *parts],
        [None] * 9 + [own, other] + [None] * 3,
        jax.ShapeDtypeStruct((chips, rows // chips, eighth), BF16),
        work=2 * rows * 8 * lanes * eighth,
    )


def residual_kernel(parts_ref, stream_ref, gain_ref, residual_ref, out_ref):
    rows, width = residual_ref.shape
    residual = stream_ref[...] + jnp.sum(parts_ref[...].astype(F32), axis=0)
    residual_ref[...] = residual
    squares = jnp.sum(residual * residual, axis=1, keepdims=True)
    high = rounded(squares)
    low = rounded(squares - high)
    lane = lax.broadcasted_iota(jnp.int32, (SUB, LANES), 1)
    table = jnp.zeros((SUB, LANES), F32)
    scaled = residual * gain_ref[...]
    groups = rows // SUB
    columns = width // LANES
    chips = out_ref.shape[0]
    for group in range(groups):
        span = slice(group * SUB, group * SUB + SUB)
        table = jnp.where(lane == group, high[span], table)
        table = jnp.where(lane == SUB + group, low[span], table)
    tiles = [
        scaled[group * SUB : group * SUB + SUB, column * LANES : column * LANES + LANES]
        for column in range(columns)
        for group in range(groups)
    ] + [table]
    for index, tile in enumerate(tiles):
        out_ref[:, index] = jnp.broadcast_to(tile.astype(BF16)[None], (chips, SUB, LANES))


def residual_rows(parts, stream, gain, chips):
    _, rows, width = parts.shape
    tiles = rows * width // (SUB * LANES) + 1
    return call(
        residual_kernel,
        "residual",
        [],
        [parts, stream, gain],
        [None] * 3,
        [
            jax.ShapeDtypeStruct((rows, width), F32),
            jax.ShapeDtypeStruct((chips, tiles, SUB, LANES), BF16),
        ],
    )


def units_kernel(groups, last, info_ref, recv_ref, weight_ref, *refs):
    sides, quarters, tiles, _, _ = recv_ref.shape
    columns = (tiles - 1) // groups
    rows = sides * groups * SUB
    depth = columns * LANES
    which = 4 if last else 3
    lane = lax.broadcasted_iota(jnp.int32, (SUB, LANES), 1)
    total = squares = None
    for quarter in range(quarters):
        left = jnp.concatenate(
            [
                recv_ref[:, quarter, column * groups : column * groups + groups]
                .astype(F32)
                .reshape(rows, LANES)
                for column in range(columns)
            ],
            axis=1,
        ).astype(BF16)
        start = pl.multiple_of((info_ref[which] * quarters + quarter) * depth, LANES)
        part = lax.dot_general(
            left,
            weight_ref[:, pl.ds(start, depth)],
            (((1,), (1,)), ((), ())),
            preferred_element_type=F32,
        )
        total = part if total is None else total + part
        table = recv_ref[:, quarter, tiles - 1].astype(F32)
        pieces = [
            jnp.sum(
                jnp.where((lane == group) | (lane == SUB + group), table, F32(0.0)),
                axis=2,
                keepdims=True,
            )
            for group in range(groups)
        ]
        part = jnp.stack(pieces, axis=1).reshape(rows, 1)
        squares = part if squares is None else squares + part
    if not last:
        acc_ref, sq_ref = refs
        acc_ref[...] = total
        sq_ref[...] = jnp.broadcast_to(squares, (rows, LANES))
    else:
        acc_ref, sq_ref, out_ref = refs
        hidden = out_ref.shape[1]
        scale = lax.rsqrt((sq_ref[:, :1] + squares) / weight_ref.shape[1] + 1e-06)
        total = total + acc_ref[...]
        gate = total[:, :hidden] * scale
        upper = total[:, hidden:] * scale
        out_ref[...] = (gate / (1.0 + jnp.exp(-gate)) * upper).astype(BF16)


def units(info, received, weight, groups, carry=()):
    sides, quarters, tiles = received.shape[:3]
    hidden = weight.shape[0] // 2
    rows = sides * groups * SUB
    last = bool(carry)
    single = jax.ShapeDtypeStruct((rows, hidden), BF16)
    double = [
        jax.ShapeDtypeStruct((rows, 2 * hidden), F32),
        jax.ShapeDtypeStruct((rows, LANES), F32),
    ]
    return call(
        functools.partial(units_kernel, groups, last),
        "units_last" if last else "units_first",
        [info],
        [received, weight, *carry],
        [WHOLE] * (2 + len(carry)),
        single if last else double,
        work=rows * weight.size,
        out_specs=WHOLE if last else [WHOLE] * 2,
    )


def down_kernel(info_ref, mine_ref, theirs_ref, own_ref, other_ref, held_ref, out_ref, total):
    chips, steps = out_ref.shape[:2]
    rows = mine_ref.shape[0]
    count = rows // chips
    left = jnp.concatenate(
        [mine_ref[...].astype(F32), theirs_ref[...].astype(F32)], axis=1
    ).astype(BF16)
    width = 4 * LANES
    for step in range(steps):
        span = slice(step * width, step * width + width)
        weight = jnp.concatenate([own_ref[:, span], other_ref[:, span]], axis=0)
        total[:rows, span] = jnp.dot(left, weight, preferred_element_type=F32)
    total[pl.ds(rows, SUB), :] = jnp.zeros((SUB, total.shape[1]), F32)
    lines, columns = held_ref.shape
    place = pl.ds(pl.multiple_of(info_ref[2] * lines, SUB), lines)
    across = pl.ds(pl.multiple_of(info_ref[5] * columns, LANES), columns)
    total[place, across] += held_ref[...]
    sub = lax.broadcasted_iota(jnp.int32, (SUB, LANES), 0)
    for chip in range(chips):
        for step in range(steps):
            span = slice(step * width, step * width + width)
            part = total[chip * count : chip * count + SUB, span]
            quads = [part[:, tile * LANES : tile * LANES + LANES] for tile in range(4)]
            packed = [
                jnp.where(
                    sub < count, quads[tile], pltpu.roll(quads[3], count - 2 * tile, 0)
                )
                for tile in range(3)
            ]
            out_ref[chip, step] = jnp.concatenate(packed, axis=0).astype(BF16)


def down(info, mine, theirs, own, other, held, chips):
    rows = mine.shape[0]
    half = own.shape[1]
    return call(
        down_kernel,
        "down",
        [info],
        [mine, theirs, own, other, held],
        [WHOLE] * 5,
        jax.ShapeDtypeStruct((chips, half // (4 * LANES), 3 * SUB, LANES), BF16),
        [pltpu.VMEM((rows + SUB, half), F32)],
        4 * rows * own.size,
        out_specs=WHOLE,
    )


def finish_kernel(info_ref, parts_ref, mine_ref, theirs_ref):
    total = jnp.sum(parts_ref[...].astype(F32), axis=0)
    sub = lax.broadcasted_iota(jnp.int32, (SUB, LANES), 0)
    columns = []
    for step in range(total.shape[0]):
        quads = [total[step, tile * SUB : tile * SUB + SUB] for tile in range(3)]
        last = jnp.where(
            sub < 2,
            pltpu.roll(quads[0], 2, 0),
            jnp.where(sub < 4, pltpu.roll(quads[1], 4, 0), pltpu.roll(quads[2], 6, 0)),
        )
        columns += quads + [last]
    rows = jnp.concatenate(columns, axis=1)
    first, second = rows[0:3], rows[3:6]
    is_first = info_ref[3] == 0
    mine_ref[...] = jnp.where(is_first, first, second).astype(BF16)
    theirs_ref[...] = jnp.where(is_first, second, first).astype(BF16)


def finish(info, parts):
    shape = jax.ShapeDtypeStruct((3, parts.shape[1] * 4 * LANES), BF16)
    return call(
        finish_kernel,
        "finish",
        [info],
        [parts],
        [WHOLE],
        [shape, shape],
        out_specs=[WHOLE] * 2,
    )


def local(
    query_latent,
    latent_cache,
    lengths,
    stream,
    norm_gain,
    value_up,
    out_proj,
    gate_proj,
    up_proj,
    down_proj,
):
    core = lax.axis_index("core")
    ring = lax.axis_index("y")
    group = lax.axis_index("zl") * 4 + lax.axis_index("x")
    rows_own, width = stream.shape
    rows = query_latent.shape[0]
    half = width // 2
    eighth = width // 8
    first = core == 0
    info = [core * 4 + ring, core, group, core, 1 - core, ring, lax.axis_index("zh"), 0]
    info = jnp.stack(info).astype(jnp.int32)

    out_send, own, *starts = early(info, value_up, stream, out_proj)
    out_theirs = swap(out_send)
    firsts = [shift(part, step) for step, part in zip((1, 2, 3), starts)]
    gain = block(norm_gain, core * 4 + ring, eighth, 0)[None]

    payload, *cuts = attend(
        info,
        lengths,
        query_latent.transpose(0, 2, 1),
        latent_cache.transpose(0, 2, 1),
        out_proj,
        out_theirs,
    )
    payload, *firsts = lax.optimization_barrier((payload, *firsts))
    firsts_theirs = [swap(part) for part in [own] + firsts]
    parts = [shift(part, step) for step, part in zip((1, 2, 3), cuts)]
    received = lax.all_to_all(payload, OUTER, split_axis=0, concat_axis=0, tiled=True)
    chip = (ring - jnp.arange(8)) % 4
    side = jnp.where(jnp.arange(8) < 4, core, 1 - core)
    line = jnp.arange(SUB)[None]
    place = ((chip * 2 + side) * rows_own)[:, None] + line
    place = jnp.where(line < rows_own, place, -1).reshape(1, 8 * SUB).astype(jnp.int32)
    blocks = [own] + firsts + firsts_theirs
    values, stream_rows = join(info, received, value_up, place, blocks, rows, eighth)

    last, parts[0] = lax.optimization_barrier((values, parts[0]))
    ring_values = [values, shift(values, 1), shift(values, 2), shift(last, 3)]
    late, _ = lax.optimization_barrier((values, ring_values[1]))
    both_values = ring_values + [swap(piece) for piece in [late] + ring_values[1:]]
    row = jnp.arange(8 * rows)
    natural = jnp.tile(row % 8 * (8 * rows) + row // 8, 8).reshape(8, 8 * rows)
    place = natural[:, : 8 * rows] + ((chip * 2 + side) * rows)[:, None]
    place = place.reshape(1, 64 * rows).astype(jnp.int32)
    partial = project(
        info,
        place,
        both_values,
        out_proj,
        out_theirs,
        parts,
        16,
    )
    parts = lax.all_to_all(partial, OUTER, split_axis=0, concat_axis=0, tiled=True)

    residual, payload = residual_rows(parts, stream_rows, gain, 32)
    payload, gate_proj, up_proj, down_proj = lax.optimization_barrier(
        (payload, gate_proj, up_proj, down_proj)
    )
    piece = lax.all_to_all(payload, SIDE_CHIPS, split_axis=0, concat_axis=0, tiled=True)
    piece = piece.reshape((8, 4) + piece.shape[1:])
    other = swap(piece)
    weight, down_own, down_send = stage(info, gate_proj.T, up_proj.T, down_proj)
    down_theirs = swap(down_send)
    groups = 8 * rows_own // SUB
    carry = units(info, piece, weight, groups)
    hidden = units(info, other, weight, groups, carry)
    partial = down(info, hidden, swap(hidden), down_own, down_theirs, residual, 32)
    parts = lax.all_to_all(partial, SIDE_CHIPS, split_axis=0, concat_axis=0, tiled=True)
    mine, theirs = finish(info, parts)
    theirs = swap(theirs)
    return jnp.concatenate(
        [jnp.where(first, mine, theirs), jnp.where(first, theirs, mine)], axis=1
    )


def solution(mesh):
    fine = Mesh(mesh.devices.reshape(2, 2, 4, 4, 2), AXES)
    placed = (
        P(DEV, None, None),
        P(DEV, "zh", None),
        P(DEV),
        P(AXES, None),
        P(),
        P(AXES, None, None),
        P(AXES, None),
        P(None, DEV),
        P(None, DEV),
        P(DEV, None),
    )
    return jax.shard_map(
        local, mesh=fine, in_specs=placed, out_specs=P(AXES, None), check_vma=False
    )
```

```python
import functools
import math

import jax
import jax.numpy as jnp
import numpy as np
from jax import lax
from jax.experimental import pallas as pl
from jax.experimental.pallas import tpu as pltpu
from jax.sharding import Mesh, PartitionSpec as P

LAT = 512
QKD = 192
LANES = 128
SUB = 8
AXES = ("zh", "zl", "x", "y", "core")
DEV = ("zl", "x", "y", "core")
OUTER = ("zh", "zl", "x")
SIDE_CHIPS = ("zl", "x", "y")
SWAP = [(0, 1), (1, 0)]
F32 = jnp.float32
BF16 = jnp.bfloat16
VMEM_MOST = 60 * 1024 * 1024
VMEM_STAGE = 44 * 1024 * 1024
VMEM_SOME = 24 * 1024 * 1024


def swap(array):
    return lax.ppermute(array, "core", SWAP)


def shift(array, step):
    return lax.ppermute(array, "y", [(i, (i + step) % 4) for i in range(4)])


def block(array, index, size, axis):
    return lax.dynamic_slice_in_dim(array, index * size, size, axis)


WHOLE = pl.BlockSpec(memory_space=pltpu.VMEM)
ANYWHERE = pl.BlockSpec(memory_space=pl.ANY)


def full(shape):
    return pl.BlockSpec(shape, lambda i, *info: (0,) * len(shape))


def call(kernel, name, scalars, arrays, specs, outs, scratch=(), work=None, limit=VMEM_SOME, out_specs=None):
    single = not isinstance(outs, list)
    shapes = [outs] if single else outs
    return pl.pallas_call(
        kernel,
        out_shape=outs,
        grid_spec=pltpu.PrefetchScalarGridSpec(
            num_scalar_prefetch=len(scalars),
            grid=(1,),
            in_specs=[full(a.shape) if s is None else s for a, s in zip(arrays, specs)],
            out_specs=out_specs
            or (full(outs.shape) if single else [full(o.shape) for o in outs]),
            scratch_shapes=list(scratch),
        ),
        compiler_params=pltpu.CompilerParams(
            vmem_limit_bytes=limit, dimension_semantics=("arbitrary",)
        ),
        cost_estimate=pl.CostEstimate(
            flops=work or 0,
            bytes_accessed=2 * sum(math.prod(a.shape) for a in list(arrays) + shapes),
            transcendentals=0,
        ),
        name=name,
    )(*scalars, *arrays)


def rounded(value):
    return value.astype(BF16).astype(F32)


def attend_kernel(
    info_ref,
    lengths_ref,
    query_hbm,
    cache_hbm,
    up_hbm,
    stream_hbm,
    out_ref,
    *refs,
):
    maps = refs[:4]
    query_ref, cache_ref, up_ref, stream_ref, sems = refs[4:]
    rows, _, heads = query_ref.shape
    keys = cache_ref.shape[2]
    pairs = rows // 2
    copies = [pltpu.make_async_copy(query_hbm, query_ref, sems.at[pairs])] + [
        pltpu.make_async_copy(
            cache_hbm.at[pl.ds(2 * pair, 2)], cache_ref.at[pl.ds(2 * pair, 2)], sems.at[pair]
        )
        for pair in range(pairs)
    ]
    copies += [
        pltpu.make_async_copy(up_hbm, up_ref, sems.at[pairs + 1]),
        pltpu.make_async_copy(stream_hbm, stream_ref, sems.at[pairs + 2]),
    ]
    for copy in copies:
        copy.start()
    copies[0].wait()
    tiles = [slice(start, start + LANES) for start in range(0, LAT, LANES)]
    position = lax.broadcasted_iota(jnp.int32, (1, keys), 1) + info_ref[6] * keys
    lane = lax.broadcasted_iota(jnp.int32, (heads, LANES), 1)
    table = jnp.zeros((heads, LANES), F32)
    for row in range(rows):
        if row % 2 == 0:
            copies[1 + row // 2].wait()
        cached = cache_ref[row]
        scores = lax.dot_general(
            query_ref[row], cached, (((0,), (0,)), ((), ())), preferred_element_type=F32
        ) * (1.0 / math.sqrt(QKD))
        usable = position < lengths_ref[row]
        scores = jnp.where(usable, scores, F32(-1e30))
        top = jnp.max(scores, axis=1, keepdims=True)
        top_high = rounded(top)
        top_low = rounded(top - top_high)
        exponent = jnp.where(usable, jnp.exp(scores - (top_high + top_low)), F32(0.0))
        total = jnp.sum(exponent, axis=1, keepdims=True)
        total_high = rounded(total)
        total_low = rounded(total - total_high)
        weighted = lax.dot_general(
            exponent.astype(BF16),
            cached[:LAT],
            (((1,), (1,)), ((), ())),
            preferred_element_type=F32,
        )
        for number, tile in enumerate(tiles):
            out_ref[:, row * len(tiles) + number] = (
                weighted[:, tile].reshape(heads // SUB, SUB, LANES).astype(BF16)
            )
        table = jnp.where(lane == row, top_high, table)
        table = jnp.where(lane == row + SUB, top_low, table)
        table = jnp.where(lane == row + 2 * SUB, total_high, table)
        table = jnp.where(lane == row + 3 * SUB, total_low, table)
    out_ref[:, rows * len(tiles)] = table.reshape(heads // SUB, SUB, LANES).astype(BF16)
    for copy in copies[-2:]:
        copy.wait()
    eighth = stream_ref.shape[1] // 8
    columns = eighth // LANES
    ups = up_ref.shape[1] // LANES
    lines_own = stream_ref.shape[0]
    for step, map_ref in enumerate(maps):
        map_ref[:ups] = up_ref[0].reshape(ups, LANES, LANES)
        lines = []
        for side in (3, 4):
            chip = info_ref[side] * 4 + lax.rem(info_ref[5] + step, 4)
            first = pl.multiple_of(chip * eighth, LANES)
            data = stream_ref[:, pl.ds(first, eighth)].astype(F32)
            for lane in range(0, eighth, LANES):
                lines.append(data[:, lane : lane + LANES])
                lines.append(jnp.zeros((SUB - lines_own, LANES), F32))
            lines.append(jnp.zeros((LANES // 2 - columns * SUB, LANES), F32))
        map_ref[ups] = jnp.concatenate(lines, axis=0).astype(BF16)


def attend(info, lengths, query, cache, value_up, stream):
    rows, depth, heads = query.shape
    keys = cache.shape[2]
    shape = (heads // SUB, rows * (LAT // LANES) + 1, SUB, LANES)
    return call(
        attend_kernel,
        "attend",
        [info, lengths],
        [query, cache, value_up, stream],
        [ANYWHERE] * 4,
        [jax.ShapeDtypeStruct(shape, BF16)]
        + [jax.ShapeDtypeStruct((value_up.shape[1] // LANES + 1, LANES, LANES), BF16)] * 4,
        [
            pltpu.VMEM(query.shape, BF16),
            pltpu.VMEM(cache.shape, BF16),
            pltpu.VMEM(value_up.shape, BF16),
            pltpu.VMEM(stream.shape, BF16),
            pltpu.SemaphoreType.DMA((rows // 2 + 3,)),
        ],
        2 * rows * heads * keys * (depth + LAT),
        VMEM_MOST,
    )


def cut_kernel(info_ref, *refs):
    del info_ref
    steps = len(refs) // 3
    for step in range(steps):
        out_ref = refs[2 * steps + step]
        columns = out_ref.shape[0] // 2
        for side in range(2):
            for column in range(columns):
                span = slice(column * LANES, column * LANES + LANES)
                out_ref[side * columns + column] = refs[side * steps + step][:, span]


def cut(info, mine, theirs):
    rows, half = theirs.shape
    eighth = half // 4
    part = jax.ShapeDtypeStruct((2 * eighth // LANES, rows, LANES), BF16)

    def column(side, step):
        return pl.BlockSpec(
            (rows, eighth),
            lambda i, info: (0, info[side] * 4 + lax.rem(info[5] + step, 4)),
        )

    return call(
        cut_kernel,
        "cut",
        [info],
        [mine] * 3 + [theirs] * 3,
        [column(3, step) for step in (1, 2, 3)] + [column(7, step) for step in (1, 2, 3)],
        [part] * 3,
        limit=VMEM_MOST,
    )


def stage_kernel(info_ref, gate_ref, up_ref, down_ref, *refs):
    outs, own_ref, send_ref, sems = refs[:2], refs[2], refs[3], refs[4]
    rows, width = gate_ref.shape
    half = width // 2

    def part(ref, side):
        return ref.at[:, pl.ds(pl.multiple_of(info_ref[side] * half, LANES), half)]

    copies = [(part(down_ref, 4), send_ref)]
    for side, out_ref in zip((3, 4), outs):
        copies.append((part(gate_ref, side), out_ref.at[pl.ds(0, rows), :]))
        copies.append((part(up_ref, side), out_ref.at[pl.ds(rows, rows), :]))
    copies.append((part(down_ref, 3), own_ref))
    copies = [
        pltpu.make_async_copy(source, target, sems.at[index])
        for index, (source, target) in enumerate(copies)
    ]
    for copy in copies:
        copy.start()
    for copy in copies:
        copy.wait()


def stage(info, gate, up, down_proj):
    rows, width = gate.shape
    both = jax.ShapeDtypeStruct((2 * rows, width // 2), BF16)
    half = jax.ShapeDtypeStruct((down_proj.shape[0], down_proj.shape[1] // 2), BF16)
    return call(
        stage_kernel,
        "stage",
        [info],
        [gate, up, down_proj],
        [ANYWHERE] * 3,
        [both, both, half, half],
        [pltpu.SemaphoreType.DMA((6,))],
        limit=VMEM_STAGE,
        out_specs=[WHOLE] * 4,
    )


def join_kernel(rows, info_ref, recv_ref, own_ref, *refs):
    blocks, sum_ref, out_ref, stream_ref = refs[:8], refs[8], refs[9], refs[10]
    lines_own = stream_ref.shape[0] // len(blocks)
    shape = (stream_ref.shape[0], SUB)
    target = lax.broadcasted_iota(jnp.int32, shape, 0)
    line = lax.broadcasted_iota(jnp.int32, shape, 1)
    stream = None
    for index, ref in enumerate(blocks):
        lines = ref[ref.shape[0] - 1].astype(F32)
        base = LANES // 2 * (index // 4)
        spans = range(base, base + stream_ref.shape[1] // LANES * SUB, SUB)
        lines = jnp.concatenate([lines[span : span + SUB] for span in spans], axis=1)
        chip = lax.rem(info_ref[5] + 4 - index % 4, 4)
        first = (chip * 2 + info_ref[3 + index // 4]) * lines_own
        order = (target == line + first) & (line < lines_own)
        order = jnp.where(order, F32(1.0), F32(0.0)).astype(BF16)
        part = jnp.dot(order, lines.astype(BF16), preferred_element_type=F32)
        stream = part if stream is None else stream + part
    stream_ref[...] = stream
    sides = 2
    devs = recv_ref.shape[0] // sides
    tiles = LAT // LANES
    table = recv_ref[:, rows * tiles].astype(F32).reshape(sides, devs, SUB, LANES)
    lane = lax.broadcasted_iota(jnp.int32, (SUB, LANES), 1)

    def pick(first):
        chosen = (lane == first) | (lane == first + SUB)
        return jnp.sum(jnp.where(chosen, table, F32(0.0)), axis=3, keepdims=True)

    latents = []
    for row in range(rows):
        peaks = pick(row)
        totals = pick(2 * SUB + row)
        factor = jnp.exp(peaks - jnp.maximum(peaks[:1], peaks[1:]))
        factor = factor / (factor[:1] * totals[:1] + factor[1:] * totals[1:])
        parts = [
            recv_ref[:, row * tiles + number].astype(F32).reshape(sides, devs, SUB, LANES)
            for number in range(tiles)
        ]
        joined = [part[0] * factor[0] + part[1] * factor[1] for part in parts]
        latents.append(
            jnp.concatenate([part.reshape(devs * SUB, LANES) for part in joined], axis=1)
        )
    latent = jnp.concatenate(latents, axis=0).astype(BF16)
    maps = [own_ref[0]]
    maps += [ref[:tiles].reshape(LAT, LANES) for ref in blocks[1:]]
    products = jnp.dot(
        latent, jnp.concatenate(maps, axis=1), preferred_element_type=F32
    ).reshape(rows * devs, SUB, len(maps) * LANES)
    sub = lax.broadcasted_iota(jnp.int32, (1, SUB, LANES), 1)
    masked = []
    for piece in range(len(maps)):
        chip = lax.rem(info_ref[5] + 4 - piece % 4, 4)
        head = chip * 2 + info_ref[3 + piece // 4]
        part = products[:, :, piece * LANES : piece * LANES + LANES]
        masked.append(jnp.where(sub == head, part, F32(0.0)))
    masked = jnp.concatenate(masked, axis=2).reshape(rows * devs * SUB, len(maps) * LANES)
    out_ref[...] = jnp.dot(
        sum_ref[...], masked.astype(BF16), preferred_element_type=F32
    ).astype(BF16)


def join(info, received, value_up, blocks, rows, eighth):
    devs = received.shape[0] // 2
    count = rows * devs
    sums = np.repeat(np.eye(count, dtype=np.float32), SUB, axis=1)
    arrays = [received, value_up, *blocks, jnp.asarray(sums, BF16)]
    return call(
        functools.partial(join_kernel, rows),
        "join",
        [info],
        arrays,
        [None] * len(arrays),
        [
            jax.ShapeDtypeStruct((count, SUB * LANES), BF16),
            jax.ShapeDtypeStruct((4 * rows, eighth), F32),
        ],
        work=480_000_000,
        limit=VMEM_MOST,
    )


def project_kernel(info_ref, natural_ref, *refs):
    values, own_ref, theirs_ref = refs[:8], refs[8], refs[9]
    parts, out_ref = refs[10:13], refs[13]
    rows = []
    for source, ref in enumerate(values):
        data = ref[...]
        lanes = []
        for piece in range(8):
            step = (piece - source) % 4
            side = piece // 4 ^ source // 4
            start = (side * 4 + step) * LANES
            lanes.append(data[:, start : start + LANES])
        rows.append(jnp.concatenate(lanes, axis=1))
    left = jnp.concatenate(rows, axis=0)
    count = left.shape[0]
    place = natural_ref[0:1]
    for source in range(8):
        chip = lax.rem(info_ref[5] + 4 - source % 4, 4)
        first = (chip * 2 + info_ref[3 + source // 4]) * (count // 64)
        place = place + jnp.where(natural_ref[1:2] == source, first, 0)
    order = lax.broadcasted_iota(jnp.int32, (count, count), 0) == place
    order = jnp.where(order, F32(1.0), F32(0.0)).astype(BF16)
    left = jnp.dot(order, left, preferred_element_type=F32).astype(BF16)
    columns = own_ref.shape[1] // LANES
    right = []
    for side, held_ref in enumerate((own_ref, theirs_ref)):
        right.append(held_ref[...])
        for ref in parts:
            tiles = [ref[side * columns + column] for column in range(columns)]
            right.append(jnp.concatenate(tiles, axis=1))
    right = jnp.concatenate(right, axis=0)
    total = jnp.dot(left, right, preferred_element_type=F32)
    out_ref[...] = total.reshape(out_ref.shape).astype(BF16)


def project(info, values, out_proj, out_theirs, parts, chips):
    rows = sum(value.shape[0] for value in values)
    lanes = out_proj.shape[0]
    eighth = out_proj.shape[1] // 8
    line = np.arange(rows) % (rows // 8)
    natural = np.stack([line % 8 * (rows // 8) + line // 8, np.arange(rows) // (rows // 8)])
    natural = jnp.asarray(natural, jnp.int32)
    own = pl.BlockSpec((lanes, eighth), lambda i, info: (0, info[0]))
    other = pl.BlockSpec((lanes, eighth), lambda i, info: (0, info[5]))
    return call(
        project_kernel,
        "project",
        [info],
        [natural, *values, out_proj, out_theirs, *parts],
        [None] * 9 + [own, other] + [None] * 3,
        jax.ShapeDtypeStruct((chips, rows // chips, eighth), BF16),
        work=2 * rows * 8 * lanes * eighth,
        limit=VMEM_MOST,
    )


def residual_kernel(parts_ref, stream_ref, gain_ref, residual_ref, out_ref):
    rows, width = residual_ref.shape
    residual = stream_ref[...] + jnp.sum(parts_ref[...].astype(F32), axis=0)
    residual_ref[...] = residual
    squares = jnp.sum(residual * residual, axis=1, keepdims=True)
    high = rounded(squares)
    low = rounded(squares - high)
    lane = lax.broadcasted_iota(jnp.int32, (SUB, LANES), 1)
    table = jnp.zeros((SUB, LANES), F32)
    scaled = residual * gain_ref[...]
    groups = rows // SUB
    columns = width // LANES
    chips = out_ref.shape[0]
    for group in range(groups):
        span = slice(group * SUB, group * SUB + SUB)
        table = jnp.where(lane == group, high[span], table)
        table = jnp.where(lane == SUB + group, low[span], table)
    tiles = [
        scaled[group * SUB : group * SUB + SUB, column * LANES : column * LANES + LANES]
        for column in range(columns)
        for group in range(groups)
    ] + [table]
    for index, tile in enumerate(tiles):
        out_ref[:, index] = jnp.broadcast_to(tile.astype(BF16)[None], (chips, SUB, LANES))


def residual_rows(parts, stream, gain, chips):
    _, rows, width = parts.shape
    tiles = rows * width // (SUB * LANES) + 1
    return call(
        residual_kernel,
        "residual",
        [],
        [parts, stream, gain],
        [None] * 3,
        [
            jax.ShapeDtypeStruct((rows, width), F32),
            jax.ShapeDtypeStruct((chips, tiles, SUB, LANES), BF16),
        ],
    )


def units_kernel(groups, last, recv_ref, weight_ref, *refs):
    sides, quarters, tiles, _, _ = recv_ref.shape
    columns = (tiles - 1) // groups
    rows = sides * groups * SUB
    depth = columns * LANES
    lane = lax.broadcasted_iota(jnp.int32, (SUB, LANES), 1)
    total = squares = None
    for quarter in range(quarters):
        left = jnp.concatenate(
            [
                recv_ref[:, quarter, column * groups : column * groups + groups]
                .astype(F32)
                .reshape(rows, LANES)
                for column in range(columns)
            ],
            axis=1,
        ).astype(BF16)
        part = lax.dot_general(
            left,
            weight_ref[:, quarter * depth : quarter * depth + depth],
            (((1,), (1,)), ((), ())),
            preferred_element_type=F32,
        )
        total = part if total is None else total + part
        table = recv_ref[:, quarter, tiles - 1].astype(F32)
        pieces = [
            jnp.sum(
                jnp.where((lane == group) | (lane == SUB + group), table, F32(0.0)),
                axis=2,
                keepdims=True,
            )
            for group in range(groups)
        ]
        part = jnp.stack(pieces, axis=1).reshape(rows, 1)
        squares = part if squares is None else squares + part
    if not last:
        acc_ref, sq_ref = refs
        acc_ref[...] = total
        sq_ref[...] = jnp.broadcast_to(squares, (rows, LANES))
    else:
        acc_ref, sq_ref, out_ref = refs
        hidden = out_ref.shape[1]
        scale = lax.rsqrt((sq_ref[:, :1] + squares) / (2 * weight_ref.shape[1]) + 1e-06)
        total = total + acc_ref[...]
        gate = total[:, :hidden] * scale
        upper = total[:, hidden:] * scale
        out_ref[...] = (gate / (1.0 + jnp.exp(-gate)) * upper).astype(BF16)


def units(received, weight, groups, carry=()):
    sides, quarters, tiles = received.shape[:3]
    hidden = weight.shape[0] // 2
    rows = sides * groups * SUB
    last = bool(carry)
    single = jax.ShapeDtypeStruct((rows, hidden), BF16)
    double = [
        jax.ShapeDtypeStruct((rows, 2 * hidden), F32),
        jax.ShapeDtypeStruct((rows, LANES), F32),
    ]
    return call(
        functools.partial(units_kernel, groups, last),
        "units_last" if last else "units_first",
        [],
        [received, weight, *carry],
        [WHOLE] * (2 + len(carry)),
        single if last else double,
        work=2 * rows * weight.size,
        out_specs=WHOLE if last else [WHOLE] * 2,
    )


def down_kernel(info_ref, mine_ref, theirs_ref, own_ref, other_ref, held_ref, out_ref, total):
    chips, steps = out_ref.shape[:2]
    rows = mine_ref.shape[0]
    count = rows // chips
    left = jnp.concatenate(
        [mine_ref[...].astype(F32), theirs_ref[...].astype(F32)], axis=1
    ).astype(BF16)
    width = 4 * LANES
    for step in range(steps):
        span = slice(step * width, step * width + width)
        weight = jnp.concatenate([own_ref[:, span], other_ref[:, span]], axis=0)
        total[:rows, span] = jnp.dot(left, weight, preferred_element_type=F32)
    total[pl.ds(rows, SUB), :] = jnp.zeros((SUB, total.shape[1]), F32)
    lines, columns = held_ref.shape
    place = pl.ds(pl.multiple_of(info_ref[2] * lines, SUB), lines)
    across = pl.ds(pl.multiple_of(info_ref[5] * columns, LANES), columns)
    total[place, across] += held_ref[...]
    sub = lax.broadcasted_iota(jnp.int32, (SUB, LANES), 0)
    for chip in range(chips):
        for step in range(steps):
            span = slice(step * width, step * width + width)
            part = total[chip * count : chip * count + SUB, span]
            quads = [part[:, tile * LANES : tile * LANES + LANES] for tile in range(4)]
            packed = [
                jnp.where(
                    sub < count, quads[tile], pltpu.roll(quads[3], count - 2 * tile, 0)
                )
                for tile in range(3)
            ]
            out_ref[chip, step] = jnp.concatenate(packed, axis=0).astype(BF16)


def down(info, mine, theirs, own, other, held, chips):
    rows = mine.shape[0]
    half = own.shape[1]
    return call(
        down_kernel,
        "down",
        [info],
        [mine, theirs, own, other, held],
        [WHOLE] * 5,
        jax.ShapeDtypeStruct((chips, half // (4 * LANES), 3 * SUB, LANES), BF16),
        [pltpu.VMEM((rows + SUB, half), F32)],
        4 * rows * own.size,
        out_specs=WHOLE,
    )


def finish_kernel(info_ref, parts_ref, mine_ref, theirs_ref):
    total = jnp.sum(parts_ref[...].astype(F32), axis=0)
    sub = lax.broadcasted_iota(jnp.int32, (SUB, LANES), 0)
    columns = []
    for step in range(total.shape[0]):
        quads = [total[step, tile * SUB : tile * SUB + SUB] for tile in range(3)]
        last = jnp.where(
            sub < 2,
            pltpu.roll(quads[0], 2, 0),
            jnp.where(sub < 4, pltpu.roll(quads[1], 4, 0), pltpu.roll(quads[2], 6, 0)),
        )
        columns += quads + [last]
    rows = jnp.concatenate(columns, axis=1)
    first, second = rows[0:3], rows[3:6]
    is_first = info_ref[3] == 0
    mine_ref[...] = jnp.where(is_first, first, second).astype(BF16)
    theirs_ref[...] = jnp.where(is_first, second, first).astype(BF16)


def finish(info, parts):
    shape = jax.ShapeDtypeStruct((3, parts.shape[1] * 4 * LANES), BF16)
    return call(
        finish_kernel,
        "finish",
        [info],
        [parts],
        [WHOLE],
        [shape, shape],
        out_specs=[WHOLE] * 2,
    )


def local(
    query_latent,
    latent_cache,
    lengths,
    stream,
    norm_gain,
    value_up,
    out_proj,
    gate_proj,
    up_proj,
    down_proj,
):
    core = lax.axis_index("core")
    ring = lax.axis_index("y")
    group = lax.axis_index("zl") * 4 + lax.axis_index("x")
    rows_own, width = stream.shape
    rows = query_latent.shape[0]
    half = width // 2
    eighth = width // 8
    first = core == 0
    info = [core * 4 + ring, core, group, core, 1 - core, ring, lax.axis_index("zh"), 0]
    info = jnp.stack(info).astype(jnp.int32)

    gain = block(norm_gain, core * 4 + ring, eighth, 0)[None]

    out_theirs = swap(block(out_proj, 1 - core, half, 1))
    payload, own, *firsts = attend(
        info,
        lengths,
        query_latent.transpose(0, 2, 1),
        latent_cache.transpose(0, 2, 1),
        value_up,
        stream,
    )
    payload, out_theirs = lax.optimization_barrier((payload, out_theirs))
    firsts = [shift(part, step) for step, part in zip((1, 2, 3), firsts)]
    parts = list(cut(info, out_proj, out_theirs))
    parts[0], parts[2], *firsts = lax.optimization_barrier((parts[0], parts[2], *firsts))
    firsts_theirs = [swap(part) for part in [own] + firsts]
    part_one, part_three = shift(parts[0], 1), shift(parts[2], 3)
    received = lax.all_to_all(payload, OUTER, split_axis=0, concat_axis=0, tiled=True)
    blocks = [own] + firsts + firsts_theirs
    values, stream_rows = join(info, received, value_up, blocks, rows, eighth)
    far, part_one, part_three = lax.optimization_barrier((parts[1], part_one, part_three))
    parts = [part_one, shift(far, 2), part_three]

    ring_values = [values] + [shift(values, step) for step in (1, 2, 3)]
    both_values = ring_values + [swap(piece) for piece in ring_values]
    partial = project(
        info,
        both_values,
        out_proj,
        out_theirs,
        parts,
        16,
    )
    parts = lax.all_to_all(partial, OUTER, split_axis=0, concat_axis=0, tiled=True)

    residual, payload = residual_rows(parts, stream_rows, gain, 32)
    payload, gate_proj, up_proj, down_proj = lax.optimization_barrier(
        (payload, gate_proj, up_proj, down_proj)
    )
    piece = lax.all_to_all(payload, SIDE_CHIPS, split_axis=0, concat_axis=0, tiled=True)
    piece = piece.reshape((8, 4) + piece.shape[1:])
    other = swap(piece)
    first_weight, last_weight, down_own, down_send = stage(info, gate_proj.T, up_proj.T, down_proj)
    down_theirs = swap(down_send)
    groups = 8 * rows_own // SUB
    carry = units(piece, first_weight, groups)
    hidden = units(other, last_weight, groups, carry)
    partial = down(info, hidden, swap(hidden), down_own, down_theirs, residual, 32)
    parts = lax.all_to_all(partial, SIDE_CHIPS, split_axis=0, concat_axis=0, tiled=True)
    mine, theirs = finish(info, parts)
    theirs = swap(theirs)
    return jnp.concatenate(
        [jnp.where(first, mine, theirs), jnp.where(first, theirs, mine)], axis=1
    )


def solution(mesh):
    fine = Mesh(mesh.devices.reshape(2, 2, 4, 4, 2), AXES)
    placed = (
        P(DEV, None, None),
        P(DEV, "zh", None),
        P(DEV),
        P(AXES, None),
        P(),
        P(AXES, None, None),
        P(AXES, None),
        P(None, DEV),
        P(None, DEV),
        P(DEV, None),
    )
    return jax.shard_map(
        local, mesh=fine, in_specs=placed, out_specs=P(AXES, None), check_vma=False
    )
```

```python
import functools
import math

import jax
import jax.numpy as jnp
import numpy as np
from jax import lax
from jax.experimental import pallas as pl
from jax.experimental.pallas import tpu as pltpu
from jax.sharding import Mesh, PartitionSpec as P

LAT = 512
QKD = 192
LANES = 128
SUB = 8
AXES = ("zh", "zl", "x", "y", "core")
DEV = ("zl", "x", "y", "core")
OUTER = ("zh", "zl", "x")
SIDE_CHIPS = ("zl", "x", "y")
SWAP = [(0, 1), (1, 0)]
F32 = jnp.float32
BF16 = jnp.bfloat16
VMEM_MOST = 60 * 1024 * 1024
VMEM_STAGE = 44 * 1024 * 1024
VMEM_SOME = 24 * 1024 * 1024


def swap(array):
    return lax.ppermute(array, "core", SWAP)


def shift(array, step):
    return lax.ppermute(array, "y", [(i, (i + step) % 4) for i in range(4)])


def block(array, index, size, axis):
    return lax.dynamic_slice_in_dim(array, index * size, size, axis)


WHOLE = pl.BlockSpec(memory_space=pltpu.VMEM)
ANYWHERE = pl.BlockSpec(memory_space=pl.ANY)


def full(shape):
    return pl.BlockSpec(shape, lambda i, *info: (0,) * len(shape))


def call(kernel, name, scalars, arrays, specs, outs, scratch=(), work=None, limit=VMEM_SOME, out_specs=None):
    single = not isinstance(outs, list)
    shapes = [outs] if single else outs
    return pl.pallas_call(
        kernel,
        out_shape=outs,
        grid_spec=pltpu.PrefetchScalarGridSpec(
            num_scalar_prefetch=len(scalars),
            grid=(1,),
            in_specs=[full(a.shape) if s is None else s for a, s in zip(arrays, specs)],
            out_specs=out_specs
            or (full(outs.shape) if single else [full(o.shape) for o in outs]),
            scratch_shapes=list(scratch),
        ),
        compiler_params=pltpu.CompilerParams(
            vmem_limit_bytes=limit, dimension_semantics=("arbitrary",)
        ),
        cost_estimate=pl.CostEstimate(
            flops=work or 0,
            bytes_accessed=2 * sum(math.prod(a.shape) for a in list(arrays) + shapes),
            transcendentals=0,
        ),
        name=name,
    )(*scalars, *arrays)


def rounded(value):
    return value.astype(BF16).astype(F32)


def attend_kernel(
    info_ref, lengths_ref, query_hbm, cache_hbm, out_proj_hbm, theirs_hbm, out_ref, *refs
):
    cuts, (query_ref, cache_ref, weight_ref, sems) = refs[:3], refs[3:]
    half = theirs_hbm.shape[1]
    mine = out_proj_hbm.at[:, pl.ds(pl.multiple_of(info_ref[3] * half, LANES), half)]
    rows, _, heads = query_ref.shape
    keys = cache_ref.shape[2]
    pairs = rows // 2
    copies = [pltpu.make_async_copy(query_hbm, query_ref, sems.at[pairs])] + [
        pltpu.make_async_copy(
            cache_hbm.at[pl.ds(2 * pair, 2)], cache_ref.at[pl.ds(2 * pair, 2)], sems.at[pair]
        )
        for pair in range(pairs)
    ]
    for side, ref in enumerate((mine, theirs_hbm)):
        copies.append(
            pltpu.make_async_copy(ref, weight_ref.at[side], sems.at[pairs + 1 + side])
        )
    for copy in copies:
        copy.start()
    copies[0].wait()
    tiles = [slice(start, start + LANES) for start in range(0, LAT, LANES)]
    position = lax.broadcasted_iota(jnp.int32, (1, keys), 1) + info_ref[6] * keys
    lane = lax.broadcasted_iota(jnp.int32, (heads, LANES), 1)
    table = jnp.zeros((heads, LANES), F32)
    for row in range(rows):
        if row % 2 == 0:
            copies[1 + row // 2].wait()
        cached = cache_ref[row]
        scores = lax.dot_general(
            query_ref[row], cached, (((0,), (0,)), ((), ())), preferred_element_type=F32
        ) * (1.0 / math.sqrt(QKD))
        usable = position < lengths_ref[row]
        scores = jnp.where(usable, scores, F32(-1e30))
        top = jnp.max(scores, axis=1, keepdims=True)
        top_high = rounded(top)
        top_low = rounded(top - top_high)
        exponent = jnp.where(usable, jnp.exp(scores - (top_high + top_low)), F32(0.0))
        total = jnp.sum(exponent, axis=1, keepdims=True)
        total_high = rounded(total)
        total_low = rounded(total - total_high)
        weighted = lax.dot_general(
            exponent.astype(BF16),
            cached[:LAT],
            (((1,), (1,)), ((), ())),
            preferred_element_type=F32,
        )
        for number, tile in enumerate(tiles):
            out_ref[:, row * len(tiles) + number] = (
                weighted[:, tile].reshape(heads // SUB, SUB, LANES).astype(BF16)
            )
        table = jnp.where(lane == row, top_high, table)
        table = jnp.where(lane == row + SUB, top_low, table)
        table = jnp.where(lane == row + 2 * SUB, total_high, table)
        table = jnp.where(lane == row + 3 * SUB, total_low, table)
    out_ref[:, rows * len(tiles)] = table.reshape(heads // SUB, SUB, LANES).astype(BF16)
    copies[-2].wait()
    copies[-1].wait()
    for step, cut_ref in enumerate(cuts):
        columns = cut_ref.shape[0] // 2
        first = lax.rem(info_ref[5] + step + 1, 4) * columns
        for side in range(2):
            for column in range(columns):
                start = pl.multiple_of((first + column) * LANES, LANES)
                cut_ref[side * columns + column] = weight_ref[side, :, pl.ds(start, LANES)]


def attend(info, lengths, query, cache, out_proj, theirs):
    rows, depth, heads = query.shape
    keys = cache.shape[2]
    shape = (heads // SUB, rows * (LAT // LANES) + 1, SUB, LANES)
    columns = out_proj.shape[1] // 8 // LANES
    return call(
        attend_kernel,
        "attend",
        [info, lengths],
        [query, cache, out_proj, theirs],
        [ANYWHERE] * 4,
        [jax.ShapeDtypeStruct(shape, BF16)]
        + [jax.ShapeDtypeStruct((2 * columns, LANES, LANES), BF16)] * 3,
        [
            pltpu.VMEM(query.shape, BF16),
            pltpu.VMEM(cache.shape, BF16),
            pltpu.VMEM((2,) + theirs.shape, BF16),
            pltpu.SemaphoreType.DMA((rows // 2 + 3,)),
        ],
        2 * rows * heads * keys * (depth + LAT),
        VMEM_MOST,
    )


def early_kernel(info_ref, up_ref, stream_ref, half_ref, send_ref, *outs):
    send_ref[...] = half_ref[...]
    rows, width = stream_ref.shape
    eighth = width // 8
    ups = up_ref.shape[1] // LANES
    for step, out_ref in enumerate(outs):
        out_ref[:ups] = up_ref[0].reshape(ups, LANES, LANES)
        chip = lax.rem(info_ref[5] + step, 4)
        lines = []
        for side in (3, 4):
            start = pl.multiple_of((info_ref[side] * 4 + chip) * eighth, LANES)
            data = stream_ref[:, pl.ds(start, eighth)].astype(F32)
            for lane in range(0, eighth, LANES):
                lines.append(data[:, lane : lane + LANES])
                lines.append(jnp.zeros((SUB - rows, LANES), F32))
            lines.append(jnp.zeros((LANES // 2 - eighth // LANES * SUB, LANES), F32))
        out_ref[ups] = jnp.concatenate(lines, axis=0).astype(BF16)


def early(info, value_up, stream, out_proj):
    part = jax.ShapeDtypeStruct((value_up.shape[1] // LANES + 1, LANES, LANES), BF16)
    half = (out_proj.shape[0], out_proj.shape[1] // 2)
    return call(
        early_kernel,
        "early",
        [info],
        [value_up, stream, out_proj],
        [None, None, pl.BlockSpec(half, lambda i, info: (0, info[4]))],
        [jax.ShapeDtypeStruct(half, BF16)] + [part] * 4,
        limit=VMEM_MOST,
    )


def stage_kernel(info_ref, gate_ref, up_ref, down_ref, *refs):
    outs, own_ref, send_ref, sems = refs[:2], refs[2], refs[3], refs[4]
    rows, width = gate_ref.shape
    half = width // 2

    def part(ref, side):
        return ref.at[:, pl.ds(pl.multiple_of(info_ref[side] * half, LANES), half)]

    copies = [(part(down_ref, 4), send_ref)]
    for side, out_ref in zip((3, 4), outs):
        copies.append((part(gate_ref, side), out_ref.at[pl.ds(0, rows), :]))
        copies.append((part(up_ref, side), out_ref.at[pl.ds(rows, rows), :]))
    copies.append((part(down_ref, 3), own_ref))
    copies = [
        pltpu.make_async_copy(source, target, sems.at[index])
        for index, (source, target) in enumerate(copies)
    ]
    for copy in copies:
        copy.start()
    for copy in copies:
        copy.wait()


def stage(info, gate, up, down_proj):
    rows, width = gate.shape
    both = jax.ShapeDtypeStruct((2 * rows, width // 2), BF16)
    half = jax.ShapeDtypeStruct((down_proj.shape[0], down_proj.shape[1] // 2), BF16)
    return call(
        stage_kernel,
        "stage",
        [info],
        [gate, up, down_proj],
        [ANYWHERE] * 3,
        [both, both, half, half],
        [pltpu.SemaphoreType.DMA((6,))],
        limit=VMEM_STAGE,
        out_specs=[WHOLE] * 4,
    )


def join_kernel(rows, info_ref, recv_ref, own_ref, *refs):
    blocks, sum_ref, out_ref, stream_ref = refs[:8], refs[8], refs[9], refs[10]
    lines_own = stream_ref.shape[0] // len(blocks)
    shape = (stream_ref.shape[0], SUB)
    target = lax.broadcasted_iota(jnp.int32, shape, 0)
    line = lax.broadcasted_iota(jnp.int32, shape, 1)
    stream = None
    for index, ref in enumerate(blocks):
        lines = ref[ref.shape[0] - 1].astype(F32)
        base = LANES // 2 * (index // 4)
        spans = range(base, base + stream_ref.shape[1] // LANES * SUB, SUB)
        lines = jnp.concatenate([lines[span : span + SUB] for span in spans], axis=1)
        chip = lax.rem(info_ref[5] + 4 - index % 4, 4)
        first = (chip * 2 + info_ref[3 + index // 4]) * lines_own
        order = (target == line + first) & (line < lines_own)
        order = jnp.where(order, F32(1.0), F32(0.0)).astype(BF16)
        part = jnp.dot(order, lines.astype(BF16), preferred_element_type=F32)
        stream = part if stream is None else stream + part
    stream_ref[...] = stream
    sides = 2
    devs = recv_ref.shape[0] // sides
    tiles = LAT // LANES
    table = recv_ref[:, rows * tiles].astype(F32).reshape(sides, devs, SUB, LANES)
    lane = lax.broadcasted_iota(jnp.int32, (SUB, LANES), 1)

    def pick(first):
        chosen = (lane == first) | (lane == first + SUB)
        return jnp.sum(jnp.where(chosen, table, F32(0.0)), axis=3, keepdims=True)

    latents = []
    for row in range(rows):
        peaks = pick(row)
        totals = pick(2 * SUB + row)
        factor = jnp.exp(peaks - jnp.maximum(peaks[:1], peaks[1:]))
        factor = factor / (factor[:1] * totals[:1] + factor[1:] * totals[1:])
        parts = [
            recv_ref[:, row * tiles + number].astype(F32).reshape(sides, devs, SUB, LANES)
            for number in range(tiles)
        ]
        joined = [part[0] * factor[0] + part[1] * factor[1] for part in parts]
        latents.append(
            jnp.concatenate([part.reshape(devs * SUB, LANES) for part in joined], axis=1)
        )
    latent = jnp.concatenate(latents, axis=0).astype(BF16)
    maps = [own_ref[0]]
    maps += [ref[:tiles].reshape(LAT, LANES) for ref in blocks[1:]]
    products = jnp.dot(
        latent, jnp.concatenate(maps, axis=1), preferred_element_type=F32
    ).reshape(rows * devs, SUB, len(maps) * LANES)
    sub = lax.broadcasted_iota(jnp.int32, (1, SUB, LANES), 1)
    masked = []
    for piece in range(len(maps)):
        chip = lax.rem(info_ref[5] + 4 - piece % 4, 4)
        head = chip * 2 + info_ref[3 + piece // 4]
        part = products[:, :, piece * LANES : piece * LANES + LANES]
        masked.append(jnp.where(sub == head, part, F32(0.0)))
    masked = jnp.concatenate(masked, axis=2).reshape(rows * devs * SUB, len(maps) * LANES)
    out_ref[...] = jnp.dot(
        sum_ref[...], masked.astype(BF16), preferred_element_type=F32
    ).astype(BF16)


def join(info, received, value_up, blocks, rows, eighth):
    devs = received.shape[0] // 2
    count = rows * devs
    sums = np.repeat(np.eye(count, dtype=np.float32), SUB, axis=1)
    arrays = [received, value_up, *blocks, jnp.asarray(sums, BF16)]
    return call(
        functools.partial(join_kernel, rows),
        "join",
        [info],
        arrays,
        [None] * len(arrays),
        [
            jax.ShapeDtypeStruct((count, SUB * LANES), BF16),
            jax.ShapeDtypeStruct((4 * rows, eighth), F32),
        ],
        work=480_000_000,
        limit=VMEM_MOST,
    )


def project_kernel(info_ref, natural_ref, *refs):
    values, own_ref, theirs_ref = refs[:8], refs[8], refs[9]
    parts, out_ref = refs[10:13], refs[13]
    rows = []
    for source, ref in enumerate(values):
        data = ref[...]
        lanes = []
        for piece in range(8):
            step = (piece - source) % 4
            side = piece // 4 ^ source // 4
            start = (side * 4 + step) * LANES
            lanes.append(data[:, start : start + LANES])
        rows.append(jnp.concatenate(lanes, axis=1))
    left = jnp.concatenate(rows, axis=0)
    count = left.shape[0]
    place = natural_ref[0:1]
    for source in range(8):
        chip = lax.rem(info_ref[5] + 4 - source % 4, 4)
        first = (chip * 2 + info_ref[3 + source // 4]) * (count // 64)
        place = place + jnp.where(natural_ref[1:2] == source, first, 0)
    order = lax.broadcasted_iota(jnp.int32, (count, count), 0) == place
    order = jnp.where(order, F32(1.0), F32(0.0)).astype(BF16)
    left = jnp.dot(order, left, preferred_element_type=F32).astype(BF16)
    columns = own_ref.shape[1] // LANES
    right = []
    for side, held_ref in enumerate((own_ref, theirs_ref)):
        right.append(held_ref[...])
        for ref in parts:
            tiles = [ref[side * columns + column] for column in range(columns)]
            right.append(jnp.concatenate(tiles, axis=1))
    right = jnp.concatenate(right, axis=0)
    total = jnp.dot(left, right, preferred_element_type=F32)
    out_ref[...] = total.reshape(out_ref.shape).astype(BF16)


def project(info, values, out_proj, out_theirs, parts, chips):
    rows = sum(value.shape[0] for value in values)
    lanes = out_proj.shape[0]
    eighth = out_proj.shape[1] // 8
    line = np.arange(rows) % (rows // 8)
    natural = np.stack([line % 8 * (rows // 8) + line // 8, np.arange(rows) // (rows // 8)])
    natural = jnp.asarray(natural, jnp.int32)
    own = pl.BlockSpec((lanes, eighth), lambda i, info: (0, info[0]))
    other = pl.BlockSpec((lanes, eighth), lambda i, info: (0, info[5]))
    return call(
        project_kernel,
        "project",
        [info],
        [natural, *values, out_proj, out_theirs, *parts],
        [None] * 9 + [own, other] + [None] * 3,
        jax.ShapeDtypeStruct((chips, rows // chips, eighth), BF16),
        work=2 * rows * 8 * lanes * eighth,
    )


def residual_kernel(parts_ref, stream_ref, gain_ref, residual_ref, out_ref):
    rows, width = residual_ref.shape
    residual = stream_ref[...] + jnp.sum(parts_ref[...].astype(F32), axis=0)
    residual_ref[...] = residual
    squares = jnp.sum(residual * residual, axis=1, keepdims=True)
    high = rounded(squares)
    low = rounded(squares - high)
    lane = lax.broadcasted_iota(jnp.int32, (SUB, LANES), 1)
    table = jnp.zeros((SUB, LANES), F32)
    scaled = residual * gain_ref[...]
    groups = rows // SUB
    columns = width // LANES
    chips = out_ref.shape[0]
    for group in range(groups):
        span = slice(group * SUB, group * SUB + SUB)
        table = jnp.where(lane == group, high[span], table)
        table = jnp.where(lane == SUB + group, low[span], table)
    tiles = [
        scaled[group * SUB : group * SUB + SUB, column * LANES : column * LANES + LANES]
        for column in range(columns)
        for group in range(groups)
    ] + [table]
    for index, tile in enumerate(tiles):
        out_ref[:, index] = jnp.broadcast_to(tile.astype(BF16)[None], (chips, SUB, LANES))


def residual_rows(parts, stream, gain, chips):
    _, rows, width = parts.shape
    tiles = rows * width // (SUB * LANES) + 1
    return call(
        residual_kernel,
        "residual",
        [],
        [parts, stream, gain],
        [None] * 3,
        [
            jax.ShapeDtypeStruct((rows, width), F32),
            jax.ShapeDtypeStruct((chips, tiles, SUB, LANES), BF16),
        ],
    )


def units_kernel(groups, last, recv_ref, weight_ref, *refs):
    sides, quarters, tiles, _, _ = recv_ref.shape
    columns = (tiles - 1) // groups
    rows = sides * groups * SUB
    depth = columns * LANES
    lane = lax.broadcasted_iota(jnp.int32, (SUB, LANES), 1)
    total = squares = None
    for quarter in range(quarters):
        left = jnp.concatenate(
            [
                recv_ref[:, quarter, column * groups : column * groups + groups]
                .astype(F32)
                .reshape(rows, LANES)
                for column in range(columns)
            ],
            axis=1,
        ).astype(BF16)
        part = lax.dot_general(
            left,
            weight_ref[:, quarter * depth : quarter * depth + depth],
            (((1,), (1,)), ((), ())),
            preferred_element_type=F32,
        )
        total = part if total is None else total + part
        table = recv_ref[:, quarter, tiles - 1].astype(F32)
        pieces = [
            jnp.sum(
                jnp.where((lane == group) | (lane == SUB + group), table, F32(0.0)),
                axis=2,
                keepdims=True,
            )
            for group in range(groups)
        ]
        part = jnp.stack(pieces, axis=1).reshape(rows, 1)
        squares = part if squares is None else squares + part
    if not last:
        acc_ref, sq_ref = refs
        acc_ref[...] = total
        sq_ref[...] = jnp.broadcast_to(squares, (rows, LANES))
    else:
        acc_ref, sq_ref, out_ref = refs
        hidden = out_ref.shape[1]
        scale = lax.rsqrt((sq_ref[:, :1] + squares) / (2 * weight_ref.shape[1]) + 1e-06)
        total = total + acc_ref[...]
        gate = total[:, :hidden] * scale
        upper = total[:, hidden:] * scale
        out_ref[...] = (gate / (1.0 + jnp.exp(-gate)) * upper).astype(BF16)


def units(received, weight, groups, carry=()):
    sides, quarters, tiles = received.shape[:3]
    hidden = weight.shape[0] // 2
    rows = sides * groups * SUB
    last = bool(carry)
    single = jax.ShapeDtypeStruct((rows, hidden), BF16)
    double = [
        jax.ShapeDtypeStruct((rows, 2 * hidden), F32),
        jax.ShapeDtypeStruct((rows, LANES), F32),
    ]
    return call(
        functools.partial(units_kernel, groups, last),
        "units_last" if last else "units_first",
        [],
        [received, weight, *carry],
        [WHOLE] * (2 + len(carry)),
        single if last else double,
        work=2 * rows * weight.size,
        out_specs=WHOLE if last else [WHOLE] * 2,
    )


def down_kernel(info_ref, mine_ref, theirs_ref, own_ref, other_ref, held_ref, out_ref, total):
    chips, steps = out_ref.shape[:2]
    rows = mine_ref.shape[0]
    count = rows // chips
    left = jnp.concatenate(
        [mine_ref[...].astype(F32), theirs_ref[...].astype(F32)], axis=1
    ).astype(BF16)
    width = 4 * LANES
    for step in range(steps):
        span = slice(step * width, step * width + width)
        weight = jnp.concatenate([own_ref[:, span], other_ref[:, span]], axis=0)
        total[:rows, span] = jnp.dot(left, weight, preferred_element_type=F32)
    total[pl.ds(rows, SUB), :] = jnp.zeros((SUB, total.shape[1]), F32)
    lines, columns = held_ref.shape
    place = pl.ds(pl.multiple_of(info_ref[2] * lines, SUB), lines)
    across = pl.ds(pl.multiple_of(info_ref[5] * columns, LANES), columns)
    total[place, across] += held_ref[...]
    sub = lax.broadcasted_iota(jnp.int32, (SUB, LANES), 0)
    for chip in range(chips):
        for step in range(steps):
            span = slice(step * width, step * width + width)
            part = total[chip * count : chip * count + SUB, span]
            quads = [part[:, tile * LANES : tile * LANES + LANES] for tile in range(4)]
            packed = [
                jnp.where(
                    sub < count, quads[tile], pltpu.roll(quads[3], count - 2 * tile, 0)
                )
                for tile in range(3)
            ]
            out_ref[chip, step] = jnp.concatenate(packed, axis=0).astype(BF16)


def down(info, mine, theirs, own, other, held, chips):
    rows = mine.shape[0]
    half = own.shape[1]
    return call(
        down_kernel,
        "down",
        [info],
        [mine, theirs, own, other, held],
        [WHOLE] * 5,
        jax.ShapeDtypeStruct((chips, half // (4 * LANES), 3 * SUB, LANES), BF16),
        [pltpu.VMEM((rows + SUB, half), F32)],
        4 * rows * own.size,
        out_specs=WHOLE,
    )


def finish_kernel(info_ref, parts_ref, mine_ref, theirs_ref):
    total = jnp.sum(parts_ref[...].astype(F32), axis=0)
    sub = lax.broadcasted_iota(jnp.int32, (SUB, LANES), 0)
    columns = []
    for step in range(total.shape[0]):
        quads = [total[step, tile * SUB : tile * SUB + SUB] for tile in range(3)]
        last = jnp.where(
            sub < 2,
            pltpu.roll(quads[0], 2, 0),
            jnp.where(sub < 4, pltpu.roll(quads[1], 4, 0), pltpu.roll(quads[2], 6, 0)),
        )
        columns += quads + [last]
    rows = jnp.concatenate(columns, axis=1)
    first, second = rows[0:3], rows[3:6]
    is_first = info_ref[3] == 0
    mine_ref[...] = jnp.where(is_first, first, second).astype(BF16)
    theirs_ref[...] = jnp.where(is_first, second, first).astype(BF16)


def finish(info, parts):
    shape = jax.ShapeDtypeStruct((3, parts.shape[1] * 4 * LANES), BF16)
    return call(
        finish_kernel,
        "finish",
        [info],
        [parts],
        [WHOLE],
        [shape, shape],
        out_specs=[WHOLE] * 2,
    )


def local(
    query_latent,
    latent_cache,
    lengths,
    stream,
    norm_gain,
    value_up,
    out_proj,
    gate_proj,
    up_proj,
    down_proj,
):
    core = lax.axis_index("core")
    ring = lax.axis_index("y")
    group = lax.axis_index("zl") * 4 + lax.axis_index("x")
    rows_own, width = stream.shape
    rows = query_latent.shape[0]
    half = width // 2
    eighth = width // 8
    first = core == 0
    info = [core * 4 + ring, core, group, core, 1 - core, ring, lax.axis_index("zh"), 0]
    info = jnp.stack(info).astype(jnp.int32)

    out_send, own, *starts = early(info, value_up, stream, out_proj)
    out_theirs = swap(out_send)
    firsts = [shift(part, step) for step, part in zip((1, 2, 3), starts)]
    gain = block(norm_gain, core * 4 + ring, eighth, 0)[None]

    payload, *cuts = attend(
        info,
        lengths,
        query_latent.transpose(0, 2, 1),
        latent_cache.transpose(0, 2, 1),
        out_proj,
        out_theirs,
    )
    payload, *firsts = lax.optimization_barrier((payload, *firsts))
    firsts_theirs = [swap(part) for part in [own] + firsts]
    parts = [shift(part, step) for step, part in zip((1, 2, 3), cuts)]
    received = lax.all_to_all(payload, OUTER, split_axis=0, concat_axis=0, tiled=True)
    blocks = [own] + firsts + firsts_theirs
    values, stream_rows = join(info, received, value_up, blocks, rows, eighth)

    last, parts[0] = lax.optimization_barrier((values, parts[0]))
    ring_values = [values, shift(values, 1), shift(values, 2), shift(last, 3)]
    late, _ = lax.optimization_barrier((values, ring_values[1]))
    both_values = ring_values + [swap(piece) for piece in [late] + ring_values[1:]]
    partial = project(
        info,
        both_values,
        out_proj,
        out_theirs,
        parts,
        16,
    )
    parts = lax.all_to_all(partial, OUTER, split_axis=0, concat_axis=0, tiled=True)

    residual, payload = residual_rows(parts, stream_rows, gain, 32)
    payload, gate_proj, up_proj, down_proj = lax.optimization_barrier(
        (payload, gate_proj, up_proj, down_proj)
    )
    piece = lax.all_to_all(payload, SIDE_CHIPS, split_axis=0, concat_axis=0, tiled=True)
    piece = piece.reshape((8, 4) + piece.shape[1:])
    other = swap(piece)
    first_weight, last_weight, down_own, down_send = stage(info, gate_proj.T, up_proj.T, down_proj)
    down_theirs = swap(down_send)
    groups = 8 * rows_own // SUB
    carry = units(piece, first_weight, groups)
    hidden = units(other, last_weight, groups, carry)
    partial = down(info, hidden, swap(hidden), down_own, down_theirs, residual, 32)
    parts = lax.all_to_all(partial, SIDE_CHIPS, split_axis=0, concat_axis=0, tiled=True)
    mine, theirs = finish(info, parts)
    theirs = swap(theirs)
    return jnp.concatenate(
        [jnp.where(first, mine, theirs), jnp.where(first, theirs, mine)], axis=1
    )


def solution(mesh):
    fine = Mesh(mesh.devices.reshape(2, 2, 4, 4, 2), AXES)
    placed = (
        P(DEV, None, None),
        P(DEV, "zh", None),
        P(DEV),
        P(AXES, None),
        P(),
        P(AXES, None, None),
        P(AXES, None),
        P(None, DEV),
        P(None, DEV),
        P(DEV, None),
    )
    return jax.shard_map(
        local, mesh=fine, in_specs=placed, out_specs=P(AXES, None), check_vma=False
    )
```

```python
import functools
import math

import jax
import jax.numpy as jnp
import numpy as np
from jax import lax
from jax.experimental import pallas as pl
from jax.experimental.pallas import tpu as pltpu
from jax.sharding import Mesh, PartitionSpec as P

LAT = 512
QKD = 192
LANES = 128
SUB = 8
AXES = ("zh", "zl", "x", "y", "core")
DEV = ("zl", "x", "y", "core")
OUTER = ("zh", "zl", "x")
SIDE_CHIPS = ("zl", "x", "y")
SWAP = [(0, 1), (1, 0)]
F32 = jnp.float32
BF16 = jnp.bfloat16
VMEM_MOST = 60 * 1024 * 1024
VMEM_STAGE = 44 * 1024 * 1024
VMEM_SOME = 24 * 1024 * 1024


def swap(array):
    return lax.ppermute(array, "core", SWAP)


def shift(array, step):
    return lax.ppermute(array, "y", [(i, (i + step) % 4) for i in range(4)])


def block(array, index, size, axis):
    return lax.dynamic_slice_in_dim(array, index * size, size, axis)


WHOLE = pl.BlockSpec(memory_space=pltpu.VMEM)
ANYWHERE = pl.BlockSpec(memory_space=pl.ANY)


def full(shape):
    return pl.BlockSpec(shape, lambda i, *info: (0,) * len(shape))


def call(kernel, name, scalars, arrays, specs, outs, scratch=(), work=None, limit=VMEM_SOME, out_specs=None):
    single = not isinstance(outs, list)
    shapes = [outs] if single else outs
    return pl.pallas_call(
        kernel,
        out_shape=outs,
        grid_spec=pltpu.PrefetchScalarGridSpec(
            num_scalar_prefetch=len(scalars),
            grid=(1,),
            in_specs=[full(a.shape) if s is None else s for a, s in zip(arrays, specs)],
            out_specs=out_specs
            or (full(outs.shape) if single else [full(o.shape) for o in outs]),
            scratch_shapes=list(scratch),
        ),
        compiler_params=pltpu.CompilerParams(
            vmem_limit_bytes=limit, dimension_semantics=("arbitrary",)
        ),
        cost_estimate=pl.CostEstimate(
            flops=work or 0,
            bytes_accessed=2 * sum(math.prod(a.shape) for a in list(arrays) + shapes),
            transcendentals=0,
        ),
        name=name,
    )(*scalars, *arrays)


def rounded(value):
    return value.astype(BF16).astype(F32)


def attend_kernel(
    info_ref, lengths_ref, query_hbm, cache_hbm, out_proj_hbm, theirs_hbm, out_ref, *refs
):
    cuts, (query_ref, cache_ref, weight_ref, sems) = refs[:3], refs[3:]
    half = theirs_hbm.shape[1]
    mine = out_proj_hbm.at[:, pl.ds(pl.multiple_of(info_ref[3] * half, LANES), half)]
    rows, _, heads = query_ref.shape
    keys = cache_ref.shape[2]
    pairs = rows // 2
    copies = [pltpu.make_async_copy(query_hbm, query_ref, sems.at[pairs])] + [
        pltpu.make_async_copy(
            cache_hbm.at[pl.ds(2 * pair, 2)], cache_ref.at[pl.ds(2 * pair, 2)], sems.at[pair]
        )
        for pair in range(pairs)
    ]
    for side, ref in enumerate((mine, theirs_hbm)):
        copies.append(
            pltpu.make_async_copy(ref, weight_ref.at[side], sems.at[pairs + 1 + side])
        )
    for copy in copies:
        copy.start()
    copies[0].wait()
    tiles = [slice(start, start + LANES) for start in range(0, LAT, LANES)]
    position = lax.broadcasted_iota(jnp.int32, (1, keys), 1) + info_ref[6] * keys
    lane = lax.broadcasted_iota(jnp.int32, (heads, LANES), 1)
    table = jnp.zeros((heads, LANES), F32)
    for row in range(rows):
        if row % 2 == 0:
            copies[1 + row // 2].wait()
        cached = cache_ref[row]
        scores = lax.dot_general(
            query_ref[row], cached, (((0,), (0,)), ((), ())), preferred_element_type=F32
        ) * (1.0 / math.sqrt(QKD))
        usable = position < lengths_ref[row]
        scores = jnp.where(usable, scores, F32(-1e30))
        top = jnp.max(scores, axis=1, keepdims=True)
        top_high = rounded(top)
        top_low = rounded(top - top_high)
        exponent = jnp.where(usable, jnp.exp(scores - (top_high + top_low)), F32(0.0))
        total = jnp.sum(exponent, axis=1, keepdims=True)
        total_high = rounded(total)
        total_low = rounded(total - total_high)
        weighted = lax.dot_general(
            exponent.astype(BF16),
            cached[:LAT],
            (((1,), (1,)), ((), ())),
            preferred_element_type=F32,
        )
        for number, tile in enumerate(tiles):
            out_ref[:, row * len(tiles) + number] = (
                weighted[:, tile].reshape(heads // SUB, SUB, LANES).astype(BF16)
            )
        table = jnp.where(lane == row, top_high, table)
        table = jnp.where(lane == row + SUB, top_low, table)
        table = jnp.where(lane == row + 2 * SUB, total_high, table)
        table = jnp.where(lane == row + 3 * SUB, total_low, table)
    out_ref[:, rows * len(tiles)] = table.reshape(heads // SUB, SUB, LANES).astype(BF16)
    copies[-2].wait()
    copies[-1].wait()
    for step, cut_ref in enumerate(cuts):
        columns = cut_ref.shape[0] // 2
        first = lax.rem(info_ref[5] + step + 1, 4) * columns
        for side in range(2):
            for column in range(columns):
                start = pl.multiple_of((first + column) * LANES, LANES)
                cut_ref[side * columns + column] = weight_ref[side, :, pl.ds(start, LANES)]


def attend(info, lengths, query, cache, out_proj, theirs):
    rows, depth, heads = query.shape
    keys = cache.shape[2]
    shape = (heads // SUB, rows * (LAT // LANES) + 1, SUB, LANES)
    columns = out_proj.shape[1] // 8 // LANES
    return call(
        attend_kernel,
        "attend",
        [info, lengths],
        [query, cache, out_proj, theirs],
        [ANYWHERE] * 4,
        [jax.ShapeDtypeStruct(shape, BF16)]
        + [jax.ShapeDtypeStruct((2 * columns, LANES, LANES), BF16)] * 3,
        [
            pltpu.VMEM(query.shape, BF16),
            pltpu.VMEM(cache.shape, BF16),
            pltpu.VMEM((2,) + theirs.shape, BF16),
            pltpu.SemaphoreType.DMA((rows // 2 + 3,)),
        ],
        2 * rows * heads * keys * (depth + LAT),
        VMEM_MOST,
    )


def early_kernel(info_ref, up_ref, stream_ref, half_ref, send_ref, *outs):
    send_ref[...] = half_ref[...]
    rows, width = stream_ref.shape
    eighth = width // 8
    ups = up_ref.shape[1] // LANES
    for step, out_ref in enumerate(outs):
        out_ref[:ups] = up_ref[0].reshape(ups, LANES, LANES)
        chip = lax.rem(info_ref[5] + step, 4)
        lines = []
        for side in (3, 4):
            start = pl.multiple_of((info_ref[side] * 4 + chip) * eighth, LANES)
            data = stream_ref[:, pl.ds(start, eighth)].astype(F32)
            for lane in range(0, eighth, LANES):
                lines.append(data[:, lane : lane + LANES])
                lines.append(jnp.zeros((SUB - rows, LANES), F32))
            lines.append(jnp.zeros((LANES // 2 - eighth // LANES * SUB, LANES), F32))
        out_ref[ups] = jnp.concatenate(lines, axis=0).astype(BF16)


def early(info, value_up, stream, out_proj):
    part = jax.ShapeDtypeStruct((value_up.shape[1] // LANES + 1, LANES, LANES), BF16)
    half = (out_proj.shape[0], out_proj.shape[1] // 2)
    return call(
        early_kernel,
        "early",
        [info],
        [value_up, stream, out_proj],
        [None, None, pl.BlockSpec(half, lambda i, info: (0, info[4]))],
        [jax.ShapeDtypeStruct(half, BF16)] + [part] * 4,
        limit=VMEM_MOST,
    )


def stage_kernel(info_ref, gate_ref, up_ref, down_ref, *refs):
    outs, own_ref, send_ref, sems = refs[:2], refs[2], refs[3], refs[4]
    rows, width = gate_ref.shape
    half = width // 2

    def part(ref, side):
        return ref.at[:, pl.ds(pl.multiple_of(info_ref[side] * half, LANES), half)]

    copies = [(part(down_ref, 4), send_ref)]
    for side, out_ref in zip((3, 4), outs):
        copies.append((part(gate_ref, side), out_ref.at[pl.ds(0, rows), :]))
        copies.append((part(up_ref, side), out_ref.at[pl.ds(rows, rows), :]))
    copies.append((part(down_ref, 3), own_ref))
    copies = [
        pltpu.make_async_copy(source, target, sems.at[index])
        for index, (source, target) in enumerate(copies)
    ]
    for copy in copies:
        copy.start()
    for copy in copies:
        copy.wait()


def stage(info, gate, up, down_proj):
    rows, width = gate.shape
    both = jax.ShapeDtypeStruct((2 * rows, width // 2), BF16)
    half = jax.ShapeDtypeStruct((down_proj.shape[0], down_proj.shape[1] // 2), BF16)
    return call(
        stage_kernel,
        "stage",
        [info],
        [gate, up, down_proj],
        [ANYWHERE] * 3,
        [both, both, half, half],
        [pltpu.SemaphoreType.DMA((6,))],
        limit=VMEM_STAGE,
        out_specs=[WHOLE] * 4,
    )


def join_kernel(rows, info_ref, recv_ref, own_ref, *refs):
    blocks, sum_ref, out_ref, stream_ref = refs[:8], refs[8], refs[9], refs[10]
    lines_own = stream_ref.shape[0] // len(blocks)
    shape = (stream_ref.shape[0], SUB)
    target = lax.broadcasted_iota(jnp.int32, shape, 0)
    line = lax.broadcasted_iota(jnp.int32, shape, 1)
    stream = None
    for index, ref in enumerate(blocks):
        lines = ref[ref.shape[0] - 1].astype(F32)
        base = LANES // 2 * (index // 4)
        spans = range(base, base + stream_ref.shape[1] // LANES * SUB, SUB)
        lines = jnp.concatenate([lines[span : span + SUB] for span in spans], axis=1)
        chip = lax.rem(info_ref[5] + 4 - index % 4, 4)
        first = (chip * 2 + info_ref[3 + index // 4]) * lines_own
        order = (target == line + first) & (line < lines_own)
        order = jnp.where(order, F32(1.0), F32(0.0)).astype(BF16)
        part = jnp.dot(order, lines.astype(BF16), preferred_element_type=F32)
        stream = part if stream is None else stream + part
    stream_ref[...] = stream
    sides = 2
    devs = recv_ref.shape[0] // sides
    tiles = LAT // LANES
    table = recv_ref[:, rows * tiles].astype(F32).reshape(sides, devs, SUB, LANES)
    lane = lax.broadcasted_iota(jnp.int32, (SUB, LANES), 1)

    def pick(first):
        chosen = (lane == first) | (lane == first + SUB)
        return jnp.sum(jnp.where(chosen, table, F32(0.0)), axis=3, keepdims=True)

    latents = []
    for row in range(rows):
        peaks = pick(row)
        totals = pick(2 * SUB + row)
        factor = jnp.exp(peaks - jnp.maximum(peaks[:1], peaks[1:]))
        factor = factor / (factor[:1] * totals[:1] + factor[1:] * totals[1:])
        parts = [
            recv_ref[:, row * tiles + number].astype(F32).reshape(sides, devs, SUB, LANES)
            for number in range(tiles)
        ]
        joined = [part[0] * factor[0] + part[1] * factor[1] for part in parts]
        latents.append(
            jnp.concatenate([part.reshape(devs * SUB, LANES) for part in joined], axis=1)
        )
    latent = jnp.concatenate(latents, axis=0).astype(BF16)
    maps = [own_ref[0]]
    maps += [ref[:tiles].reshape(LAT, LANES) for ref in blocks[1:]]
    products = jnp.dot(
        latent, jnp.concatenate(maps, axis=1), preferred_element_type=F32
    ).reshape(rows * devs, SUB, len(maps) * LANES)
    sub = lax.broadcasted_iota(jnp.int32, (1, SUB, LANES), 1)
    masked = []
    for piece in range(len(maps)):
        chip = lax.rem(info_ref[5] + 4 - piece % 4, 4)
        head = chip * 2 + info_ref[3 + piece // 4]
        part = products[:, :, piece * LANES : piece * LANES + LANES]
        masked.append(jnp.where(sub == head, part, F32(0.0)))
    masked = jnp.concatenate(masked, axis=2).reshape(rows * devs * SUB, len(maps) * LANES)
    out_ref[...] = jnp.dot(
        sum_ref[...], masked.astype(BF16), preferred_element_type=F32
    ).astype(BF16)


def join(info, received, value_up, blocks, rows, eighth):
    devs = received.shape[0] // 2
    count = rows * devs
    sums = np.repeat(np.eye(count, dtype=np.float32), SUB, axis=1)
    arrays = [received, value_up, *blocks, jnp.asarray(sums, BF16)]
    return call(
        functools.partial(join_kernel, rows),
        "join",
        [info],
        arrays,
        [None] * len(arrays),
        [
            jax.ShapeDtypeStruct((count, SUB * LANES), BF16),
            jax.ShapeDtypeStruct((4 * rows, eighth), F32),
        ],
        work=480_000_000,
        limit=VMEM_MOST,
    )


def project_kernel(info_ref, natural_ref, *refs):
    values, own_ref, theirs_ref = refs[:8], refs[8], refs[9]
    parts, out_ref = refs[10:13], refs[13]
    rows = []
    for source, ref in enumerate(values):
        data = ref[...]
        lanes = []
        for piece in range(8):
            step = (piece - source) % 4
            side = piece // 4 ^ source // 4
            start = (side * 4 + step) * LANES
            lanes.append(data[:, start : start + LANES])
        rows.append(jnp.concatenate(lanes, axis=1))
    left = jnp.concatenate(rows, axis=0)
    count = left.shape[0]
    place = natural_ref[0:1]
    for source in range(8):
        chip = lax.rem(info_ref[5] + 4 - source % 4, 4)
        first = (chip * 2 + info_ref[3 + source // 4]) * (count // 64)
        place = place + jnp.where(natural_ref[1:2] == source, first, 0)
    order = lax.broadcasted_iota(jnp.int32, (count, count), 0) == place
    order = jnp.where(order, F32(1.0), F32(0.0)).astype(BF16)
    left = jnp.dot(order, left, preferred_element_type=F32).astype(BF16)
    columns = own_ref.shape[1] // LANES
    right = []
    for side, held_ref in enumerate((own_ref, theirs_ref)):
        right.append(held_ref[...])
        for ref in parts:
            tiles = [ref[side * columns + column] for column in range(columns)]
            right.append(jnp.concatenate(tiles, axis=1))
    right = jnp.concatenate(right, axis=0)
    total = jnp.dot(left, right, preferred_element_type=F32)
    out_ref[...] = total.reshape(out_ref.shape).astype(BF16)


def project(info, values, out_proj, out_theirs, parts, chips):
    rows = sum(value.shape[0] for value in values)
    lanes = out_proj.shape[0]
    eighth = out_proj.shape[1] // 8
    line = np.arange(rows) % (rows // 8)
    natural = np.stack([line % 8 * (rows // 8) + line // 8, np.arange(rows) // (rows // 8)])
    natural = jnp.asarray(natural, jnp.int32)
    own = pl.BlockSpec((lanes, eighth), lambda i, info: (0, info[0]))
    other = pl.BlockSpec((lanes, eighth), lambda i, info: (0, info[5]))
    return call(
        project_kernel,
        "project",
        [info],
        [natural, *values, out_proj, out_theirs, *parts],
        [None] * 9 + [own, other] + [None] * 3,
        jax.ShapeDtypeStruct((chips, rows // chips, eighth), BF16),
        work=2 * rows * 8 * lanes * eighth,
    )


def residual_kernel(parts_ref, stream_ref, gain_ref, residual_ref, out_ref):
    rows, width = residual_ref.shape
    residual = stream_ref[...] + jnp.sum(parts_ref[...].astype(F32), axis=0)
    residual_ref[...] = residual
    squares = jnp.sum(residual * residual, axis=1, keepdims=True)
    high = rounded(squares)
    low = rounded(squares - high)
    lane = lax.broadcasted_iota(jnp.int32, (SUB, LANES), 1)
    table = jnp.zeros((SUB, LANES), F32)
    scaled = residual * gain_ref[...]
    groups = rows // SUB
    columns = width // LANES
    chips = out_ref.shape[0]
    for group in range(groups):
        span = slice(group * SUB, group * SUB + SUB)
        table = jnp.where(lane == group, high[span], table)
        table = jnp.where(lane == SUB + group, low[span], table)
    tiles = [
        scaled[group * SUB : group * SUB + SUB, column * LANES : column * LANES + LANES]
        for column in range(columns)
        for group in range(groups)
    ] + [table]
    for index, tile in enumerate(tiles):
        out_ref[:, index] = jnp.broadcast_to(tile.astype(BF16)[None], (chips, SUB, LANES))


def residual_rows(parts, stream, gain, chips):
    _, rows, width = parts.shape
    tiles = rows * width // (SUB * LANES) + 1
    return call(
        residual_kernel,
        "residual",
        [],
        [parts, stream, gain],
        [None] * 3,
        [
            jax.ShapeDtypeStruct((rows, width), F32),
            jax.ShapeDtypeStruct((chips, tiles, SUB, LANES), BF16),
        ],
    )


def units_kernel(groups, last, recv_ref, weight_ref, *refs):
    sides, quarters, tiles, _, _ = recv_ref.shape
    columns = (tiles - 1) // groups
    rows = sides * groups * SUB
    depth = columns * LANES
    lane = lax.broadcasted_iota(jnp.int32, (SUB, LANES), 1)
    total = squares = None
    for quarter in range(quarters):
        left = jnp.concatenate(
            [
                recv_ref[:, quarter, column * groups : column * groups + groups]
                .astype(F32)
                .reshape(rows, LANES)
                for column in range(columns)
            ],
            axis=1,
        ).astype(BF16)
        part = lax.dot_general(
            left,
            weight_ref[:, quarter * depth : quarter * depth + depth],
            (((1,), (1,)), ((), ())),
            preferred_element_type=F32,
        )
        total = part if total is None else total + part
        table = recv_ref[:, quarter, tiles - 1].astype(F32)
        pieces = [
            jnp.sum(
                jnp.where((lane == group) | (lane == SUB + group), table, F32(0.0)),
                axis=2,
                keepdims=True,
            )
            for group in range(groups)
        ]
        part = jnp.stack(pieces, axis=1).reshape(rows, 1)
        squares = part if squares is None else squares + part
    if not last:
        acc_ref, sq_ref = refs
        acc_ref[...] = total
        sq_ref[...] = jnp.broadcast_to(squares, (rows, LANES))
    else:
        acc_ref, sq_ref, out_ref = refs
        hidden = out_ref.shape[1]
        scale = lax.rsqrt((sq_ref[:, :1] + squares) / (2 * weight_ref.shape[1]) + 1e-06)
        total = total + acc_ref[...]
        gate = total[:, :hidden] * scale
        upper = total[:, hidden:] * scale
        out_ref[...] = (gate / (1.0 + jnp.exp(-gate)) * upper).astype(BF16)


def units(received, weight, groups, carry=()):
    sides, quarters, tiles = received.shape[:3]
    hidden = weight.shape[0] // 2
    rows = sides * groups * SUB
    last = bool(carry)
    single = jax.ShapeDtypeStruct((rows, hidden), BF16)
    double = [
        jax.ShapeDtypeStruct((rows, 2 * hidden), F32),
        jax.ShapeDtypeStruct((rows, LANES), F32),
    ]
    return call(
        functools.partial(units_kernel, groups, last),
        "units_last" if last else "units_first",
        [],
        [received, weight, *carry],
        [WHOLE] * (2 + len(carry)),
        single if last else double,
        work=2 * rows * weight.size,
        out_specs=WHOLE if last else [WHOLE] * 2,
    )


def down_kernel(
    info_ref, mine_ref, theirs_ref, own_ref, other_hbm, held_ref, out_ref, total, other_ref, sems
):
    spans = [pl.ds(start, 4 * LANES) for start in range(0, own_ref.shape[1], 4 * LANES)]
    copies = [
        pltpu.make_async_copy(other_hbm.at[:, span], other_ref.at[:, span], sems.at[index])
        for index, span in enumerate(spans)
    ]
    for copy in copies:
        copy.start()
    chips, steps = out_ref.shape[:2]
    rows = mine_ref.shape[0]
    count = rows // chips
    left = jnp.concatenate(
        [mine_ref[...].astype(F32), theirs_ref[...].astype(F32)], axis=1
    ).astype(BF16)
    width = 4 * LANES
    for step in range(steps):
        span = slice(step * width, step * width + width)
        copies[step].wait()
        weight = jnp.concatenate([own_ref[:, span], other_ref[:, span]], axis=0)
        total[:rows, span] = jnp.dot(left, weight, preferred_element_type=F32)
    total[pl.ds(rows, SUB), :] = jnp.zeros((SUB, total.shape[1]), F32)
    lines, columns = held_ref.shape
    place = pl.ds(pl.multiple_of(info_ref[2] * lines, SUB), lines)
    across = pl.ds(pl.multiple_of(info_ref[5] * columns, LANES), columns)
    total[place, across] += held_ref[...]
    sub = lax.broadcasted_iota(jnp.int32, (SUB, LANES), 0)
    for chip in range(chips):
        for step in range(steps):
            span = slice(step * width, step * width + width)
            part = total[chip * count : chip * count + SUB, span]
            quads = [part[:, tile * LANES : tile * LANES + LANES] for tile in range(4)]
            packed = [
                jnp.where(
                    sub < count, quads[tile], pltpu.roll(quads[3], count - 2 * tile, 0)
                )
                for tile in range(3)
            ]
            out_ref[chip, step] = jnp.concatenate(packed, axis=0).astype(BF16)


def down(info, mine, theirs, own, other, held, chips):
    rows = mine.shape[0]
    half = own.shape[1]
    return call(
        down_kernel,
        "down",
        [info],
        [mine, theirs, own, other, held],
        [WHOLE, WHOLE, WHOLE, ANYWHERE, WHOLE],
        jax.ShapeDtypeStruct((chips, half // (4 * LANES), 3 * SUB, LANES), BF16),
        [
            pltpu.VMEM((rows + SUB, half), F32),
            pltpu.VMEM(other.shape, BF16),
            pltpu.SemaphoreType.DMA((half // (4 * LANES),)),
        ],
        4 * rows * own.size,
        out_specs=WHOLE,
    )


def finish_kernel(info_ref, parts_ref, mine_ref, theirs_ref):
    total = jnp.sum(parts_ref[...].astype(F32), axis=0)
    sub = lax.broadcasted_iota(jnp.int32, (SUB, LANES), 0)
    columns = []
    for step in range(total.shape[0]):
        quads = [total[step, tile * SUB : tile * SUB + SUB] for tile in range(3)]
        last = jnp.where(
            sub < 2,
            pltpu.roll(quads[0], 2, 0),
            jnp.where(sub < 4, pltpu.roll(quads[1], 4, 0), pltpu.roll(quads[2], 6, 0)),
        )
        columns += quads + [last]
    rows = jnp.concatenate(columns, axis=1)
    first, second = rows[0:3], rows[3:6]
    is_first = info_ref[3] == 0
    mine_ref[...] = jnp.where(is_first, first, second).astype(BF16)
    theirs_ref[...] = jnp.where(is_first, second, first).astype(BF16)


def finish(info, parts):
    shape = jax.ShapeDtypeStruct((3, parts.shape[1] * 4 * LANES), BF16)
    return call(
        finish_kernel,
        "finish",
        [info],
        [parts],
        [WHOLE],
        [shape, shape],
        out_specs=[WHOLE] * 2,
    )


def local(
    query_latent,
    latent_cache,
    lengths,
    stream,
    norm_gain,
    value_up,
    out_proj,
    gate_proj,
    up_proj,
    down_proj,
):
    core = lax.axis_index("core")
    ring = lax.axis_index("y")
    group = lax.axis_index("zl") * 4 + lax.axis_index("x")
    rows_own, width = stream.shape
    rows = query_latent.shape[0]
    half = width // 2
    eighth = width // 8
    first = core == 0
    info = [core * 4 + ring, core, group, core, 1 - core, ring, lax.axis_index("zh"), 0]
    info = jnp.stack(info).astype(jnp.int32)

    out_send, own, *starts = early(info, value_up, stream, out_proj)
    out_theirs = swap(out_send)
    firsts = [shift(part, step) for step, part in zip((1, 2, 3), starts)]
    gain = block(norm_gain, core * 4 + ring, eighth, 0)[None]

    payload, *cuts = attend(
        info,
        lengths,
        query_latent.transpose(0, 2, 1),
        latent_cache.transpose(0, 2, 1),
        out_proj,
        out_theirs,
    )
    payload, *firsts = lax.optimization_barrier((payload, *firsts))
    firsts_theirs = [swap(part) for part in [own] + firsts]
    parts = [shift(part, step) for step, part in zip((1, 2, 3), cuts)]
    received = lax.all_to_all(payload, OUTER, split_axis=0, concat_axis=0, tiled=True)
    blocks = [own] + firsts + firsts_theirs
    values, stream_rows = join(info, received, value_up, blocks, rows, eighth)

    last, parts[0] = lax.optimization_barrier((values, parts[0]))
    ring_values = [values, shift(values, 1), shift(values, 2), shift(last, 3)]
    late, _ = lax.optimization_barrier((values, ring_values[1]))
    both_values = ring_values + [swap(piece) for piece in [late] + ring_values[1:]]
    partial = project(
        info,
        both_values,
        out_proj,
        out_theirs,
        parts,
        16,
    )
    parts = lax.all_to_all(partial, OUTER, split_axis=0, concat_axis=0, tiled=True)

    residual, payload = residual_rows(parts, stream_rows, gain, 32)
    payload, gate_proj, up_proj, down_proj = lax.optimization_barrier(
        (payload, gate_proj, up_proj, down_proj)
    )
    piece = lax.all_to_all(payload, SIDE_CHIPS, split_axis=0, concat_axis=0, tiled=True)
    piece = piece.reshape((8, 4) + piece.shape[1:])
    other = swap(piece)
    first_weight, last_weight, down_own, down_send = stage(info, gate_proj.T, up_proj.T, down_proj)
    down_theirs = swap(down_send)
    groups = 8 * rows_own // SUB
    carry = units(piece, first_weight, groups)
    hidden = units(other, last_weight, groups, carry)
    partial = down(info, hidden, swap(hidden), down_own, down_theirs, residual, 32)
    parts = lax.all_to_all(partial, SIDE_CHIPS, split_axis=0, concat_axis=0, tiled=True)
    mine, theirs = finish(info, parts)
    theirs = swap(theirs)
    return jnp.concatenate(
        [jnp.where(first, mine, theirs), jnp.where(first, theirs, mine)], axis=1
    )


def solution(mesh):
    fine = Mesh(mesh.devices.reshape(2, 2, 4, 4, 2), AXES)
    placed = (
        P(DEV, None, None),
        P(DEV, "zh", None),
        P(DEV),
        P(AXES, None),
        P(),
        P(AXES, None, None),
        P(AXES, None),
        P(None, DEV),
        P(None, DEV),
        P(DEV, None),
    )
    return jax.shard_map(
        local, mesh=fine, in_specs=placed, out_specs=P(AXES, None), check_vma=False
    )
```
